1024 devices in a mesh: gx: 8 (over z_lo), gy: 32 (over y, x), gz: 4 (over z_hi, core).
Axes of the slice: x: 4, y: 8, z: 16 (z_hi: 2, z_lo: 8; z = z_hi * 8 + z_lo), core: 2. Of those that a mesh axis runs over, the one named last changes fastest.
Arguments:
- old_field: float32 [64, 128, 4096], P('gx', 'gz', 'gy'), may hold values from -6 to 6
- new_home: int32 [8, 4, 128], P('gx', 'gz', 'gy'), may hold values from 0 to 127, as said below
- conduct: float32 [64, 128, 4096], P('gx', 'gz', 'gy'), may hold values from 0.2 to 4
- reaction: float32 [64, 128, 4096], P('gx', 'gz', 'gy'), may hold values from 0.05 to 2
- source: float32 [64, 128, 4096], P('gx', 'gz', 'gy'), may hold values from -6 to 6
- coarse: float32 [32, 64, 2048], P('gx', 'gz', 'gy'), may hold values from -12 to 12
Outputs:
- relaxed: float32 [64, 128, 4096], P('gx', 'gz', 'gy')
The draws below stay inside these ranges and needn't reach their ends.
Inputs may be any that keep to these rules, and one draw needn't show every extreme that they name: In each line of box positions along the second direction (fixed a and c), new_home is a permutation of 0 to 127. Of the 4 positions i * 4 to i * 4 + 3 of each block i, exactly one has a new home outside the block, and it is the position in its target block whose own box leaves; every other position is its own new home.
All inputs are finite; a program needn't handle non-finite values.
Results may differ from the reference program's by a relative error of at most 0.00002.
Values sent between devices are 32-bit elements; how exact they have to be, the bound alone decides.
No kernel may reach another device: no remote copies, remote signals or barrier semaphores. Data moves between devices by JAX's collectives and lax.ppermute only.
A program may use at most 32 MiB of HBM per device.

```python
import math
import jax
import jax.numpy as jnp
from jax import lax

BX = 8
BY = 32
BZ = 32
BOX_DEV = 4
KX = 8
KY = 128
KZ = 4
NX = 64
NY = 4096
NZ = 128


def draw_new_home(key, part):
    line_count = KX * KZ
    line_devs = KY // BOX_DEV
    line_keys = jax.random.split(jax.random.fold_in(key, 11), line_count)
    order = jax.vmap(lambda key_line: jax.random.permutation(key_line, line_devs))(line_keys).astype(jnp.int32)
    exit_slot = jax.random.randint(jax.random.fold_in(key, 12), (line_count, line_devs), 0, BOX_DEV).astype(jnp.int32)
    following = jnp.roll(order, -1, axis=1)
    row_ids = jnp.arange(line_count, dtype=jnp.int32)[:, None]
    successor = jnp.zeros((line_count, line_devs), jnp.int32).at[row_ids, order].set(following)
    target = successor * BOX_DEV + jnp.take_along_axis(exit_slot, successor, axis=1)
    own_ids = jnp.arange(KY, dtype=jnp.int32)[None, :]
    block_ids = own_ids // BOX_DEV
    leaves = own_ids % BOX_DEV == jnp.take_along_axis(exit_slot, jnp.broadcast_to(block_ids, (line_count, KY)), axis=1)
    result = jnp.where(leaves, jnp.take_along_axis(target, jnp.broadcast_to(block_ids, (line_count, KY)), axis=1), own_ids)
    return result.reshape(KX, KZ, KY).astype(jnp.int32)


def block_scale(key, shape, shards, least, high):
    factor_of = 1.0
    for position, parts in shards:
        draws = jax.random.uniform(jax.random.fold_in(jax.random.fold_in(key, 6), position), (parts,), jnp.float32, least / len(shards), high / len(shards))
        factor_of = factor_of * jnp.repeat(jnp.exp(draws), shape[position] // parts).reshape((-1,) + (1,) * (len(shape) - 1 - position))
    return factor_of


def gaussian(key, dims, scale, most, cuts=(), held_as=jnp.bfloat16):
    drawn = scale * jax.random.normal(key, dims, jnp.float32)
    if cuts:
        drawn = drawn * block_scale(key, dims, cuts, -0.22, 0.18)
    return jnp.clip(drawn, -most, most).astype(held_as)


def setup_inputs(seed: int = 0) -> dict:
    key_list = jax.random.split(jax.random.key(seed), 7)
    return {
        "old_field": gaussian(key_list[0], (NX, NZ, NY), 1.0, 6.0, ((0, 8), (1, 4), (2, 32)), jnp.float32),
        "new_home": draw_new_home(jax.random.fold_in(key_list[6], 71), 0),
        "conduct": jnp.clip(jnp.exp(math.log(4.0) - 2.9957323 * jax.random.uniform(key_list[2], (NX, NZ, NY), jnp.float32) ** block_scale(key_list[2], (NX, NZ, NY), ((0, 8), (1, 4), (2, 32)), -0.2, 0.2)), 0.2, 4.0),
        "reaction": jnp.clip(jnp.exp(math.log(2.0) - 3.6888794 * jax.random.uniform(key_list[3], (NX, NZ, NY), jnp.float32) ** block_scale(key_list[3], (NX, NZ, NY), ((0, 8), (1, 4), (2, 32)), -0.2, 0.2)), 0.05, 2.0),
        "source": gaussian(key_list[4], (NX, NZ, NY), 1.0, 6.0, ((0, 8), (1, 4), (2, 32)), jnp.float32),
        "coarse": gaussian(key_list[5], (NX // 2, NZ // 2, NY // 2), 2.0, 12.0, ((0, 8), (1, 4), (2, 32)), jnp.float32),
    }


def neighbours(values, ghosts, direction):
    extent = values.shape[direction]
    lower = jnp.concatenate([lax.slice_in_dim(ghosts, 0, 1, axis=direction), lax.slice_in_dim(values, 0, extent - 1, axis=direction)], axis=direction)
    upper = jnp.concatenate([lax.slice_in_dim(values, 1, extent, axis=direction), lax.slice_in_dim(ghosts, extent - 1, extent, axis=direction)], axis=direction)
    return lower, upper


def relax_cells(current, start_field, conduct, source, reaction, upsampled):
    numerator = start_field + source
    denominator = 1.0 + reaction
    for direction in range(3):
        lower_phi, upper_phi = neighbours(current, upsampled, direction)
        lower_kappa, upper_kappa = neighbours(conduct, conduct, direction)
        for beside_phi, beside_kappa in ((lower_phi, lower_kappa), (upper_phi, upper_kappa)):
            weight = 0.5 * (conduct + beside_kappa)
            numerator = numerator + weight * beside_phi
            denominator = denominator + weight
    return numerator / denominator


def reference(old_field, new_home, conduct, reaction, source, coarse):
    box_rows = old_field.reshape(KX, BX, KZ, BZ, KY, BY).transpose(0, 2, 4, 1, 3, 5)
    line_x = jnp.arange(KX, dtype=jnp.int32)[:, None, None]
    line_z = jnp.arange(KZ, dtype=jnp.int32)[None, :, None]
    line_y = jnp.arange(KY, dtype=jnp.int32)[None, None, :]
    anchor = jnp.zeros((KX, KZ, KY), jnp.int32).at[line_x, line_z, new_home].set(jnp.broadcast_to(line_y, (KX, KZ, KY)))
    placed = jax.vmap(jax.vmap(lambda line_blocks, chosen_rows: line_blocks[chosen_rows]))(box_rows, anchor)
    start_field = placed.transpose(0, 3, 1, 4, 2, 5).reshape(NX, NZ, NY)
    upsampled = jnp.repeat(jnp.repeat(jnp.repeat(coarse, 2, axis=0), 2, axis=1), 2, axis=2)
    current = start_field
    for sweep_num in range(2):
        current = relax_cells(current, start_field, conduct, source, reaction, upsampled)
    return current
```

```python
import jax
import jax.numpy as jnp
from jax import lax
from jax.experimental import pallas as pl
from jax.experimental.pallas import tpu as pltpu
from jax.sharding import PartitionSpec as P

LANES = 128
VMEM = pl.BlockSpec(memory_space=pltpu.VMEM)
SMEM = pl.BlockSpec(memory_space=pltpu.SMEM)
PARAMS = pltpu.CompilerParams(vmem_limit_bytes=24 * 1024 * 1024)
F32 = jnp.float32


def lane_of(shape):
    return lax.broadcasted_iota(jnp.int32, shape, len(shape) - 1)


def moved_slot(home_ref, slots):
    position = lax.axis_index("gy")
    slot = jnp.int32(0)
    target = jnp.int32(0)
    for j in range(slots):
        home = home_ref[j]
        leaves = home != position * slots + j
        slot = jnp.where(leaves, j, slot)
        target = jnp.where(leaves, home, target)
    return slot, target


def pack_kernel(home_ref, old_ref, send_ref):
    slots = home_ref.shape[0]
    width = LANES // slots
    rows = old_ref.shape[1] // slots
    slot, target = moved_slot(home_ref, slots)
    shape = (old_ref.shape[0], rows, LANES)
    group = lax.div(lane_of(shape), width)
    box = jnp.zeros(shape, F32)
    for g in range(slots):
        shift = lax.rem(width * (g - slot) + LANES, LANES)
        rolled = pltpu.roll(old_ref[:, g * rows : (g + 1) * rows, :], shift, 2)
        box = jnp.where(group == g, rolled, box)
    send_ref[...] = jnp.zeros(send_ref.shape, F32)
    send_ref[lax.div(target, slots)] = box


def write_y_faces(planes, low_ref, high_ref):
    low = high = jnp.zeros(low_ref.shape, F32)
    lane = lane_of(low_ref.shape)
    for i, plane in enumerate(planes):
        low = jnp.where(lane == i, pltpu.roll(plane, i, 1) if i else plane, low)
        high = jnp.where(lane == i, pltpu.roll(plane, i + 1, 1), high)
    low_ref[...] = low
    high_ref[...] = high


def place_kernel(
    home_ref, recv_ref, old_ref, conduct_ref, start_ref, xl_ref, xh_ref, zl_ref, zh_ref, yl_ref, yh_ref
):
    slots = home_ref.shape[0]
    width = LANES // slots
    nx, nz, _ = old_ref.shape
    rows = nz // slots
    slot, _ = moved_slot(home_ref, slots)
    arrived = recv_ref[0]
    for i in range(1, recv_ref.shape[0]):
        arrived = arrived + recv_ref[i]
    here = lax.div(lane_of(arrived.shape), width) == slot
    for g in range(slots):
        shift = lax.rem(width * (slot - g) + LANES, LANES)
        part = pl.ds(g * rows, rows)
        start_ref[:, part, :] = jnp.where(here, pltpu.roll(arrived, shift, 2), old_ref[:, part, :])
    for f, ref in enumerate((start_ref, conduct_ref)):
        xl_ref[f] = ref[0]
        xh_ref[f] = ref[nx - 1]
        zl_ref[f] = ref[:, 0, :]
        zh_ref[f] = ref[:, nz - 1, :]
    planes = [start_ref[x] for x in range(nx)] + [conduct_ref[x] for x in range(nx)]
    write_y_faces(planes, yl_ref, yh_ref)


def edges():
    flags = []
    for axis in ("gx", "gz", "gy"):
        index = lax.axis_index(axis)
        flags.append((index == 0, index == lax.axis_size(axis) - 1))
    return flags


def refine(coarse_ref):
    _, cz, cy = coarse_ref.shape
    left = lax.div(lax.broadcasted_iota(jnp.int32, (2 * cz, cz), 0), 2)
    left = (left == lax.broadcasted_iota(jnp.int32, (2 * cz, cz), 1)).astype(F32)
    right = lax.div(lax.broadcasted_iota(jnp.int32, (cy, 2 * cy), 1), 2)
    right = (right == lax.broadcasted_iota(jnp.int32, (cy, 2 * cy), 0)).astype(F32)
    planes = []
    for x in range(coarse_ref.shape[0]):
        wide = jnp.dot(
            coarse_ref[x], right, precision=lax.Precision.HIGHEST, preferred_element_type=F32
        )
        planes.append(
            jnp.dot(left, wide, precision=lax.Precision.HIGHEST, preferred_element_type=F32)
        )
    return planes


def beside(values, ghosts, x, nx, halo, flags):
    (x_first, x_last), (z_first, z_last), (y_first, y_last) = flags
    plane = values[x]
    ghost = ghosts[x]
    nz = plane.shape[0]
    row = lax.broadcasted_iota(jnp.int32, plane.shape, 0)
    lane = lane_of(plane.shape)
    xl, xh, zl, zh, yl, yh = halo
    below = values[x - 1] if x else jnp.where(x_first, ghost, xl)
    above = values[x + 1] if x < nx - 1 else jnp.where(x_last, ghost, xh)
    front = jnp.where(row == 0, jnp.where(z_first, ghost, zl[x : x + 1]), pltpu.roll(plane, 1, 0))
    back = jnp.where(
        row == nz - 1, jnp.where(z_last, ghost, zh[x : x + 1]), pltpu.roll(plane, nz - 1, 0)
    )
    left = jnp.where(lane == 0, jnp.where(y_first, ghost, yl(x)), pltpu.roll(plane, 1, 1))
    right = jnp.where(
        lane == LANES - 1, jnp.where(y_last, ghost, yh(x)), pltpu.roll(plane, LANES - 1, 1)
    )
    return below, above, front, back, left, right


def to_lane(packed, index, lane):
    shift = (lane - index) % LANES
    return pltpu.roll(packed, shift, 1) if shift else packed


def sweep_planes(refs, phi_planes, phi_halo):
    (start_ref, conduct_ref, source_ref, reaction_ref, coarse_ref, kappa_halo) = refs
    nx = start_ref.shape[0]
    flags = edges()
    refined = refine(coarse_ref)
    ghosts = [refined[x // 2] for x in range(nx)]
    kappas = [conduct_ref[x] for x in range(nx)]
    results = []
    for x in range(nx):
        numerator = start_ref[x] + source_ref[x]
        denominator = 1.0 + reaction_ref[x]
        phis = beside(phi_planes, ghosts, x, nx, phi_halo, flags)
        beside_kappas = beside(kappas, kappas, x, nx, kappa_halo, flags)
        for phi, kappa in zip(phis, beside_kappas):
            weight = 0.5 * (kappas[x] + kappa)
            numerator = numerator + weight * phi
            denominator = denominator + weight
        results.append(numerator / denominator)
    return results


def halo_of(xl, xh, zl, zh, yl, yh, offset):
    return (
        xl,
        xh,
        zl,
        zh,
        lambda x: to_lane(yl, offset + x, 0),
        lambda x: to_lane(yh, offset + x, LANES - 1),
    )


def first_kernel(
    start_ref, conduct_ref, source_ref, reaction_ref, coarse_ref,
    hxl, hxh, hzl, hzh, hyl, hyh,
    out_ref, xl_ref, xh_ref, zl_ref, zh_ref, yl_ref, yh_ref,
):
    nx, nz, _ = start_ref.shape
    ylow, yhigh = hyl[...], hyh[...]
    phi_halo = halo_of(hxl[0], hxh[0], hzl[0], hzh[0], ylow, yhigh, 0)
    kappa_halo = halo_of(hxl[1], hxh[1], hzl[1], hzh[1], ylow, yhigh, nx)
    refs = (start_ref, conduct_ref, source_ref, reaction_ref, coarse_ref, kappa_halo)
    planes = sweep_planes(refs, [start_ref[x] for x in range(nx)], phi_halo)
    for x, plane in enumerate(planes):
        out_ref[x] = plane
        zl_ref[x : x + 1] = plane[0:1]
        zh_ref[x : x + 1] = plane[nz - 1 : nz]
    xl_ref[...] = planes[0]
    xh_ref[...] = planes[nx - 1]
    write_y_faces(planes, yl_ref, yh_ref)


def second_kernel(
    first_ref, start_ref, conduct_ref, source_ref, reaction_ref, coarse_ref,
    kxl, kxh, kzl, kzh, kyl, kyh,
    hxl, hxh, hzl, hzh, hyl, hyh,
    out_ref,
):
    nx = start_ref.shape[0]
    phi_halo = halo_of(hxl[...], hxh[...], hzl[...], hzh[...], hyl[...], hyh[...], 0)
    kappa_halo = halo_of(kxl[1], kxh[1], kzl[1], kzh[1], kyl[...], kyh[...], nx)
    refs = (start_ref, conduct_ref, source_ref, reaction_ref, coarse_ref, kappa_halo)
    planes = sweep_planes(refs, [first_ref[x] for x in range(nx)], phi_halo)
    for x, plane in enumerate(planes):
        out_ref[x] = plane


def swap_faces(faces):
    halos = []
    for axis, low, high in (
        ("gx", faces[0], faces[1]),
        ("gz", faces[2], faces[3]),
        ("gy", faces[4], faces[5]),
    ):
        count = lax.axis_size(axis)
        forward = [(i, i + 1) for i in range(count - 1)]
        backward = [(b, a) for a, b in forward]
        halos.append(lax.ppermute(high, axis, forward))
        halos.append(lax.ppermute(low, axis, backward))
    return halos


def call(kernel, operands, outs, smem=0):
    specs = [SMEM] * smem + [VMEM] * (len(operands) - smem)
    return pl.pallas_call(
        kernel,
        out_shape=[jax.ShapeDtypeStruct(shape, F32) for shape in outs],
        in_specs=specs,
        out_specs=[VMEM] * len(outs),
        compiler_params=PARAMS,
    )(*operands)


def on_device(old_field, new_home, conduct, reaction, source, coarse):
    nx, nz, ny = old_field.shape
    home = new_home[0, 0]
    slots = home.shape[0]
    line = lax.axis_size("gy")
    (send,) = call(
        pack_kernel, (home, old_field), [(line, nx, nz // slots, ny)], smem=1
    )
    recv = lax.all_to_all(send, "gy", 0, 0, tiled=True)
    start, *faces = call(
        place_kernel,
        (home, recv, old_field, conduct),
        [old_field.shape]
        + [(2, nz, ny)] * 2
        + [(2, nx, ny)] * 2
        + [(nz, ny)] * 2,
        smem=1,
    )
    halos = swap_faces(faces)
    first, *faces = call(
        first_kernel,
        (start, conduct, source, reaction, coarse, *halos),
        [old_field.shape] + [(nz, ny)] * 2 + [(nx, ny)] * 2 + [(nz, ny)] * 2,
    )
    first_halos = swap_faces(faces)
    (relaxed,) = call(
        second_kernel,
        (first, start, conduct, source, reaction, coarse, *halos, *first_halos),
        [old_field.shape],
    )
    return relaxed


def solution(mesh):
    return jax.shard_map(
        on_device,
        mesh=mesh,
        in_specs=(P("gx", "gz", "gy"),) * 6,
        out_specs=P("gx", "gz", "gy"),
        check_vma=False,
    )
```

```python
import jax
import jax.numpy as jnp
from jax import lax
from jax.experimental import pallas as pl
from jax.experimental.pallas import tpu as pltpu
from jax.sharding import PartitionSpec as P

LANES = 128
RUN = 4
VMEM = pl.BlockSpec(memory_space=pltpu.VMEM)
SMEM = pl.BlockSpec(memory_space=pltpu.SMEM)
PARAMS = pltpu.CompilerParams(vmem_limit_bytes=24 * 1024 * 1024)
F32 = jnp.float32


def lane_of(shape):
    return lax.broadcasted_iota(jnp.int32, shape, len(shape) - 1)


def moved_slot(home_ref, slots):
    position = lax.axis_index("gy")
    slot = jnp.int32(0)
    target = jnp.int32(0)
    for j in range(slots):
        home = home_ref[j]
        leaves = home != position * slots + j
        slot = jnp.where(leaves, j, slot)
        target = jnp.where(leaves, home, target)
    return slot, target


def split_kernel(home_ref, old_ref, parts_ref):
    slots = home_ref.shape[0]
    width = LANES // slots
    rows = old_ref.shape[1] // slots
    slot, target = moved_slot(home_ref, slots)
    count, planes = parts_ref.shape[0], parts_ref.shape[1] - 1
    shape = (old_ref.shape[0], rows, LANES)
    group = lax.div(lane_of(shape), width)
    box = jnp.zeros(shape, F32)
    for g in range(slots):
        shift = lax.rem(width * (g - slot) + LANES, LANES)
        rolled = pltpu.roll(old_ref[:, g * rows : (g + 1) * rows, :], shift, 2)
        box = jnp.where(group == g, rolled, box)
    tag = jnp.full((rows, LANES), lax.div(target, slots), jnp.int32).astype(F32)
    for k in range(count):
        parts_ref[k, :planes] = box[k * planes : (k + 1) * planes]
        parts_ref[k, planes] = tag


def address_kernel(parts_ref, send_ref):
    planes = send_ref.shape[1]
    for device in range(send_ref.shape[0]):
        for i in range(planes):
            value = jnp.zeros(send_ref.shape[2:], F32)
            for k in range(parts_ref.shape[0]):
                value = jnp.where(parts_ref[k, planes] == device, parts_ref[k, i], value)
            send_ref[device, i] = value


def is_even(axis):
    return lax.rem(lax.axis_index(axis), 2) == 0


def write_pair(axis, first_ref, second_ref, index, low, high):
    even = is_even(axis)
    first_ref[index] = jnp.where(even, high, low)
    second_ref[index] = jnp.where(even, low, high)


def read_pair(axis, first, second):
    even = is_even(axis)
    return jnp.where(even, second, first), jnp.where(even, first, second)


def write_y_pair(planes, first_ref, second_ref):
    low = high = jnp.zeros(first_ref.shape, F32)
    lane = lane_of(first_ref.shape)
    for i, plane in enumerate(planes):
        low = jnp.where(lane == i, pltpu.roll(plane, i, 1) if i else plane, low)
        high = jnp.where(lane == i, pltpu.roll(plane, i + 1, 1), high)
    write_pair("gy", first_ref, second_ref, Ellipsis, low, high)


def place_kernel(
    home_ref, recv_ref, old_ref, conduct_ref, start_ref, xa_ref, xb_ref, za_ref, zb_ref, ya_ref, yb_ref
):
    slots = home_ref.shape[0]
    width = LANES // slots
    nx, nz, _ = old_ref.shape
    rows = nz // slots
    slot, _ = moved_slot(home_ref, slots)
    planes = recv_ref.shape[1]
    run = nx // planes
    here = lax.div(lane_of((rows, LANES)), width) == slot
    for k in range(run):
        for i in range(planes):
            x = k * planes + i
            arrived = recv_ref[k, i]
            for source in range(k + run, recv_ref.shape[0], run):
                arrived = arrived + recv_ref[source, i]
            for g in range(slots):
                shift = lax.rem(width * (slot - g) + LANES, LANES)
                part = pl.ds(g * rows, rows)
                start_ref[x, part, :] = jnp.where(here, pltpu.roll(arrived, shift, 1), old_ref[x, part, :])
    for f, ref in enumerate((start_ref, conduct_ref)):
        write_pair("gx", xa_ref, xb_ref, f, ref[0], ref[nx - 1])
        write_pair("gz", za_ref, zb_ref, f, ref[:, 0, :], ref[:, nz - 1, :])
    planes = [start_ref[x] for x in range(nx)] + [conduct_ref[x] for x in range(nx)]
    write_y_pair(planes, ya_ref, yb_ref)


def edges():
    flags = []
    for axis in ("gx", "gz", "gy"):
        index = lax.axis_index(axis)
        flags.append((index == 0, index == lax.axis_size(axis) - 1))
    return flags


def refine(coarse_ref):
    _, cz, cy = coarse_ref.shape
    left = lax.div(lax.broadcasted_iota(jnp.int32, (2 * cz, cz), 0), 2)
    left = (left == lax.broadcasted_iota(jnp.int32, (2 * cz, cz), 1)).astype(F32)
    right = lax.div(lax.broadcasted_iota(jnp.int32, (cy, 2 * cy), 1), 2)
    right = (right == lax.broadcasted_iota(jnp.int32, (cy, 2 * cy), 0)).astype(F32)
    planes = []
    for x in range(coarse_ref.shape[0]):
        wide = jnp.dot(
            coarse_ref[x], right, precision=lax.Precision.HIGHEST, preferred_element_type=F32
        )
        planes.append(
            jnp.dot(left, wide, precision=lax.Precision.HIGHEST, preferred_element_type=F32)
        )
    return planes


def beside(values, ghosts, x, nx, halo, flags):
    (x_first, x_last), (z_first, z_last), (y_first, y_last) = flags
    plane = values[x]
    ghost = ghosts[x]
    nz = plane.shape[0]
    row = lax.broadcasted_iota(jnp.int32, plane.shape, 0)
    lane = lane_of(plane.shape)
    xl, xh, zl, zh, yl, yh = halo
    below = values[x - 1] if x else jnp.where(x_first, ghost, xl)
    above = values[x + 1] if x < nx - 1 else jnp.where(x_last, ghost, xh)
    front = jnp.where(row == 0, jnp.where(z_first, ghost, zl[x : x + 1]), pltpu.roll(plane, 1, 0))
    back = jnp.where(
        row == nz - 1, jnp.where(z_last, ghost, zh[x : x + 1]), pltpu.roll(plane, nz - 1, 0)
    )
    left = jnp.where(lane == 0, jnp.where(y_first, ghost, yl(x)), pltpu.roll(plane, 1, 1))
    right = jnp.where(
        lane == LANES - 1, jnp.where(y_last, ghost, yh(x)), pltpu.roll(plane, LANES - 1, 1)
    )
    return below, above, front, back, left, right


def to_lane(packed, index, lane):
    shift = (lane - index) % LANES
    return pltpu.roll(packed, shift, 1) if shift else packed


def sweep_planes(refs, phi_planes, phi_halo):
    (start_ref, conduct_ref, source_ref, reaction_ref, coarse_ref, kappa_halo) = refs
    nx = start_ref.shape[0]
    flags = edges()
    refined = refine(coarse_ref)
    ghosts = [refined[x // 2] for x in range(nx)]
    kappas = [conduct_ref[x] for x in range(nx)]
    results = []
    for x in range(nx):
        numerator = start_ref[x] + source_ref[x]
        denominator = 1.0 + reaction_ref[x]
        phis = beside(phi_planes, ghosts, x, nx, phi_halo, flags)
        beside_kappas = beside(kappas, kappas, x, nx, kappa_halo, flags)
        for phi, kappa in zip(phis, beside_kappas):
            weight = 0.5 * (kappas[x] + kappa)
            numerator = numerator + weight * phi
            denominator = denominator + weight
        results.append(numerator / denominator)
    return results


def halo_of(halos, offset, index=Ellipsis):
    xa, xb, za, zb, ya, yb = halos
    xl, xh = read_pair("gx", xa[index], xb[index])
    zl, zh = read_pair("gz", za[index], zb[index])
    yl, yh = read_pair("gy", ya[...], yb[...])
    return (
        xl,
        xh,
        zl,
        zh,
        lambda x: to_lane(yl, offset + x, 0),
        lambda x: to_lane(yh, offset + x, LANES - 1),
    )


def first_kernel(
    start_ref, conduct_ref, source_ref, reaction_ref, coarse_ref, *rest
):
    halos, out_ref, (xa_ref, xb_ref, za_ref, zb_ref, ya_ref, yb_ref) = rest[:6], rest[6], rest[7:]
    nx, nz, _ = start_ref.shape
    phi_halo = halo_of(halos, 0, 0)
    kappa_halo = halo_of(halos, nx, 1)
    refs = (start_ref, conduct_ref, source_ref, reaction_ref, coarse_ref, kappa_halo)
    planes = sweep_planes(refs, [start_ref[x] for x in range(nx)], phi_halo)
    for x, plane in enumerate(planes):
        out_ref[x] = plane
        write_pair("gz", za_ref, zb_ref, slice(x, x + 1), plane[0:1], plane[nz - 1 : nz])
    write_pair("gx", xa_ref, xb_ref, Ellipsis, planes[0], planes[nx - 1])
    write_y_pair(planes, ya_ref, yb_ref)


def second_kernel(
    first_ref, start_ref, conduct_ref, source_ref, reaction_ref, coarse_ref, *rest
):
    halos, first_halos, out_ref = rest[:6], rest[6:12], rest[12]
    nx = start_ref.shape[0]
    phi_halo = halo_of(first_halos, 0)
    kappa_halo = halo_of(halos, nx, 1)
    refs = (start_ref, conduct_ref, source_ref, reaction_ref, coarse_ref, kappa_halo)
    planes = sweep_planes(refs, [first_ref[x] for x in range(nx)], phi_halo)
    for x, plane in enumerate(planes):
        out_ref[x] = plane


def swap_faces(faces):
    halos = []
    for i, axis in enumerate(("gx", "gz", "gy")):
        count = lax.axis_size(axis)
        for j in range(2):
            pairs = []
            for low in range(j, count - 1, 2):
                pairs += [(low, low + 1), (low + 1, low)]
            halos.append(lax.ppermute(faces[2 * i + j], axis, pairs))
    return halos


def call(kernel, operands, outs, smem=0):
    specs = [SMEM] * smem + [VMEM] * (len(operands) - smem)
    return pl.pallas_call(
        kernel,
        out_shape=[jax.ShapeDtypeStruct(shape, F32) for shape in outs],
        in_specs=specs,
        out_specs=[VMEM] * len(outs),
        compiler_params=PARAMS,
    )(*operands)


def on_device(old_field, new_home, conduct, reaction, source, coarse):
    nx, nz, ny = old_field.shape
    home = new_home[0, 0]
    slots = home.shape[0]
    line = lax.axis_size("gy")
    run = RUN
    part = nx // run
    (parts,) = call(
        split_kernel, (home, old_field), [(run, part + 1, nz // slots, ny)], smem=1
    )
    groups = [[i * run + k for k in range(run)] for i in range(line // run)]
    parts = lax.all_to_all(parts, "gy", 0, 0, tiled=True, axis_index_groups=groups)
    (send,) = call(address_kernel, (parts,), [(line, part, nz // slots, ny)])
    recv = lax.all_to_all(send, "gy", 0, 0, tiled=True)
    start, *faces = call(
        place_kernel,
        (home, recv, old_field, conduct),
        [old_field.shape]
        + [(2, nz, ny)] * 2
        + [(2, nx, ny)] * 2
        + [(nz, ny)] * 2,
        smem=1,
    )
    halos = swap_faces(faces)
    first, *faces = call(
        first_kernel,
        (start, conduct, source, reaction, coarse, *halos),
        [old_field.shape] + [(nz, ny)] * 2 + [(nx, ny)] * 2 + [(nz, ny)] * 2,
    )
    first_halos = swap_faces(faces)
    (relaxed,) = call(
        second_kernel,
        (first, start, conduct, source, reaction, coarse, *halos, *first_halos),
        [old_field.shape],
    )
    return relaxed


def solution(mesh):
    return jax.shard_map(
        on_device,
        mesh=mesh,
        in_specs=(P("gx", "gz", "gy"),) * 6,
        out_specs=P("gx", "gz", "gy"),
        check_vma=False,
    )
```

```python
import jax
import jax.numpy as jnp
from jax import lax
from jax.experimental import pallas as pl
from jax.experimental.pallas import tpu as pltpu
from jax.sharding import PartitionSpec as P

LANES = 128
RUN = 4
VMEM = pl.BlockSpec(memory_space=pltpu.VMEM)
SMEM = pl.BlockSpec(memory_space=pltpu.SMEM)
PARAMS = pltpu.CompilerParams(vmem_limit_bytes=24 * 1024 * 1024)
F32 = jnp.float32

PHI1, PHI2, KAP1, KAP2, SRC, REA, RIM = range(7)


def lane_of(shape):
    return lax.broadcasted_iota(jnp.int32, shape, len(shape) - 1)


def row_of(shape):
    return lax.broadcasted_iota(jnp.int32, shape, len(shape) - 2)


def roll_lanes(value, shift):
    shift = shift % LANES
    return pltpu.roll(value, shift, value.ndim - 1) if shift else value


def roll_rows(value, shift):
    return pltpu.roll(value, shift % value.shape[0], 0)


def moved_slot(home_ref, slots):
    position = lax.axis_index("gy")
    slot = jnp.int32(0)
    target = jnp.int32(0)
    for j in range(slots):
        home = home_ref[j]
        leaves = home != position * slots + j
        slot = jnp.where(leaves, j, slot)
        target = jnp.where(leaves, home, target)
    return slot, target


def edges():
    flags = []
    for axis in ("gx", "gz", "gy"):
        index = lax.axis_index(axis)
        flags.append((index == 0, index == lax.axis_size(axis) - 1))
    return flags


def is_even(axis):
    return lax.rem(lax.axis_index(axis), 2) == 0


def write_pair(axis, first_ref, second_ref, index, low, high):
    even = is_even(axis)
    first_ref[index] = jnp.where(even, high, low)
    second_ref[index] = jnp.where(even, low, high)


def received(axis, first, second):
    even = is_even(axis)
    return jnp.where(even, second, first), jnp.where(even, first, second)


def sent(axis, first, second):
    even = is_even(axis)
    return jnp.where(even, second, first), jnp.where(even, first, second)


def refine(coarse_ref):
    _, cz, cy = coarse_ref.shape
    left = lax.div(lax.broadcasted_iota(jnp.int32, (2 * cz, cz), 0), 2)
    left = (left == lax.broadcasted_iota(jnp.int32, (2 * cz, cz), 1)).astype(F32)
    right = lax.div(lax.broadcasted_iota(jnp.int32, (cy, 2 * cy), 1), 2)
    right = (right == lax.broadcasted_iota(jnp.int32, (cy, 2 * cy), 0)).astype(F32)
    planes = []
    for x in range(coarse_ref.shape[0]):
        wide = jnp.dot(
            coarse_ref[x], right, precision=lax.Precision.HIGHEST, preferred_element_type=F32
        )
        planes.append(
            jnp.dot(left, wide, precision=lax.Precision.HIGHEST, preferred_element_type=F32)
        )
    return planes


def prepare_kernel(
    home_ref, old_ref, conduct_ref, source_ref, reaction_ref, coarse_ref,
    parts_ref, src_ref, rea_ref, za_ref, zb_ref,
):
    slots = home_ref.shape[0]
    width = LANES // slots
    nx, nz, _ = old_ref.shape
    rows = nz // slots
    slot, target = moved_slot(home_ref, slots)
    device = lax.div(target, slots)
    back = LANES - width * slot

    count, planes = parts_ref.shape[0], parts_ref.shape[1] - 1
    shape = (nx, rows, LANES)
    group = lax.div(lane_of(shape), width)
    box = jnp.zeros(shape, F32)
    for g in range(slots):
        shift = lax.rem(back + width * g, LANES)
        rolled = pltpu.roll(old_ref[:, g * rows : (g + 1) * rows, :], shift, 2)
        box = jnp.where(group == g, rolled, box)
    for k in range(count):
        parts_ref[k, :planes] = box[k * planes : (k + 1) * planes]
        parts_ref[k, planes] = jnp.full((rows, LANES), device, jnp.int32).astype(F32)

    (x_first, x_last), (z_first, z_last), (y_first, y_last) = edges()
    refined = refine(coarse_ref)
    row, lane = row_of((nz, LANES)), lane_of((nz, LANES))
    inner = (
        ((row == 0) & z_first).astype(F32)
        + ((row == nz - 1) & z_last).astype(F32)
        + ((lane == 0) & y_first).astype(F32)
        + ((lane == LANES - 1) & y_last).astype(F32)
    )
    for x in range(nx):
        faces = inner
        if x == 0:
            faces = faces + jnp.where(x_first, 1.0, 0.0)
        if x == nx - 1:
            faces = faces + jnp.where(x_last, 1.0, 0.0)
        weight = faces * conduct_ref[x]
        src_ref[x] = source_ref[x] + weight * refined[x // 2]
        rea_ref[x] = 1.0 + reaction_ref[x] + weight

    lane = lane_of((nx, LANES))
    note = jnp.where(lane < 3 * width, device, slot).astype(F32)

    def rims(first, second):
        near = pltpu.roll(first, lax.rem(back, LANES), 1)
        far = pltpu.roll(second, lax.rem(back + width, LANES), 1)
        return jnp.where(lane < width, near, jnp.where(lane < 2 * width, far, note))

    low = [old_ref[:, 0, :], old_ref[:, 1, :], conduct_ref[:, 0, :], conduct_ref[:, 1, :]]
    low += [src_ref[:, 0, :], rea_ref[:, 0, :], rims(low[0], low[1])]
    high = [old_ref[:, nz - 1, :], old_ref[:, nz - 2, :]]
    high += [conduct_ref[:, nz - 1, :], conduct_ref[:, nz - 2, :]]
    high += [src_ref[:, nz - 1, :], rea_ref[:, nz - 1, :], rims(high[0], high[1])]
    for i in range(7):
        write_pair("gz", za_ref, zb_ref, i, low[i], high[i])


def address_kernel(parts_ref, za_ref, zb_ref, send_ref, *, width):
    planes = send_ref.shape[1] - 1
    low, high = received("gz", za_ref[RIM], zb_ref[RIM])
    shape = low.shape
    lane = lane_of(shape)
    low_tag = jnp.broadcast_to(low[:, 2 * width : 2 * width + 1], shape)
    high_tag = jnp.broadcast_to(high[:, 2 * width : 2 * width + 1], shape)
    high = roll_lanes(high, 2 * width)
    lower = lane < 2 * width
    rims = jnp.where(lower, low, high)
    tag = jnp.where(lower, low_tag, high_tag)
    for device in range(send_ref.shape[0]):
        for i in range(planes):
            value = jnp.zeros(shape, F32)
            for k in range(parts_ref.shape[0]):
                value = jnp.where(parts_ref[k, planes] == device, parts_ref[k, i], value)
            send_ref[device, i] = value
        send_ref[device, planes] = jnp.where(tag == device, rims, 0.0)


def spread(tile, offset, width):
    piece = jnp.where(lane_of(tile.shape) < width, roll_lanes(tile, -offset), 0.0)
    result = piece
    for shift in range(width, LANES, width):
        result = result + roll_lanes(piece, shift)
    return result


def place_kernel(
    home_ref, recv_ref, old_ref, conduct_ref, src_ref, rea_ref, za_ref, zb_ref,
    start_ref, zhalo_ref, ya_ref, yb_ref,
):
    slots = home_ref.shape[0]
    width = LANES // slots
    nx, nz, _ = old_ref.shape
    rows = nz // slots
    slot, _ = moved_slot(home_ref, slots)
    planes = recv_ref.shape[1] - 1
    run = nx // planes
    count = recv_ref.shape[0]
    here = lax.div(lane_of((rows, LANES)), width) == slot
    for k in range(run):
        for i in range(planes):
            x = k * planes + i
            arrived = recv_ref[k, i]
            for source in range(k + run, count, run):
                arrived = arrived + recv_ref[source, i]
            for g in range(slots):
                shift = lax.rem(width * (slot - g) + LANES, LANES)
                part = pl.ds(g * rows, rows)
                start_ref[x, part, :] = jnp.where(
                    here, pltpu.roll(arrived, shift, 1), old_ref[x, part, :]
                )

    rims = recv_ref[0, planes]
    for source in range(1, count):
        rims = rims + recv_ref[source, planes]
    faces = [received("gz", za_ref[i], zb_ref[i]) for i in range(7)]
    group = lax.div(lane_of((nx, LANES)), width).astype(F32)
    for side in range(2):
        note = faces[RIM][side]
        there = jnp.broadcast_to(note[:, 3 * width : 3 * width + 1], note.shape) == group
        for depth in range(2):
            moved = spread(rims, (2 * side + depth) * width, width)
            zhalo_ref[side, depth] = jnp.where(there, moved, faces[depth][side])

    lane = lane_of((nz, LANES))
    low = high = jnp.zeros((nz, LANES), F32)
    for f, (ref, depth) in enumerate(
        ((start_ref, 0), (start_ref, 1), (conduct_ref, 0), (conduct_ref, 1), (src_ref, 0), (rea_ref, 0))
    ):
        for x in range(nx):
            spot = f * nx + x
            low = jnp.where(lane == spot, roll_lanes(ref[x], spot - depth), low)
            high = jnp.where(lane == spot, roll_lanes(ref[x], spot + 1 + depth), high)
    write_pair("gy", ya_ref, yb_ref, slice(0, nz), low, high)
    lane = lane_of((nx, LANES))
    low = high = jnp.zeros((nx, LANES), F32)
    for side in range(2):
        for f, tile in enumerate((zhalo_ref[side, 0], faces[KAP1][side])):
            spot = 2 * side + f
            low = jnp.where(lane == spot, roll_lanes(tile, spot), low)
            high = jnp.where(lane == spot, roll_lanes(tile, spot + 1), high)
    write_pair("gy", ya_ref, yb_ref, slice(nz, nz + nx), low, high)


def edge_kernel(
    start_ref, conduct_ref, src_ref, rea_ref, zhalo_ref, za_ref, zb_ref, ya_ref, yb_ref,
    xa_ref, xb_ref,
):
    nx, nz, _ = start_ref.shape
    for f, (ref, depth) in enumerate(
        ((start_ref, 0), (start_ref, 1), (conduct_ref, 0), (conduct_ref, 1), (src_ref, 0), (rea_ref, 0))
    ):
        write_pair(
            "gx", xa_ref, xb_ref, slice(f * nz, (f + 1) * nz), ref[depth], ref[nx - 1 - depth]
        )
    base = 6 * nz
    kappas = received("gz", za_ref[KAP1], zb_ref[KAP1])
    xa_ref[base : base + 8] = jnp.zeros((8, LANES), F32)
    xb_ref[base : base + 8] = jnp.zeros((8, LANES), F32)
    for side in range(2):
        for f, tile in enumerate((zhalo_ref[side, 0], kappas[side])):
            spot = base + 2 * side + f
            write_pair(
                "gx", xa_ref, xb_ref, slice(spot, spot + 1), tile[0:1], tile[nx - 1 : nx]
            )
    lane = lane_of((nz, LANES))
    low = high = jnp.zeros((nz, LANES), F32)
    for side, halo in enumerate(received("gy", ya_ref[:nz], yb_ref[:nz])):
        for f, offset in enumerate((PHI1 * nx, KAP1 * nx)):
            spot = 2 * side + f
            low = jnp.where(lane == spot, roll_lanes(halo, spot - offset), low)
            high = jnp.where(lane == spot, roll_lanes(halo, spot - offset - nx + 1), high)
    write_pair("gx", xa_ref, xb_ref, slice(base + 8, base + 8 + nz), low, high)


def step(numerator, denominator, kappa, sides):
    for phi, beside, outside in sides:
        weight = 0.5 * (kappa + beside)
        if outside is not None:
            weight = jnp.where(outside, 0.0, weight)
        numerator = numerator + weight * phi
        denominator = denominator + weight
    return numerator / denominator


def along_rows(phi, kappa, low, high, flags):
    row = row_of(phi.shape)
    last = phi.shape[0] - 1
    low_edge, high_edge = row == 0, row == last
    return [
        (
            jnp.where(low_edge, low[0], roll_rows(phi, 1)),
            jnp.where(low_edge, low[1], roll_rows(kappa, 1)),
            low_edge & flags[0],
        ),
        (
            jnp.where(high_edge, high[0], roll_rows(phi, last)),
            jnp.where(high_edge, high[1], roll_rows(kappa, last)),
            high_edge & flags[1],
        ),
    ]


def along_lanes(phi, kappa, low, high, flags, last=LANES - 1):
    lane = lane_of(phi.shape)
    low_edge, high_edge = lane == 0, lane == last
    return [
        (
            jnp.where(low_edge, low[0], roll_lanes(phi, 1)),
            jnp.where(low_edge, low[1], roll_lanes(kappa, 1)),
            low_edge & flags[0],
        ),
        (
            jnp.where(high_edge, high[0], roll_lanes(phi, -1)),
            jnp.where(high_edge, high[1], roll_lanes(kappa, -1)),
            high_edge & flags[1],
        ),
    ]


def to_row(tile, spot):
    column = jnp.broadcast_to(tile[:, spot : spot + 1], tile.shape)
    return jnp.sum(
        jnp.where(lane_of(tile.shape) == row_of(tile.shape), column, 0.0), axis=0, keepdims=True
    )


def sweeps_kernel(
    start_ref, conduct_ref, src_ref, rea_ref, zhalo_ref,
    za_ref, zb_ref, sya_ref, syb_ref, ya_ref, yb_ref, xa_ref, xb_ref,
    out_ref,
):
    nx, nz, _ = start_ref.shape
    flags_x, flags_z, flags_y = edges()
    start = [start_ref[x] for x in range(nx)]
    conduct = [conduct_ref[x] for x in range(nx)]
    base = 6 * nz

    def part(axis, a_ref, b_ref, begin, size):
        return received(axis, a_ref[begin : begin + size], b_ref[begin : begin + size])

    xf = [part("gx", xa_ref, xb_ref, f * nz, nz) for f in range(6)]
    xrows = part("gx", xa_ref, xb_ref, base, 8)
    xcols = part("gx", xa_ref, xb_ref, base + 8, nz)
    zf = [received("gz", za_ref[i], zb_ref[i]) for i in range(6)]
    yf = part("gy", ya_ref, yb_ref, 0, nz)
    yt = part("gy", ya_ref, yb_ref, nz, nx)
    sf = sent("gy", sya_ref[:nz], syb_ref[:nz])

    def columns(tile, phi_spot, kappa_spot, lane):
        return roll_lanes(tile, lane - phi_spot), roll_lanes(tile, lane - kappa_spot)

    x_first_sweep = []
    for side in range(2):
        phi, kappa = xf[PHI1][side], xf[KAP1][side]
        me = 0 if side == 0 else nx - 1
        rows = xrows[side]
        sides = [(xf[PHI2][side], xf[KAP2][side], None), (start[me], conduct[me], None)]
        sides += along_rows(phi, kappa, (rows[0:1], rows[1:2]), (rows[2:3], rows[3:4]), flags_z)
        tile = xcols[side]
        sides += along_lanes(
            phi, kappa, columns(tile, 0, 1, 0), columns(tile, 2, 3, LANES - 1), flags_y
        )
        x_first_sweep.append(step(phi + xf[SRC][side], xf[REA][side], kappa, sides))

    z_first_sweep = []
    for side in range(2):
        phi, kappa = zhalo_ref[side, 0], zf[KAP1][side]
        me = 0 if side == 0 else nz - 1
        at = 2 * side
        sides = [
            (zhalo_ref[side, 1], zf[KAP2][side], None),
            (start_ref[:, me, :], conduct_ref[:, me, :], None),
        ]
        sides += along_rows(
            phi,
            kappa,
            (xrows[0][at : at + 1], xrows[0][at + 1 : at + 2]),
            (xrows[1][at : at + 1], xrows[1][at + 1 : at + 2]),
            flags_x,
        )
        sides += along_lanes(
            phi,
            kappa,
            columns(yt[0], at, at + 1, 0),
            columns(yt[1], at, at + 1, LANES - 1),
            flags_y,
        )
        z_first_sweep.append(step(phi + zf[SRC][side], zf[REA][side], kappa, sides))

    y_first_sweep = []
    for side in range(2):
        phi, phi2, kappa, kappa2, src, rea = [roll_lanes(yf[side], -f * nx) for f in range(6)]
        at = 2 * side
        sides = [(phi2, kappa2, None), (sf[side], roll_lanes(sf[side], -KAP1 * nx), None)]
        sides += along_rows(
            phi,
            kappa,
            (to_row(yt[side], 0), to_row(yt[side], 1)),
            (to_row(yt[side], 2), to_row(yt[side], 3)),
            flags_z,
        )
        sides += along_lanes(
            phi,
            kappa,
            columns(xcols[0], at, at + 1, 0),
            columns(xcols[1], at, at + 1, nx - 1),
            flags_x,
            nx - 1,
        )
        y_first_sweep.append(step(phi + src, rea, kappa, sides))

    def sweep(phis, x_phi, z_phi, y_phi):
        results = []
        for x in range(nx):
            phi, kappa = phis[x], conduct[x]
            sides = []
            if x:
                sides.append((phis[x - 1], conduct[x - 1], None))
            else:
                sides.append((x_phi[0], xf[KAP1][0], flags_x[0]))
            if x < nx - 1:
                sides.append((phis[x + 1], conduct[x + 1], None))
            else:
                sides.append((x_phi[1], xf[KAP1][1], flags_x[1]))
            sides += along_rows(
                phi,
                kappa,
                (z_phi[0][x : x + 1], zf[KAP1][0][x : x + 1]),
                (z_phi[1][x : x + 1], zf[KAP1][1][x : x + 1]),
                flags_z,
            )
            spot = KAP1 * nx + x
            sides += along_lanes(
                phi,
                kappa,
                (roll_lanes(y_phi[0], -x), roll_lanes(yf[0], -spot)),
                (roll_lanes(y_phi[1], LANES - 1 - x), roll_lanes(yf[1], LANES - 1 - spot)),
                flags_y,
            )
            results.append(step(start[x] + src_ref[x], rea_ref[x], kappa, sides))
        return results

    first = sweep(start, xf[PHI1], (zhalo_ref[0, 0], zhalo_ref[1, 0]), yf)
    second = sweep(first, x_first_sweep, z_first_sweep, y_first_sweep)
    for x in range(nx):
        out_ref[x] = second[x]


def swap(axis, first, second):
    count = lax.axis_size(axis)
    results = []
    for j, value in enumerate((first, second)):
        pairs = []
        for low in range(j, count - 1, 2):
            pairs += [(low, low + 1), (low + 1, low)]
        results.append(lax.ppermute(value, axis, pairs))
    return results


def call(kernel, operands, outs, smem=0):
    specs = [SMEM] * smem + [VMEM] * (len(operands) - smem)
    return pl.pallas_call(
        kernel,
        out_shape=[jax.ShapeDtypeStruct(shape, F32) for shape in outs],
        in_specs=specs,
        out_specs=[VMEM] * len(outs),
        compiler_params=PARAMS,
    )(*operands)


def on_device(old_field, new_home, conduct, reaction, source, coarse):
    nx, nz, ny = block = old_field.shape
    home = new_home[0, 0]
    slots = home.shape[0]
    rows, width = nz // slots, ny // slots
    line = lax.axis_size("gy")
    part = nx // RUN

    parts, src, rea, za, zb = call(
        prepare_kernel,
        (home, old_field, conduct, source, reaction, coarse),
        [(RUN, part + 1, rows, ny), block, block, (7, nx, ny), (7, nx, ny)],
        smem=1,
    )
    za, zb = swap("gz", za, zb)
    groups = [[i * RUN + k for k in range(RUN)] for i in range(line // RUN)]
    parts = lax.all_to_all(parts, "gy", 0, 0, tiled=True, axis_index_groups=groups)

    def address(*refs):
        address_kernel(*refs, width=width)

    (send,) = call(address, (parts, za, zb), [(line, part + 1, rows, ny)])
    recv = lax.all_to_all(send, "gy", 0, 0, tiled=True)
    start, zhalo, sya, syb = call(
        place_kernel,
        (home, recv, old_field, conduct, src, rea, za, zb),
        [block, (2, 2, nx, ny), (nz + nx, ny), (nz + nx, ny)],
        smem=1,
    )
    ya, yb = swap("gy", sya, syb)
    xa, xb = call(
        edge_kernel,
        (start, conduct, src, rea, zhalo, za, zb, ya, yb),
        [(7 * nz + 8, ny)] * 2,
    )
    xa, xb = swap("gx", xa, xb)
    (relaxed,) = call(
        sweeps_kernel,
        (start, conduct, src, rea, zhalo, za, zb, sya, syb, ya, yb, xa, xb),
        [block],
    )
    return relaxed


def solution(mesh):
    return jax.shard_map(
        on_device,
        mesh=mesh,
        in_specs=(P("gx", "gz", "gy"),) * 6,
        out_specs=P("gx", "gz", "gy"),
        check_vma=False,
    )
```

```python
import jax
import jax.numpy as jnp
from jax import lax
from jax.experimental import pallas as pl
from jax.experimental.pallas import tpu as pltpu
from jax.sharding import PartitionSpec as P

LANES = 128
RUN = 4
VMEM = pl.BlockSpec(memory_space=pltpu.VMEM)
SMEM = pl.BlockSpec(memory_space=pltpu.SMEM)
HBM = pl.BlockSpec(memory_space=pltpu.HBM)
PARAMS = pltpu.CompilerParams(vmem_limit_bytes=24 * 1024 * 1024)
F32 = jnp.float32

PHI1, PHI2, KAP1, KAP2, SRC, REA, RIM = range(7)


def lane_of(shape):
    return lax.broadcasted_iota(jnp.int32, shape, len(shape) - 1)


def row_of(shape):
    return lax.broadcasted_iota(jnp.int32, shape, len(shape) - 2)


def roll_lanes(value, shift):
    shift = shift % LANES
    return pltpu.roll(value, shift, value.ndim - 1) if shift else value


def roll_rows(value, shift):
    return pltpu.roll(value, shift % value.shape[0], 0)


def moved_slot(home_ref, slots):
    position = lax.axis_index("gy")
    slot = jnp.int32(0)
    target = jnp.int32(0)
    for j in range(slots):
        home = home_ref[j]
        leaves = home != position * slots + j
        slot = jnp.where(leaves, j, slot)
        target = jnp.where(leaves, home, target)
    return slot, target


def edges():
    flags = []
    for axis in ("gx", "gz", "gy"):
        index = lax.axis_index(axis)
        flags.append((index == 0, index == lax.axis_size(axis) - 1))
    return flags


def is_even(axis):
    return lax.rem(lax.axis_index(axis), 2) == 0


def write_pair(axis, first_ref, second_ref, index, low, high):
    even = is_even(axis)
    first_ref[index] = jnp.where(even, high, low)
    second_ref[index] = jnp.where(even, low, high)


def received(axis, first, second):
    even = is_even(axis)
    return jnp.where(even, second, first), jnp.where(even, first, second)


def sent(axis, first, second):
    even = is_even(axis)
    return jnp.where(even, second, first), jnp.where(even, first, second)


def doubler(count):
    half = lax.div(lax.broadcasted_iota(jnp.int32, (count, 2 * count), 1), 2)
    return (half == lax.broadcasted_iota(jnp.int32, (count, 2 * count), 0)).astype(F32)


def exact_dot(left, right):
    return jnp.dot(left, right, precision=lax.Precision.HIGHEST, preferred_element_type=F32)


def refine(coarse_ref):
    cx, cz, cy = coarse_ref.shape
    left, right = doubler(cz).T, doubler(cy)
    return [exact_dot(left, exact_dot(coarse_ref[x], right)) for x in range(cx)]


def face_kernel(
    home_ref, old_hbm, conduct_hbm, source_hbm, reaction_hbm, coarse_hbm,
    za_ref, zb_ref, rows_ref, coarse_ref, sems, coarse_sem,
):
    slots = home_ref.shape[0]
    width = LANES // slots
    nx, nz, _ = old_hbm.shape
    size = rows_ref.shape[3]
    copies = [pltpu.make_async_copy(coarse_hbm, coarse_ref, coarse_sem)]
    for i, ref in enumerate((old_hbm, conduct_hbm, source_hbm, reaction_hbm)):
        for side, begin in enumerate((0, nz - size)):
            copies.append(
                pltpu.make_async_copy(
                    ref.at[:, pl.ds(begin, size), :], rows_ref.at[i, side], sems.at[i, side]
                )
            )
    for copy in copies:
        copy.start()

    slot, target = moved_slot(home_ref, slots)
    device = lax.div(target, slots)
    back = LANES - width * slot
    (x_first, x_last), (z_first, z_last), (y_first, y_last) = edges()
    row, lane = row_of((nx, LANES)), lane_of((nx, LANES))
    note = jnp.where(lane < 3 * width, device, slot).astype(F32)
    inner = (
        ((row == 0) & x_first).astype(F32)
        + ((row == nx - 1) & x_last).astype(F32)
        + ((lane == 0) & y_first).astype(F32)
        + ((lane == LANES - 1) & y_last).astype(F32)
    )
    for copy in copies:
        copy.wait()
    cx, cz, cy = coarse_ref.shape
    left, right = doubler(cx).T, doubler(cy)

    def rims(first, second):
        near = pltpu.roll(first, lax.rem(back, LANES), 1)
        far = pltpu.roll(second, lax.rem(back + width, LANES), 1)
        return jnp.where(lane < width, near, jnp.where(lane < 2 * width, far, note))

    faces = []
    for side, first, second, end, edge in ((0, 0, 1, 0, z_first), (1, size - 1, size - 2, cz - 1, z_last)):
        refined = exact_dot(left, exact_dot(coarse_ref[:, end, :], right))
        old, old2 = rows_ref[0, side, :, first, :], rows_ref[0, side, :, second, :]
        kappa, kappa2 = rows_ref[1, side, :, first, :], rows_ref[1, side, :, second, :]
        weight = (inner + jnp.where(edge, 1.0, 0.0)) * kappa
        src = rows_ref[2, side, :, first, :] + weight * refined
        rea = 1.0 + rows_ref[3, side, :, first, :] + weight
        faces.append([old, old2, kappa, kappa2, src, rea, rims(old, old2)])
    for i in range(7):
        write_pair("gz", za_ref, zb_ref, i, faces[0][i], faces[1][i])


def split_kernel(home_ref, old_hbm, after_ref, *rest):
    del after_ref
    parts, (box_ref, old_ref, sems) = rest[:RUN], rest[RUN:]
    slots = home_ref.shape[0]
    width = LANES // slots
    nx, nz, _ = old_ref.shape
    copies = [
        pltpu.make_async_copy(old_hbm.at[x], old_ref.at[x], sems.at[x]) for x in range(nx)
    ]
    for copy in copies:
        copy.start()
    rows = nz // slots
    slot, target = moved_slot(home_ref, slots)
    device = lax.div(target, slots)
    planes = parts[0].shape[0] - 1
    group = lax.div(lane_of((rows, LANES)), width)
    for x in range(nx):
        copies[x].wait()
        box = jnp.zeros((rows, LANES), F32)
        for g in range(slots):
            shift = lax.rem(width * (g - slot) + LANES, LANES)
            rolled = pltpu.roll(old_ref[x, g * rows : (g + 1) * rows, :], shift, 1)
            box = jnp.where(group == g, rolled, box)
        box_ref[x // planes, x % planes] = box
    place = lax.rem(lax.axis_index("gy"), RUN)
    for j in range(RUN):
        parts[j][:planes] = box_ref[jnp.bitwise_xor(place, j)]
        parts[j][planes] = jnp.full((rows, LANES), device, jnp.int32).astype(F32)


def fold_kernel(conduct_ref, source_ref, reaction_ref, coarse_ref, after_ref, src_ref, rea_ref):
    del after_ref
    nx, nz, _ = conduct_ref.shape
    (x_first, x_last), (z_first, z_last), (y_first, y_last) = edges()
    refined = refine(coarse_ref)
    row, lane = row_of((nz, LANES)), lane_of((nz, LANES))
    inner = (
        ((row == 0) & z_first).astype(F32)
        + ((row == nz - 1) & z_last).astype(F32)
        + ((lane == 0) & y_first).astype(F32)
        + ((lane == LANES - 1) & y_last).astype(F32)
    )
    for x in range(nx):
        faces = inner
        if x == 0:
            faces = faces + jnp.where(x_first, 1.0, 0.0)
        if x == nx - 1:
            faces = faces + jnp.where(x_last, 1.0, 0.0)
        weight = faces * conduct_ref[x]
        src_ref[x] = source_ref[x] + weight * refined[x // 2]
        rea_ref[x] = 1.0 + reaction_ref[x] + weight


def address_kernel(*refs, width):
    parts, (za_ref, zb_ref, send_ref) = refs[:RUN], refs[RUN:]
    planes = send_ref.shape[1] - 1
    low, high = received("gz", za_ref[RIM], zb_ref[RIM])
    shape = low.shape
    lane = lane_of(shape)
    low_tag = jnp.broadcast_to(low[:, 2 * width : 2 * width + 1], shape)
    high_tag = jnp.broadcast_to(high[:, 2 * width : 2 * width + 1], shape)
    high = roll_lanes(high, 2 * width)
    lower = lane < 2 * width
    rims = jnp.where(lower, low, high)
    tag = jnp.where(lower, low_tag, high_tag)
    for device in range(send_ref.shape[0]):
        for i in range(planes):
            value = jnp.zeros(shape, F32)
            for part in parts:
                value = jnp.where(part[planes] == device, part[i], value)
            send_ref[device, i] = value
        send_ref[device, planes] = jnp.where(tag == device, rims, 0.0)


def spread(tile, offset, width):
    piece = jnp.where(lane_of(tile.shape) < width, roll_lanes(tile, -offset), 0.0)
    result = piece
    for shift in range(width, LANES, width):
        result = result + roll_lanes(piece, shift)
    return result


def place_kernel(
    home_ref, recv_ref, old_ref, conduct_ref, src_ref, rea_ref, za_ref, zb_ref,
    start_ref, zhalo_ref, ya_ref, yb_ref,
):
    slots = home_ref.shape[0]
    width = LANES // slots
    nx, nz, _ = old_ref.shape
    rows = nz // slots
    slot, _ = moved_slot(home_ref, slots)
    planes = recv_ref.shape[1] - 1
    run = nx // planes
    count = recv_ref.shape[0]
    here = lax.div(lane_of((rows, LANES)), width) == slot
    for k in range(run):
        for i in range(planes):
            x = k * planes + i
            arrived = recv_ref[k, i]
            for source in range(k + run, count, run):
                arrived = arrived + recv_ref[source, i]
            for g in range(slots):
                shift = lax.rem(width * (slot - g) + LANES, LANES)
                part = pl.ds(g * rows, rows)
                start_ref[x, part, :] = jnp.where(
                    here, pltpu.roll(arrived, shift, 1), old_ref[x, part, :]
                )

    rims = recv_ref[0, planes]
    for source in range(1, count):
        rims = rims + recv_ref[source, planes]
    faces = [received("gz", za_ref[i], zb_ref[i]) for i in range(7)]
    group = lax.div(lane_of((nx, LANES)), width).astype(F32)
    for side in range(2):
        note = faces[RIM][side]
        there = jnp.broadcast_to(note[:, 3 * width : 3 * width + 1], note.shape) == group
        for depth in range(2):
            moved = spread(rims, (2 * side + depth) * width, width)
            zhalo_ref[side, depth] = jnp.where(there, moved, faces[depth][side])

    lane = lane_of((nz, LANES))
    low = high = jnp.zeros((nz, LANES), F32)
    for f, (ref, depth) in enumerate(
        ((start_ref, 0), (start_ref, 1), (conduct_ref, 0), (conduct_ref, 1), (src_ref, 0), (rea_ref, 0))
    ):
        for x in range(nx):
            spot = f * nx + x
            low = jnp.where(lane == spot, roll_lanes(ref[x], spot - depth), low)
            high = jnp.where(lane == spot, roll_lanes(ref[x], spot + 1 + depth), high)
    write_pair("gy", ya_ref, yb_ref, slice(0, nz), low, high)
    lane = lane_of((nx, LANES))
    low = high = jnp.zeros((nx, LANES), F32)
    for side in range(2):
        for f, tile in enumerate((zhalo_ref[side, 0], faces[KAP1][side])):
            spot = 2 * side + f
            low = jnp.where(lane == spot, roll_lanes(tile, spot), low)
            high = jnp.where(lane == spot, roll_lanes(tile, spot + 1), high)
    write_pair("gy", ya_ref, yb_ref, slice(nz, nz + nx), low, high)


def edge_kernel(
    start_ref, conduct_ref, src_ref, rea_ref, zhalo_ref, za_ref, zb_ref, ya_ref, yb_ref,
    xa_ref, xb_ref,
):
    nx, nz, _ = start_ref.shape
    for f, (ref, depth) in enumerate(
        ((start_ref, 0), (start_ref, 1), (conduct_ref, 0), (conduct_ref, 1), (src_ref, 0), (rea_ref, 0))
    ):
        write_pair(
            "gx", xa_ref, xb_ref, slice(f * nz, (f + 1) * nz), ref[depth], ref[nx - 1 - depth]
        )
    base = 6 * nz
    kappas = received("gz", za_ref[KAP1], zb_ref[KAP1])
    xa_ref[base : base + 8] = jnp.zeros((8, LANES), F32)
    xb_ref[base : base + 8] = jnp.zeros((8, LANES), F32)
    for side in range(2):
        for f, tile in enumerate((zhalo_ref[side, 0], kappas[side])):
            spot = base + 2 * side + f
            write_pair(
                "gx", xa_ref, xb_ref, slice(spot, spot + 1), tile[0:1], tile[nx - 1 : nx]
            )
    lane = lane_of((nz, LANES))
    low = high = jnp.zeros((nz, LANES), F32)
    for side, halo in enumerate(received("gy", ya_ref[:nz], yb_ref[:nz])):
        for f, offset in enumerate((PHI1 * nx, KAP1 * nx)):
            spot = 2 * side + f
            low = jnp.where(lane == spot, roll_lanes(halo, spot - offset), low)
            high = jnp.where(lane == spot, roll_lanes(halo, spot - offset - nx + 1), high)
    write_pair("gx", xa_ref, xb_ref, slice(base + 8, base + 8 + nz), low, high)


def step(numerator, denominator, kappa, sides):
    for phi, beside, outside in sides:
        weight = 0.5 * (kappa + beside)
        if outside is not None:
            weight = jnp.where(outside, 0.0, weight)
        numerator = numerator + weight * phi
        denominator = denominator + weight
    return numerator / denominator


def along_rows(phi, kappa, low, high, flags):
    row = row_of(phi.shape)
    last = phi.shape[0] - 1
    low_edge, high_edge = row == 0, row == last
    return [
        (
            jnp.where(low_edge, low[0], roll_rows(phi, 1)),
            jnp.where(low_edge, low[1], roll_rows(kappa, 1)),
            low_edge & flags[0],
        ),
        (
            jnp.where(high_edge, high[0], roll_rows(phi, last)),
            jnp.where(high_edge, high[1], roll_rows(kappa, last)),
            high_edge & flags[1],
        ),
    ]


def along_lanes(phi, kappa, low, high, flags, last=LANES - 1):
    lane = lane_of(phi.shape)
    low_edge, high_edge = lane == 0, lane == last
    return [
        (
            jnp.where(low_edge, low[0], roll_lanes(phi, 1)),
            jnp.where(low_edge, low[1], roll_lanes(kappa, 1)),
            low_edge & flags[0],
        ),
        (
            jnp.where(high_edge, high[0], roll_lanes(phi, -1)),
            jnp.where(high_edge, high[1], roll_lanes(kappa, -1)),
            high_edge & flags[1],
        ),
    ]


def to_row(tile, spot):
    column = jnp.broadcast_to(tile[:, spot : spot + 1], tile.shape)
    return jnp.sum(
        jnp.where(lane_of(tile.shape) == row_of(tile.shape), column, 0.0), axis=0, keepdims=True
    )


def sweeps_kernel(
    start_ref, conduct_ref, src_ref, rea_ref, zhalo_ref,
    za_ref, zb_ref, sya_ref, syb_ref, ya_ref, yb_ref, xa_ref, xb_ref,
    out_ref,
):
    nx, nz, _ = start_ref.shape
    flags_x, flags_z, flags_y = edges()
    start = [start_ref[x] for x in range(nx)]
    conduct = [conduct_ref[x] for x in range(nx)]
    base = 6 * nz

    def part(axis, a_ref, b_ref, begin, size):
        return received(axis, a_ref[begin : begin + size], b_ref[begin : begin + size])

    xf = [part("gx", xa_ref, xb_ref, f * nz, nz) for f in range(6)]
    xrows = part("gx", xa_ref, xb_ref, base, 8)
    xcols = part("gx", xa_ref, xb_ref, base + 8, nz)
    zf = [received("gz", za_ref[i], zb_ref[i]) for i in range(6)]
    yf = part("gy", ya_ref, yb_ref, 0, nz)
    yt = part("gy", ya_ref, yb_ref, nz, nx)
    sf = sent("gy", sya_ref[:nz], syb_ref[:nz])

    def columns(tile, phi_spot, kappa_spot, lane):
        return roll_lanes(tile, lane - phi_spot), roll_lanes(tile, lane - kappa_spot)

    x_first_sweep = []
    for side in range(2):
        phi, kappa = xf[PHI1][side], xf[KAP1][side]
        me = 0 if side == 0 else nx - 1
        rows = xrows[side]
        sides = [(xf[PHI2][side], xf[KAP2][side], None), (start[me], conduct[me], None)]
        sides += along_rows(phi, kappa, (rows[0:1], rows[1:2]), (rows[2:3], rows[3:4]), flags_z)
        tile = xcols[side]
        sides += along_lanes(
            phi, kappa, columns(tile, 0, 1, 0), columns(tile, 2, 3, LANES - 1), flags_y
        )
        x_first_sweep.append(step(phi + xf[SRC][side], xf[REA][side], kappa, sides))

    z_first_sweep = []
    for side in range(2):
        phi, kappa = zhalo_ref[side, 0], zf[KAP1][side]
        me = 0 if side == 0 else nz - 1
        at = 2 * side
        sides = [
            (zhalo_ref[side, 1], zf[KAP2][side], None),
            (start_ref[:, me, :], conduct_ref[:, me, :], None),
        ]
        sides += along_rows(
            phi,
            kappa,
            (xrows[0][at : at + 1], xrows[0][at + 1 : at + 2]),
            (xrows[1][at : at + 1], xrows[1][at + 1 : at + 2]),
            flags_x,
        )
        sides += along_lanes(
            phi,
            kappa,
            columns(yt[0], at, at + 1, 0),
            columns(yt[1], at, at + 1, LANES - 1),
            flags_y,
        )
        z_first_sweep.append(step(phi + zf[SRC][side], zf[REA][side], kappa, sides))

    y_first_sweep = []
    for side in range(2):
        phi, phi2, kappa, kappa2, src, rea = [roll_lanes(yf[side], -f * nx) for f in range(6)]
        at = 2 * side
        sides = [(phi2, kappa2, None), (sf[side], roll_lanes(sf[side], -KAP1 * nx), None)]
        sides += along_rows(
            phi,
            kappa,
            (to_row(yt[side], 0), to_row(yt[side], 1)),
            (to_row(yt[side], 2), to_row(yt[side], 3)),
            flags_z,
        )
        sides += along_lanes(
            phi,
            kappa,
            columns(xcols[0], at, at + 1, 0),
            columns(xcols[1], at, at + 1, nx - 1),
            flags_x,
            nx - 1,
        )
        y_first_sweep.append(step(phi + src, rea, kappa, sides))

    def sweep(phis, x_phi, z_phi, y_phi):
        results = []
        for x in range(nx):
            phi, kappa = phis[x], conduct[x]
            sides = []
            if x:
                sides.append((phis[x - 1], conduct[x - 1], None))
            else:
                sides.append((x_phi[0], xf[KAP1][0], flags_x[0]))
            if x < nx - 1:
                sides.append((phis[x + 1], conduct[x + 1], None))
            else:
                sides.append((x_phi[1], xf[KAP1][1], flags_x[1]))
            sides += along_rows(
                phi,
                kappa,
                (z_phi[0][x : x + 1], zf[KAP1][0][x : x + 1]),
                (z_phi[1][x : x + 1], zf[KAP1][1][x : x + 1]),
                flags_z,
            )
            spot = KAP1 * nx + x
            sides += along_lanes(
                phi,
                kappa,
                (roll_lanes(y_phi[0], -x), roll_lanes(yf[0], -spot)),
                (roll_lanes(y_phi[1], LANES - 1 - x), roll_lanes(yf[1], LANES - 1 - spot)),
                flags_y,
            )
            results.append(step(start[x] + src_ref[x], rea_ref[x], kappa, sides))
        return results

    first = sweep(start, xf[PHI1], (zhalo_ref[0, 0], zhalo_ref[1, 0]), yf)
    second = sweep(first, x_first_sweep, z_first_sweep, y_first_sweep)
    for x in range(nx):
        out_ref[x] = second[x]


def swap(axis, first, second):
    count = lax.axis_size(axis)
    results = []
    for j, value in ((1, second), (0, first)):
        pairs = []
        for low in range(j, count - 1, 2):
            pairs += [(low, low + 1), (low + 1, low)]
        results.append(lax.ppermute(value, axis, pairs))
    return results[::-1]


def call(kernel, operands, outs, smem=0, hbm=(), scratch=()):
    specs = [SMEM] * smem + [VMEM] * (len(operands) - smem)
    operands = list(operands)
    for i in hbm:
        specs[i] = HBM
        operands[i] = pltpu.with_memory_space_constraint(operands[i], pltpu.HBM)
    return pl.pallas_call(
        kernel,
        out_shape=[jax.ShapeDtypeStruct(shape, F32) for shape in outs],
        in_specs=specs,
        out_specs=[VMEM] * len(outs),
        scratch_shapes=scratch,
        compiler_params=PARAMS,
    )(*operands)


def on_device(old_field, new_home, conduct, reaction, source, coarse):
    nx, nz, ny = block = old_field.shape
    home = new_home[0, 0]
    slots = home.shape[0]
    rows, width = nz // slots, ny // slots
    line = lax.axis_size("gy")
    part = nx // RUN

    sza, szb = call(
        face_kernel,
        (home, old_field, conduct, source, reaction, coarse),
        [(7, nx, ny), (7, nx, ny)],
        smem=1,
        hbm=(1, 2, 3, 4, 5),
        scratch=[
            pltpu.VMEM((4, 2, nx, 8, ny), F32),
            pltpu.VMEM(coarse.shape, F32),
            pltpu.SemaphoreType.DMA((4, 2)),
            pltpu.SemaphoreType.DMA,
        ],
    )
    za, zb = swap("gz", sza, szb)
    kept, *parts = call(
        split_kernel,
        (home, old_field, sza),
        [(part + 1, rows, ny)] * RUN,
        smem=1,
        hbm=(1,),
        scratch=[
            pltpu.VMEM((RUN, part, rows, ny), F32),
            pltpu.VMEM(block, F32),
            pltpu.SemaphoreType.DMA((nx,)),
        ],
    )
    src, rea = call(fold_kernel, (conduct, source, reaction, coarse, kept), [block, block])
    for j in range(1, RUN):
        pairs = [(i, i ^ j) for i in range(line)]
        parts[j - 1] = lax.ppermute(parts[j - 1], "gy", pairs)

    def address(*refs):
        address_kernel(*refs, width=width)

    (send,) = call(address, (kept, *parts, za, zb), [(line, part + 1, rows, ny)])
    recv = lax.all_to_all(send, "gy", 0, 0, tiled=True)
    start, zhalo, sya, syb = call(
        place_kernel,
        (home, recv, old_field, conduct, src, rea, za, zb),
        [block, (2, 2, nx, ny), (nz + nx, ny), (nz + nx, ny)],
        smem=1,
    )
    ya, yb = swap("gy", sya, syb)
    xa, xb = call(
        edge_kernel,
        (start, conduct, src, rea, zhalo, za, zb, ya, yb),
        [(7 * nz + 8, ny)] * 2,
    )
    xa, xb = swap("gx", xa, xb)
    (relaxed,) = call(
        sweeps_kernel,
        (start, conduct, src, rea, zhalo, za, zb, sya, syb, ya, yb, xa, xb),
        [block],
    )
    return relaxed


def solution(mesh):
    return jax.shard_map(
        on_device,
        mesh=mesh,
        in_specs=(P("gx", "gz", "gy"),) * 6,
        out_specs=P("gx", "gz", "gy"),
        check_vma=False,
    )
```

```python
import jax
import jax.numpy as jnp
from jax import lax
from jax.experimental import pallas as pl
from jax.experimental.pallas import tpu as pltpu
from jax.sharding import PartitionSpec as P

LANES = 128
RUN = 4
VMEM = pl.BlockSpec(memory_space=pltpu.VMEM)
SMEM = pl.BlockSpec(memory_space=pltpu.SMEM)
HBM = pl.BlockSpec(memory_space=pltpu.HBM)
PARAMS = pltpu.CompilerParams(vmem_limit_bytes=24 * 1024 * 1024)
F32 = jnp.float32

PHI1, PHI2, KAP1, KAP2, SRC, REA, RIM = range(7)


def lane_of(shape):
    return lax.broadcasted_iota(jnp.int32, shape, len(shape) - 1)


def row_of(shape):
    return lax.broadcasted_iota(jnp.int32, shape, len(shape) - 2)


def roll_lanes(value, shift):
    shift = shift % LANES
    return pltpu.roll(value, shift, value.ndim - 1) if shift else value


def roll_rows(value, shift):
    return pltpu.roll(value, shift % value.shape[0], 0)


def moved_slot(home_ref, slots):
    position = lax.axis_index("gy")
    slot = jnp.int32(0)
    target = jnp.int32(0)
    for j in range(slots):
        home = home_ref[j]
        leaves = home != position * slots + j
        slot = jnp.where(leaves, j, slot)
        target = jnp.where(leaves, home, target)
    return slot, target


def edges():
    flags = []
    for axis in ("gx", "gz", "gy"):
        index = lax.axis_index(axis)
        flags.append((index == 0, index == lax.axis_size(axis) - 1))
    return flags


def is_even(axis):
    return lax.rem(lax.axis_index(axis), 2) == 0


def write_pair(axis, first_ref, second_ref, index, low, high):
    even = is_even(axis)
    first_ref[index] = jnp.where(even, high, low)
    second_ref[index] = jnp.where(even, low, high)


def received(axis, first, second):
    even = is_even(axis)
    return jnp.where(even, second, first), jnp.where(even, first, second)


def sent(axis, first, second):
    even = is_even(axis)
    return jnp.where(even, second, first), jnp.where(even, first, second)


def doubler(count):
    half = lax.div(lax.broadcasted_iota(jnp.int32, (count, 2 * count), 1), 2)
    return (half == lax.broadcasted_iota(jnp.int32, (count, 2 * count), 0)).astype(F32)


def exact_dot(left, right):
    return jnp.dot(left, right, precision=lax.Precision.HIGHEST, preferred_element_type=F32)


def refine(coarse_ref):
    cx, cz, cy = coarse_ref.shape
    left, right = doubler(cz).T, doubler(cy)
    return [exact_dot(left, exact_dot(coarse_ref[x], right)) for x in range(cx)]


def first_kernel(
    home_ref, old_hbm, conduct_hbm, source_hbm, reaction_hbm, coarse_hbm,
    zb_ref, za_ref, parts_ref, old_ref, rows_ref, coarse_ref, old_sems, sems, coarse_sem,
):
    slots = home_ref.shape[0]
    width = LANES // slots
    nx, nz, _ = old_hbm.shape
    size = rows_ref.shape[3]
    copies = [pltpu.make_async_copy(coarse_hbm, coarse_ref, coarse_sem)]
    loads = [pltpu.make_async_copy(old_hbm.at[x], old_ref.at[x], old_sems.at[x]) for x in range(nx)]
    for i, ref in enumerate((conduct_hbm, source_hbm, reaction_hbm)):
        for side, begin in enumerate((0, nz - size)):
            copies.append(
                pltpu.make_async_copy(
                    ref.at[:, pl.ds(begin, size), :], rows_ref.at[i, side], sems.at[i, side]
                )
            )
    for copy in loads + copies:
        copy.start()

    slot, target = moved_slot(home_ref, slots)
    device = lax.div(target, slots)
    back = LANES - width * slot
    (x_first, x_last), (z_first, z_last), (y_first, y_last) = edges()
    row, lane = row_of((nx, LANES)), lane_of((nx, LANES))
    note = jnp.where(lane < 3 * width, device, slot).astype(F32)
    inner = (
        ((row == 0) & x_first).astype(F32)
        + ((row == nx - 1) & x_last).astype(F32)
        + ((lane == 0) & y_first).astype(F32)
        + ((lane == LANES - 1) & y_last).astype(F32)
    )
    rows = nz // slots
    count, planes = parts_ref.shape[0], parts_ref.shape[1] - 1
    group = lax.div(lane_of((rows, LANES)), width)
    for x in range(nx):
        loads[x].wait()
        box = jnp.zeros((rows, LANES), F32)
        for g in range(slots):
            shift = lax.rem(width * (g - slot) + LANES, LANES)
            rolled = pltpu.roll(old_ref[x, g * rows : (g + 1) * rows, :], shift, 1)
            box = jnp.where(group == g, rolled, box)
        parts_ref[x // planes, x % planes] = box
    for k in range(count):
        parts_ref[k, planes] = jnp.full((rows, LANES), device, jnp.int32).astype(F32)
    for copy in copies:
        copy.wait()
    cx, cz, cy = coarse_ref.shape
    left, right = doubler(cx).T, doubler(cy)

    def rims(first, second):
        near = pltpu.roll(first, lax.rem(back, LANES), 1)
        far = pltpu.roll(second, lax.rem(back + width, LANES), 1)
        return jnp.where(lane < width, near, jnp.where(lane < 2 * width, far, note))

    faces = []
    for side, first, second, end, edge in ((0, 0, 1, 0, z_first), (1, size - 1, size - 2, cz - 1, z_last)):
        refined = exact_dot(left, exact_dot(coarse_ref[:, end, :], right))
        top = side * (nz - size)
        old, old2 = old_ref[:, top + first, :], old_ref[:, top + second, :]
        kappa, kappa2 = rows_ref[0, side, :, first, :], rows_ref[0, side, :, second, :]
        weight = (inner + jnp.where(edge, 1.0, 0.0)) * kappa
        src = rows_ref[1, side, :, first, :] + weight * refined
        rea = 1.0 + rows_ref[2, side, :, first, :] + weight
        faces.append([old, old2, kappa, kappa2, src, rea, rims(old, old2)])
    for i in range(7):
        write_pair("gz", za_ref, zb_ref, i, faces[0][i], faces[1][i])


def fold_kernel(conduct_ref, source_ref, reaction_ref, coarse_ref, after_ref, src_ref, rea_ref):
    del after_ref
    nx, nz, _ = conduct_ref.shape
    (x_first, x_last), (z_first, z_last), (y_first, y_last) = edges()
    refined = refine(coarse_ref)
    row, lane = row_of((nz, LANES)), lane_of((nz, LANES))
    inner = (
        ((row == 0) & z_first).astype(F32)
        + ((row == nz - 1) & z_last).astype(F32)
        + ((lane == 0) & y_first).astype(F32)
        + ((lane == LANES - 1) & y_last).astype(F32)
    )
    for x in range(nx):
        faces = inner
        if x == 0:
            faces = faces + jnp.where(x_first, 1.0, 0.0)
        if x == nx - 1:
            faces = faces + jnp.where(x_last, 1.0, 0.0)
        weight = faces * conduct_ref[x]
        src_ref[x] = source_ref[x] + weight * refined[x // 2]
        rea_ref[x] = 1.0 + reaction_ref[x] + weight


def address_kernel(parts_ref, zb_ref, za_ref, send_ref, *, width):
    planes = send_ref.shape[1] - 1
    low, high = received("gz", za_ref[RIM], zb_ref[RIM])
    shape = low.shape
    lane = lane_of(shape)
    low_tag = jnp.broadcast_to(low[:, 2 * width : 2 * width + 1], shape)
    high_tag = jnp.broadcast_to(high[:, 2 * width : 2 * width + 1], shape)
    high = roll_lanes(high, 2 * width)
    lower = lane < 2 * width
    rims = jnp.where(lower, low, high)
    tag = jnp.where(lower, low_tag, high_tag)
    for device in range(send_ref.shape[0]):
        for i in range(planes):
            value = jnp.zeros(shape, F32)
            for k in range(parts_ref.shape[0]):
                value = jnp.where(parts_ref[k, planes] == device, parts_ref[k, i], value)
            send_ref[device, i] = value
        send_ref[device, planes] = jnp.where(tag == device, rims, 0.0)


def spread(tile, offset, width):
    piece = jnp.where(lane_of(tile.shape) < width, roll_lanes(tile, -offset), 0.0)
    result = piece
    for shift in range(width, LANES, width):
        result = result + roll_lanes(piece, shift)
    return result


def place_kernel(
    home_ref, recv_ref, old_ref, conduct_ref, src_ref, rea_ref, za_ref, zb_ref,
    start_ref, zhalo_ref, ya_ref, yb_ref,
):
    slots = home_ref.shape[0]
    width = LANES // slots
    nx, nz, _ = old_ref.shape
    rows = nz // slots
    slot, _ = moved_slot(home_ref, slots)
    planes = recv_ref.shape[1] - 1
    run = nx // planes
    count = recv_ref.shape[0]
    here = lax.div(lane_of((rows, LANES)), width) == slot
    for k in range(run):
        for i in range(planes):
            x = k * planes + i
            arrived = recv_ref[k, i]
            for source in range(k + run, count, run):
                arrived = arrived + recv_ref[source, i]
            for g in range(slots):
                shift = lax.rem(width * (slot - g) + LANES, LANES)
                part = pl.ds(g * rows, rows)
                start_ref[x, part, :] = jnp.where(
                    here, pltpu.roll(arrived, shift, 1), old_ref[x, part, :]
                )

    rims = recv_ref[0, planes]
    for source in range(1, count):
        rims = rims + recv_ref[source, planes]
    faces = [received("gz", za_ref[i], zb_ref[i]) for i in range(7)]
    group = lax.div(lane_of((nx, LANES)), width).astype(F32)
    for side in range(2):
        note = faces[RIM][side]
        there = jnp.broadcast_to(note[:, 3 * width : 3 * width + 1], note.shape) == group
        for depth in range(2):
            moved = spread(rims, (2 * side + depth) * width, width)
            zhalo_ref[side, depth] = jnp.where(there, moved, faces[depth][side])

    lane = lane_of((nz, LANES))
    low = high = jnp.zeros((nz, LANES), F32)
    for f, (ref, depth) in enumerate(
        ((start_ref, 0), (start_ref, 1), (conduct_ref, 0), (conduct_ref, 1), (src_ref, 0), (rea_ref, 0))
    ):
        for x in range(nx):
            spot = f * nx + x
            low = jnp.where(lane == spot, roll_lanes(ref[x], spot - depth), low)
            high = jnp.where(lane == spot, roll_lanes(ref[x], spot + 1 + depth), high)
    write_pair("gy", ya_ref, yb_ref, slice(0, nz), low, high)
    lane = lane_of((nx, LANES))
    low = high = jnp.zeros((nx, LANES), F32)
    for side in range(2):
        for f, tile in enumerate((zhalo_ref[side, 0], faces[KAP1][side])):
            spot = 2 * side + f
            low = jnp.where(lane == spot, roll_lanes(tile, spot), low)
            high = jnp.where(lane == spot, roll_lanes(tile, spot + 1), high)
    write_pair("gy", ya_ref, yb_ref, slice(nz, nz + nx), low, high)


def edge_kernel(
    start_ref, conduct_ref, src_ref, rea_ref, zhalo_ref, za_ref, zb_ref, ya_ref, yb_ref,
    xa_ref, xb_ref,
):
    nx, nz, _ = start_ref.shape
    for f, (ref, depth) in enumerate(
        ((start_ref, 0), (start_ref, 1), (conduct_ref, 0), (conduct_ref, 1), (src_ref, 0), (rea_ref, 0))
    ):
        write_pair(
            "gx", xa_ref, xb_ref, slice(f * nz, (f + 1) * nz), ref[depth], ref[nx - 1 - depth]
        )
    base = 6 * nz
    kappas = received("gz", za_ref[KAP1], zb_ref[KAP1])
    xa_ref[base : base + 8] = jnp.zeros((8, LANES), F32)
    xb_ref[base : base + 8] = jnp.zeros((8, LANES), F32)
    for side in range(2):
        for f, tile in enumerate((zhalo_ref[side, 0], kappas[side])):
            spot = base + 2 * side + f
            write_pair(
                "gx", xa_ref, xb_ref, slice(spot, spot + 1), tile[0:1], tile[nx - 1 : nx]
            )
    lane = lane_of((nz, LANES))
    low = high = jnp.zeros((nz, LANES), F32)
    for side, halo in enumerate(received("gy", ya_ref[:nz], yb_ref[:nz])):
        for f, offset in enumerate((PHI1 * nx, KAP1 * nx)):
            spot = 2 * side + f
            low = jnp.where(lane == spot, roll_lanes(halo, spot - offset), low)
            high = jnp.where(lane == spot, roll_lanes(halo, spot - offset - nx + 1), high)
    write_pair("gx", xa_ref, xb_ref, slice(base + 8, base + 8 + nz), low, high)


def step(numerator, denominator, kappa, sides):
    for phi, beside, outside in sides:
        weight = 0.5 * (kappa + beside)
        if outside is not None:
            weight = jnp.where(outside, 0.0, weight)
        numerator = numerator + weight * phi
        denominator = denominator + weight
    return numerator / denominator


def along_rows(phi, kappa, low, high, flags):
    row = row_of(phi.shape)
    last = phi.shape[0] - 1
    low_edge, high_edge = row == 0, row == last
    return [
        (
            jnp.where(low_edge, low[0], roll_rows(phi, 1)),
            jnp.where(low_edge, low[1], roll_rows(kappa, 1)),
            low_edge & flags[0],
        ),
        (
            jnp.where(high_edge, high[0], roll_rows(phi, last)),
            jnp.where(high_edge, high[1], roll_rows(kappa, last)),
            high_edge & flags[1],
        ),
    ]


def along_lanes(phi, kappa, low, high, flags, last=LANES - 1):
    lane = lane_of(phi.shape)
    low_edge, high_edge = lane == 0, lane == last
    return [
        (
            jnp.where(low_edge, low[0], roll_lanes(phi, 1)),
            jnp.where(low_edge, low[1], roll_lanes(kappa, 1)),
            low_edge & flags[0],
        ),
        (
            jnp.where(high_edge, high[0], roll_lanes(phi, -1)),
            jnp.where(high_edge, high[1], roll_lanes(kappa, -1)),
            high_edge & flags[1],
        ),
    ]


def to_row(tile, spot):
    column = jnp.broadcast_to(tile[:, spot : spot + 1], tile.shape)
    return jnp.sum(
        jnp.where(lane_of(tile.shape) == row_of(tile.shape), column, 0.0), axis=0, keepdims=True
    )


def sweeps_kernel(
    start_ref, conduct_ref, src_ref, rea_ref, zhalo_ref,
    za_ref, zb_ref, sya_ref, syb_ref, ya_ref, yb_ref, xa_ref, xb_ref,
    out_ref,
):
    nx, nz, _ = start_ref.shape
    flags_x, flags_z, flags_y = edges()
    start = [start_ref[x] for x in range(nx)]
    conduct = [conduct_ref[x] for x in range(nx)]
    base = 6 * nz

    def part(axis, a_ref, b_ref, begin, size):
        return received(axis, a_ref[begin : begin + size], b_ref[begin : begin + size])

    xf = [part("gx", xa_ref, xb_ref, f * nz, nz) for f in range(6)]
    xrows = part("gx", xa_ref, xb_ref, base, 8)
    xcols = part("gx", xa_ref, xb_ref, base + 8, nz)
    zf = [received("gz", za_ref[i], zb_ref[i]) for i in range(6)]
    yf = part("gy", ya_ref, yb_ref, 0, nz)
    yt = part("gy", ya_ref, yb_ref, nz, nx)
    sf = sent("gy", sya_ref[:nz], syb_ref[:nz])

    def columns(tile, phi_spot, kappa_spot, lane):
        return roll_lanes(tile, lane - phi_spot), roll_lanes(tile, lane - kappa_spot)

    x_first_sweep = []
    for side in range(2):
        phi, kappa = xf[PHI1][side], xf[KAP1][side]
        me = 0 if side == 0 else nx - 1
        rows = xrows[side]
        sides = [(xf[PHI2][side], xf[KAP2][side], None), (start[me], conduct[me], None)]
        sides += along_rows(phi, kappa, (rows[0:1], rows[1:2]), (rows[2:3], rows[3:4]), flags_z)
        tile = xcols[side]
        sides += along_lanes(
            phi, kappa, columns(tile, 0, 1, 0), columns(tile, 2, 3, LANES - 1), flags_y
        )
        x_first_sweep.append(step(phi + xf[SRC][side], xf[REA][side], kappa, sides))

    z_first_sweep = []
    for side in range(2):
        phi, kappa = zhalo_ref[side, 0], zf[KAP1][side]
        me = 0 if side == 0 else nz - 1
        at = 2 * side
        sides = [
            (zhalo_ref[side, 1], zf[KAP2][side], None),
            (start_ref[:, me, :], conduct_ref[:, me, :], None),
        ]
        sides += along_rows(
            phi,
            kappa,
            (xrows[0][at : at + 1], xrows[0][at + 1 : at + 2]),
            (xrows[1][at : at + 1], xrows[1][at + 1 : at + 2]),
            flags_x,
        )
        sides += along_lanes(
            phi,
            kappa,
            columns(yt[0], at, at + 1, 0),
            columns(yt[1], at, at + 1, LANES - 1),
            flags_y,
        )
        z_first_sweep.append(step(phi + zf[SRC][side], zf[REA][side], kappa, sides))

    y_first_sweep = []
    for side in range(2):
        phi, phi2, kappa, kappa2, src, rea = [roll_lanes(yf[side], -f * nx) for f in range(6)]
        at = 2 * side
        sides = [(phi2, kappa2, None), (sf[side], roll_lanes(sf[side], -KAP1 * nx), None)]
        sides += along_rows(
            phi,
            kappa,
            (to_row(yt[side], 0), to_row(yt[side], 1)),
            (to_row(yt[side], 2), to_row(yt[side], 3)),
            flags_z,
        )
        sides += along_lanes(
            phi,
            kappa,
            columns(xcols[0], at, at + 1, 0),
            columns(xcols[1], at, at + 1, nx - 1),
            flags_x,
            nx - 1,
        )
        y_first_sweep.append(step(phi + src, rea, kappa, sides))

    def sweep(phis, x_phi, z_phi, y_phi):
        results = []
        for x in range(nx):
            phi, kappa = phis[x], conduct[x]
            sides = []
            if x:
                sides.append((phis[x - 1], conduct[x - 1], None))
            else:
                sides.append((x_phi[0], xf[KAP1][0], flags_x[0]))
            if x < nx - 1:
                sides.append((phis[x + 1], conduct[x + 1], None))
            else:
                sides.append((x_phi[1], xf[KAP1][1], flags_x[1]))
            sides += along_rows(
                phi,
                kappa,
                (z_phi[0][x : x + 1], zf[KAP1][0][x : x + 1]),
                (z_phi[1][x : x + 1], zf[KAP1][1][x : x + 1]),
                flags_z,
            )
            spot = KAP1 * nx + x
            sides += along_lanes(
                phi,
                kappa,
                (roll_lanes(y_phi[0], -x), roll_lanes(yf[0], -spot)),
                (roll_lanes(y_phi[1], LANES - 1 - x), roll_lanes(yf[1], LANES - 1 - spot)),
                flags_y,
            )
            results.append(step(start[x] + src_ref[x], rea_ref[x], kappa, sides))
        return results

    first = sweep(start, xf[PHI1], (zhalo_ref[0, 0], zhalo_ref[1, 0]), yf)
    second = sweep(first, x_first_sweep, z_first_sweep, y_first_sweep)
    for x in range(nx):
        out_ref[x] = second[x]


def swap(axis, first, second):
    count = lax.axis_size(axis)
    results = []
    for j, value in ((1, second), (0, first)):
        pairs = []
        for low in range(j, count - 1, 2):
            pairs += [(low, low + 1), (low + 1, low)]
        results.append(lax.ppermute(value, axis, pairs))
    return results[::-1]


def call(kernel, operands, outs, smem=0, hbm=(), scratch=()):
    specs = [SMEM] * smem + [VMEM] * (len(operands) - smem)
    operands = list(operands)
    for i in hbm:
        specs[i] = HBM
        operands[i] = pltpu.with_memory_space_constraint(operands[i], pltpu.HBM)
    return pl.pallas_call(
        kernel,
        out_shape=[jax.ShapeDtypeStruct(shape, F32) for shape in outs],
        in_specs=specs,
        out_specs=[VMEM] * len(outs),
        scratch_shapes=scratch,
        compiler_params=PARAMS,
    )(*operands)


def on_device(old_field, new_home, conduct, reaction, source, coarse):
    nx, nz, ny = block = old_field.shape
    home = new_home[0, 0]
    slots = home.shape[0]
    rows, width = nz // slots, ny // slots
    line = lax.axis_size("gy")
    part = nx // RUN

    szb, sza, parts = call(
        first_kernel,
        (home, old_field, conduct, source, reaction, coarse),
        [(7, nx, ny), (7, nx, ny), (RUN, part + 1, rows, ny)],
        smem=1,
        hbm=(1, 2, 3, 4, 5),
        scratch=[
            pltpu.VMEM(block, F32),
            pltpu.VMEM((3, 2, nx, 8, ny), F32),
            pltpu.VMEM(coarse.shape, F32),
            pltpu.SemaphoreType.DMA((nx,)),
            pltpu.SemaphoreType.DMA((3, 2)),
            pltpu.SemaphoreType.DMA,
        ],
    )
    za, zb = swap("gz", sza, szb)
    groups = [[i * RUN + k for k in range(RUN)] for i in range(line // RUN)]
    parts = lax.all_to_all(parts, "gy", 0, 0, tiled=True, axis_index_groups=groups)
    src, rea = call(fold_kernel, (conduct, source, reaction, coarse, szb), [block, block])

    def address(*refs):
        address_kernel(*refs, width=width)

    (send,) = call(address, (parts, zb, za), [(line, part + 1, rows, ny)])
    recv = lax.all_to_all(send, "gy", 0, 0, tiled=True)
    start, zhalo, sya, syb = call(
        place_kernel,
        (home, recv, old_field, conduct, src, rea, za, zb),
        [block, (2, 2, nx, ny), (nz + nx, ny), (nz + nx, ny)],
        smem=1,
    )
    ya, yb = swap("gy", sya, syb)
    xa, xb = call(
        edge_kernel,
        (start, conduct, src, rea, zhalo, za, zb, ya, yb),
        [(7 * nz + 8, ny)] * 2,
    )
    xa, xb = swap("gx", xa, xb)
    (relaxed,) = call(
        sweeps_kernel,
        (start, conduct, src, rea, zhalo, za, zb, sya, syb, ya, yb, xa, xb),
        [block],
    )
    return relaxed


def solution(mesh):
    return jax.shard_map(
        on_device,
        mesh=mesh,
        in_specs=(P("gx", "gz", "gy"),) * 6,
        out_specs=P("gx", "gz", "gy"),
        check_vma=False,
    )
```

```python
import jax
import jax.numpy as jnp
from jax import lax
from jax.experimental import pallas as pl
from jax.experimental.pallas import tpu as pltpu
from jax.sharding import PartitionSpec as P

LANES = 128
RUN = 4
VMEM = pl.BlockSpec(memory_space=pltpu.VMEM)
SMEM = pl.BlockSpec(memory_space=pltpu.SMEM)
HBM = pl.BlockSpec(memory_space=pltpu.HBM)
PARAMS = pltpu.CompilerParams(vmem_limit_bytes=24 * 1024 * 1024)
F32 = jnp.float32

PHI1, PHI2, KAP1, KAP2, SRC, REA, RIM = range(7)


def lane_of(shape):
    return lax.broadcasted_iota(jnp.int32, shape, len(shape) - 1)


def row_of(shape):
    return lax.broadcasted_iota(jnp.int32, shape, len(shape) - 2)


def roll_lanes(value, shift):
    shift = shift % LANES
    return pltpu.roll(value, shift, value.ndim - 1) if shift else value


def roll_rows(value, shift):
    return pltpu.roll(value, shift % value.shape[0], 0)


def moved_slot(home_ref, slots):
    position = lax.axis_index("gy")
    slot = jnp.int32(0)
    target = jnp.int32(0)
    for j in range(slots):
        home = home_ref[j]
        leaves = home != position * slots + j
        slot = jnp.where(leaves, j, slot)
        target = jnp.where(leaves, home, target)
    return slot, target


def edges():
    flags = []
    for axis in ("gx", "gz", "gy"):
        index = lax.axis_index(axis)
        flags.append((index == 0, index == lax.axis_size(axis) - 1))
    return flags


def is_even(axis):
    return lax.rem(lax.axis_index(axis), 2) == 0


def write_pair(axis, first_ref, second_ref, index, low, high):
    even = is_even(axis)
    first_ref[index] = jnp.where(even, high, low)
    second_ref[index] = jnp.where(even, low, high)


def received(axis, first, second):
    even = is_even(axis)
    return jnp.where(even, second, first), jnp.where(even, first, second)


def sent(axis, first, second):
    even = is_even(axis)
    return jnp.where(even, second, first), jnp.where(even, first, second)


def doubler(count):
    half = lax.div(lax.broadcasted_iota(jnp.int32, (count, 2 * count), 1), 2)
    return (half == lax.broadcasted_iota(jnp.int32, (count, 2 * count), 0)).astype(F32)


def exact_dot(left, right):
    return jnp.dot(left, right, precision=lax.Precision.HIGHEST, preferred_element_type=F32)


def refine(coarse_ref):
    cx, cz, cy = coarse_ref.shape
    left, right = doubler(cz).T, doubler(cy)
    return [exact_dot(left, exact_dot(coarse_ref[x], right)) for x in range(cx)]


def first_kernel(
    home_ref, old_hbm, conduct_hbm, source_hbm, reaction_hbm, coarse_hbm,
    za_ref, zb_ref, parts_ref, old_ref, rows_ref, coarse_ref, old_sems, sems, coarse_sem,
):
    slots = home_ref.shape[0]
    width = LANES // slots
    nx, nz, _ = old_hbm.shape
    size = rows_ref.shape[3]
    copies = [pltpu.make_async_copy(coarse_hbm, coarse_ref, coarse_sem)]
    loads = [pltpu.make_async_copy(old_hbm.at[x], old_ref.at[x], old_sems.at[x]) for x in range(nx)]
    for i, ref in enumerate((conduct_hbm, source_hbm, reaction_hbm)):
        for side, begin in enumerate((0, nz - size)):
            copies.append(
                pltpu.make_async_copy(
                    ref.at[:, pl.ds(begin, size), :], rows_ref.at[i, side], sems.at[i, side]
                )
            )
    for copy in loads + copies:
        copy.start()

    slot, target = moved_slot(home_ref, slots)
    device = lax.div(target, slots)
    back = LANES - width * slot
    (x_first, x_last), (z_first, z_last), (y_first, y_last) = edges()
    row, lane = row_of((nx, LANES)), lane_of((nx, LANES))
    note = jnp.where(lane < 3 * width, device, slot).astype(F32)
    inner = (
        ((row == 0) & x_first).astype(F32)
        + ((row == nx - 1) & x_last).astype(F32)
        + ((lane == 0) & y_first).astype(F32)
        + ((lane == LANES - 1) & y_last).astype(F32)
    )
    rows = nz // slots
    count, planes = parts_ref.shape[0], parts_ref.shape[1] - 1
    group = lax.div(lane_of((rows, LANES)), width)
    for x in range(nx):
        loads[x].wait()
        box = jnp.zeros((rows, LANES), F32)
        for g in range(slots):
            shift = lax.rem(width * (g - slot) + LANES, LANES)
            rolled = pltpu.roll(old_ref[x, g * rows : (g + 1) * rows, :], shift, 1)
            box = jnp.where(group == g, rolled, box)
        parts_ref[x // planes, x % planes] = box
    for k in range(count):
        parts_ref[k, planes] = jnp.full((rows, LANES), device, jnp.int32).astype(F32)
    for copy in copies:
        copy.wait()
    cx, cz, cy = coarse_ref.shape
    left, right = doubler(cx).T, doubler(cy)

    def rims(first, second):
        near = pltpu.roll(first, lax.rem(back, LANES), 1)
        far = pltpu.roll(second, lax.rem(back + width, LANES), 1)
        return jnp.where(lane < width, near, jnp.where(lane < 2 * width, far, note))

    faces = []
    for side, first, second, end, edge in ((0, 0, 1, 0, z_first), (1, size - 1, size - 2, cz - 1, z_last)):
        refined = exact_dot(left, exact_dot(coarse_ref[:, end, :], right))
        top = side * (nz - size)
        old, old2 = old_ref[:, top + first, :], old_ref[:, top + second, :]
        kappa, kappa2 = rows_ref[0, side, :, first, :], rows_ref[0, side, :, second, :]
        weight = (inner + jnp.where(edge, 1.0, 0.0)) * kappa
        src = rows_ref[1, side, :, first, :] + weight * refined
        rea = 1.0 + rows_ref[2, side, :, first, :] + weight
        faces.append([old, old2, kappa, kappa2, src, rea, rims(old, old2)])
    for i in range(7):
        write_pair("gz", za_ref, zb_ref, i, faces[0][i], faces[1][i])


def fold_kernel(
    home_ref, old_ref, conduct_ref, source_ref, reaction_ref, coarse_ref, za_ref, zb_ref,
    src_ref, rea_ref, ya_ref, yb_ref,
):
    slots = home_ref.shape[0]
    width = LANES // slots
    nx, nz, _ = conduct_ref.shape
    (x_first, x_last), (z_first, z_last), (y_first, y_last) = edges()
    refined = refine(coarse_ref)
    row, lane = row_of((nz, LANES)), lane_of((nz, LANES))
    inner = (
        ((row == 0) & z_first).astype(F32)
        + ((row == nz - 1) & z_last).astype(F32)
        + ((lane == 0) & y_first).astype(F32)
        + ((lane == LANES - 1) & y_last).astype(F32)
    )
    for x in range(nx):
        faces = inner
        if x == 0:
            faces = faces + jnp.where(x_first, 1.0, 0.0)
        if x == nx - 1:
            faces = faces + jnp.where(x_last, 1.0, 0.0)
        weight = faces * conduct_ref[x]
        src_ref[x] = source_ref[x] + weight * refined[x // 2]
        rea_ref[x] = 1.0 + reaction_ref[x] + weight

    low = high = jnp.zeros((nz, LANES), F32)
    for f, (ref, depth) in enumerate(
        ((old_ref, 0), (old_ref, 1), (conduct_ref, 0), (conduct_ref, 1), (src_ref, 0), (rea_ref, 0))
    ):
        for x in range(nx):
            spot = f * nx + x
            low = jnp.where(lane == spot, roll_lanes(ref[x], spot - depth), low)
            high = jnp.where(lane == spot, roll_lanes(ref[x], spot + 1 + depth), high)
    write_pair("gy", ya_ref, yb_ref, slice(0, nz), low, high)

    lane = lane_of((nx, LANES))
    slot, _ = moved_slot(home_ref, slots)
    low = high = jnp.where(lane == 4, slot, 0).astype(F32)
    notes = received("gz", za_ref[RIM], zb_ref[RIM])
    for side in range(2):
        note = jnp.broadcast_to(notes[side][:, 3 * width : 3 * width + 1], (nx, LANES))
        low = jnp.where(lane == 5 + side, note, low)
        high = jnp.where(lane == 5 + side, note, high)
        for f, tile in enumerate((PHI1, KAP1)):
            value = received("gz", za_ref[tile], zb_ref[tile])[side]
            spot = 2 * side + f
            low = jnp.where(lane == spot, roll_lanes(value, spot), low)
            high = jnp.where(lane == spot, roll_lanes(value, spot + 1), high)
    write_pair("gy", ya_ref, yb_ref, slice(nz, nz + nx), low, high)


def address_kernel(parts_ref, za_ref, zb_ref, send_ref, *, width):
    planes = send_ref.shape[1] - 2
    low, high = received("gz", za_ref[RIM], zb_ref[RIM])
    shape = low.shape
    lane = lane_of(shape)
    low_tag = jnp.broadcast_to(low[:, 2 * width : 2 * width + 1], shape)
    high_tag = jnp.broadcast_to(high[:, 2 * width : 2 * width + 1], shape)
    high = roll_lanes(high, 2 * width)
    lower = lane < 2 * width
    rims = jnp.where(lower, low, high)
    tag = jnp.where(lower, low_tag, high_tag)
    column = lax.rem(lane, width)
    beside = jnp.where(column < 2, -1.0, jnp.where(column >= width - 2, 1.0, -4096.0))
    edge = jnp.where(column == 0, -1.0, jnp.where(column == width - 1, 1.0, -4096.0))
    count = parts_ref.shape[0]
    columns = [
        (roll_lanes(parts_ref[k, planes] + beside, 4 * i), roll_lanes(parts_ref[k, i], 4 * i))
        for k in range(count)
        for i in range(planes)
    ]
    columns.append((roll_lanes(tag + edge, 4 * planes), roll_lanes(rims, 4 * planes)))
    for device in range(send_ref.shape[0]):
        for i in range(planes):
            value = jnp.zeros(shape, F32)
            for k in range(count):
                value = jnp.where(parts_ref[k, planes] == device, parts_ref[k, i], value)
            send_ref[device, i] = value
        send_ref[device, planes] = jnp.where(tag == device, rims, 0.0)
        value = jnp.zeros(shape, F32)
        for spot, source in columns:
            value = jnp.where(spot == device, source, value)
        send_ref[device, planes + 1] = value


def spread(tile, offset, width):
    piece = jnp.where(lane_of(tile.shape) < width, roll_lanes(tile, -offset), 0.0)
    result = piece
    for shift in range(width, LANES, width):
        result = result + roll_lanes(piece, shift)
    return result


def place_kernel(
    home_ref, recv_ref, old_ref, za_ref, zb_ref, ya_ref, yb_ref,
    start_ref, zhalo_ref, yhalo_ref, own_ref,
):
    slots = home_ref.shape[0]
    width = LANES // slots
    nx, nz, _ = old_ref.shape
    rows = nz // slots
    slot, _ = moved_slot(home_ref, slots)
    planes = recv_ref.shape[1] - 2
    run = nx // planes
    count = recv_ref.shape[0]
    here = lax.div(lane_of((rows, LANES)), width) == slot

    def total(first, stride, tile):
        value = recv_ref[first, tile]
        for source in range(first + stride, count, stride):
            value = value + recv_ref[source, tile]
        return value

    for k in range(run):
        for i in range(planes):
            x = k * planes + i
            arrived = total(k, run, i)
            for g in range(slots):
                shift = lax.rem(width * (slot - g) + LANES, LANES)
                part = pl.ds(g * rows, rows)
                start_ref[x, part, :] = jnp.where(
                    here, pltpu.roll(arrived, shift, 1), old_ref[x, part, :]
                )

    rims = total(0, 1, planes)
    faces = [received("gz", za_ref[i], zb_ref[i]) for i in range(7)]
    group = lax.div(lane_of((nx, LANES)), width).astype(F32)
    for side in range(2):
        note = faces[RIM][side]
        there = jnp.broadcast_to(note[:, 3 * width : 3 * width + 1], note.shape) == group
        for depth in range(2):
            moved = spread(rims, (2 * side + depth) * width, width)
            zhalo_ref[side, depth] = jnp.where(there, moved, faces[depth][side])

    beside = [total(k, run, planes + 1) for k in range(run)]
    every = beside[0]
    for k in range(1, run):
        every = every + beside[k]
    lane = lane_of((rows, LANES))
    corner_lane = lane_of((nx, LANES))
    halos = received("gy", ya_ref[:nz], yb_ref[:nz])
    corners = received("gy", ya_ref[nz : nz + nx], yb_ref[nz : nz + nx])
    for side in range(2):
        outer = width - 1 if side == 0 else 0
        inward = -1 if side == 0 else 1
        touched = float(slots - 1 if side == 0 else 0)
        note = jnp.broadcast_to(corners[side][0:1, 4:5], (rows, LANES)) == touched
        for g in range(slots):
            value = jnp.zeros((rows, LANES), F32)
            for x in range(nx):
                source = beside[x // planes]
                for depth in range(2):
                    at = g * width + outer + inward * depth + 4 * (x % planes)
                    spot = depth * nx + x
                    value = jnp.where(lane == spot, roll_lanes(source, spot - at), value)
            held = halos[side][g * rows : (g + 1) * rows]
            yhalo_ref[side, g * rows : (g + 1) * rows] = jnp.where(
                note & (lane < 2 * nx), value, held
            )
        corner = corners[side]
        for z_side in range(2):
            note = jnp.broadcast_to(corner[:, 5 + z_side : 6 + z_side], (nx, LANES)) == touched
            at = 2 * width * z_side + outer + 4 * planes
            spot = 2 * z_side
            corner = jnp.where(
                note & (corner_lane == spot), roll_lanes(every, spot - at), corner
            )
        yhalo_ref[side, nz : nz + nx] = corner

    lane = lane_of((nz, LANES))
    low = high = jnp.zeros((nz, LANES), F32)
    for x in range(nx):
        low = jnp.where(lane == x, roll_lanes(start_ref[x], x), low)
        high = jnp.where(lane == x, roll_lanes(start_ref[x], x + 1), high)
    own_ref[0] = low
    own_ref[1] = high


def edge_kernel(
    start_ref, conduct_ref, src_ref, rea_ref, zhalo_ref, yhalo_ref, za_ref, zb_ref,
    xa_ref, xb_ref,
):
    nx, nz, _ = start_ref.shape
    for f, (ref, depth) in enumerate(
        ((start_ref, 0), (start_ref, 1), (conduct_ref, 0), (conduct_ref, 1), (src_ref, 0), (rea_ref, 0))
    ):
        write_pair(
            "gx", xa_ref, xb_ref, slice(f * nz, (f + 1) * nz), ref[depth], ref[nx - 1 - depth]
        )
    base = 6 * nz
    kappas = received("gz", za_ref[KAP1], zb_ref[KAP1])
    xa_ref[base : base + 8] = jnp.zeros((8, LANES), F32)
    xb_ref[base : base + 8] = jnp.zeros((8, LANES), F32)
    for side in range(2):
        for f, tile in enumerate((zhalo_ref[side, 0], kappas[side])):
            spot = base + 2 * side + f
            write_pair(
                "gx", xa_ref, xb_ref, slice(spot, spot + 1), tile[0:1], tile[nx - 1 : nx]
            )
    lane = lane_of((nz, LANES))
    low = high = jnp.zeros((nz, LANES), F32)
    for side in range(2):
        halo = yhalo_ref[side, :nz]
        for f, offset in enumerate((PHI1 * nx, KAP1 * nx)):
            spot = 2 * side + f
            low = jnp.where(lane == spot, roll_lanes(halo, spot - offset), low)
            high = jnp.where(lane == spot, roll_lanes(halo, spot - offset - nx + 1), high)
    write_pair("gx", xa_ref, xb_ref, slice(base + 8, base + 8 + nz), low, high)


def step(numerator, denominator, kappa, sides):
    for phi, beside, outside in sides:
        weight = 0.5 * (kappa + beside)
        if outside is not None:
            weight = jnp.where(outside, 0.0, weight)
        numerator = numerator + weight * phi
        denominator = denominator + weight
    return numerator / denominator


def along_rows(phi, kappa, low, high, flags):
    row = row_of(phi.shape)
    last = phi.shape[0] - 1
    low_edge, high_edge = row == 0, row == last
    return [
        (
            jnp.where(low_edge, low[0], roll_rows(phi, 1)),
            jnp.where(low_edge, low[1], roll_rows(kappa, 1)),
            low_edge & flags[0],
        ),
        (
            jnp.where(high_edge, high[0], roll_rows(phi, last)),
            jnp.where(high_edge, high[1], roll_rows(kappa, last)),
            high_edge & flags[1],
        ),
    ]


def along_lanes(phi, kappa, low, high, flags, last=LANES - 1):
    lane = lane_of(phi.shape)
    low_edge, high_edge = lane == 0, lane == last
    return [
        (
            jnp.where(low_edge, low[0], roll_lanes(phi, 1)),
            jnp.where(low_edge, low[1], roll_lanes(kappa, 1)),
            low_edge & flags[0],
        ),
        (
            jnp.where(high_edge, high[0], roll_lanes(phi, -1)),
            jnp.where(high_edge, high[1], roll_lanes(kappa, -1)),
            high_edge & flags[1],
        ),
    ]


def to_row(tile, spot):
    column = jnp.broadcast_to(tile[:, spot : spot + 1], tile.shape)
    return jnp.sum(
        jnp.where(lane_of(tile.shape) == row_of(tile.shape), column, 0.0), axis=0, keepdims=True
    )


def sweeps_kernel(
    start_ref, conduct_ref, src_ref, rea_ref, zhalo_ref, yhalo_ref, own_ref,
    za_ref, zb_ref, sya_ref, syb_ref, xa_ref, xb_ref,
    out_ref,
):
    nx, nz, _ = start_ref.shape
    flags_x, flags_z, flags_y = edges()
    start = [start_ref[x] for x in range(nx)]
    conduct = [conduct_ref[x] for x in range(nx)]
    base = 6 * nz

    def part(axis, a_ref, b_ref, begin, size):
        return received(axis, a_ref[begin : begin + size], b_ref[begin : begin + size])

    xf = [part("gx", xa_ref, xb_ref, f * nz, nz) for f in range(6)]
    xrows = part("gx", xa_ref, xb_ref, base, 8)
    xcols = part("gx", xa_ref, xb_ref, base + 8, nz)
    zf = [received("gz", za_ref[i], zb_ref[i]) for i in range(6)]
    yf = [yhalo_ref[side, :nz] for side in range(2)]
    yt = [yhalo_ref[side, nz : nz + nx] for side in range(2)]
    sf = sent("gy", sya_ref[:nz], syb_ref[:nz])

    def columns(tile, phi_spot, kappa_spot, lane):
        return roll_lanes(tile, lane - phi_spot), roll_lanes(tile, lane - kappa_spot)

    x_first_sweep = []
    for side in range(2):
        phi, kappa = xf[PHI1][side], xf[KAP1][side]
        me = 0 if side == 0 else nx - 1
        rows = xrows[side]
        sides = [(xf[PHI2][side], xf[KAP2][side], None), (start[me], conduct[me], None)]
        sides += along_rows(phi, kappa, (rows[0:1], rows[1:2]), (rows[2:3], rows[3:4]), flags_z)
        tile = xcols[side]
        sides += along_lanes(
            phi, kappa, columns(tile, 0, 1, 0), columns(tile, 2, 3, LANES - 1), flags_y
        )
        x_first_sweep.append(step(phi + xf[SRC][side], xf[REA][side], kappa, sides))

    z_first_sweep = []
    for side in range(2):
        phi, kappa = zhalo_ref[side, 0], zf[KAP1][side]
        me = 0 if side == 0 else nz - 1
        at = 2 * side
        sides = [
            (zhalo_ref[side, 1], zf[KAP2][side], None),
            (start_ref[:, me, :], conduct_ref[:, me, :], None),
        ]
        sides += along_rows(
            phi,
            kappa,
            (xrows[0][at : at + 1], xrows[0][at + 1 : at + 2]),
            (xrows[1][at : at + 1], xrows[1][at + 1 : at + 2]),
            flags_x,
        )
        sides += along_lanes(
            phi,
            kappa,
            columns(yt[0], at, at + 1, 0),
            columns(yt[1], at, at + 1, LANES - 1),
            flags_y,
        )
        z_first_sweep.append(step(phi + zf[SRC][side], zf[REA][side], kappa, sides))

    y_first_sweep = []
    for side in range(2):
        phi, phi2, kappa, kappa2, src, rea = [roll_lanes(yf[side], -f * nx) for f in range(6)]
        at = 2 * side
        sides = [(phi2, kappa2, None), (own_ref[side], roll_lanes(sf[side], -KAP1 * nx), None)]
        sides += along_rows(
            phi,
            kappa,
            (to_row(yt[side], 0), to_row(yt[side], 1)),
            (to_row(yt[side], 2), to_row(yt[side], 3)),
            flags_z,
        )
        sides += along_lanes(
            phi,
            kappa,
            columns(xcols[0], at, at + 1, 0),
            columns(xcols[1], at, at + 1, nx - 1),
            flags_x,
            nx - 1,
        )
        y_first_sweep.append(step(phi + src, rea, kappa, sides))

    def sweep(phis, x_phi, z_phi, y_phi):
        results = []
        for x in range(nx):
            phi, kappa = phis[x], conduct[x]
            sides = []
            if x:
                sides.append((phis[x - 1], conduct[x - 1], None))
            else:
                sides.append((x_phi[0], xf[KAP1][0], flags_x[0]))
            if x < nx - 1:
                sides.append((phis[x + 1], conduct[x + 1], None))
            else:
                sides.append((x_phi[1], xf[KAP1][1], flags_x[1]))
            sides += along_rows(
                phi,
                kappa,
                (z_phi[0][x : x + 1], zf[KAP1][0][x : x + 1]),
                (z_phi[1][x : x + 1], zf[KAP1][1][x : x + 1]),
                flags_z,
            )
            spot = KAP1 * nx + x
            sides += along_lanes(
                phi,
                kappa,
                (roll_lanes(y_phi[0], -x), roll_lanes(yf[0], -spot)),
                (roll_lanes(y_phi[1], LANES - 1 - x), roll_lanes(yf[1], LANES - 1 - spot)),
                flags_y,
            )
            results.append(step(start[x] + src_ref[x], rea_ref[x], kappa, sides))
        return results

    first = sweep(start, xf[PHI1], (zhalo_ref[0, 0], zhalo_ref[1, 0]), yf)
    second = sweep(first, x_first_sweep, z_first_sweep, y_first_sweep)
    for x in range(nx):
        out_ref[x] = second[x]


def swap(axis, first, second):
    count = lax.axis_size(axis)
    results = []
    for j, value in ((1, second), (0, first)):
        pairs = []
        for low in range(j, count - 1, 2):
            pairs += [(low, low + 1), (low + 1, low)]
        results.append(lax.ppermute(value, axis, pairs))
    return results[::-1]


def call(kernel, operands, outs, smem=0, hbm=(), scratch=()):
    specs = [SMEM] * smem + [VMEM] * (len(operands) - smem)
    operands = list(operands)
    for i in hbm:
        specs[i] = HBM
        operands[i] = pltpu.with_memory_space_constraint(operands[i], pltpu.HBM)
    return pl.pallas_call(
        kernel,
        out_shape=[jax.ShapeDtypeStruct(shape, F32) for shape in outs],
        in_specs=specs,
        out_specs=[VMEM] * len(outs),
        scratch_shapes=scratch,
        compiler_params=PARAMS,
    )(*operands)


def on_device(old_field, new_home, conduct, reaction, source, coarse):
    nx, nz, ny = block = old_field.shape
    home = new_home[0, 0]
    slots = home.shape[0]
    rows, width = nz // slots, ny // slots
    line = lax.axis_size("gy")
    part = nx // RUN

    sza, szb, parts = call(
        first_kernel,
        (home, old_field, conduct, source, reaction, coarse),
        [(7, nx, ny), (7, nx, ny), (RUN, part + 1, rows, ny)],
        smem=1,
        hbm=(1, 2, 3, 4, 5),
        scratch=[
            pltpu.VMEM(block, F32),
            pltpu.VMEM((3, 2, nx, 8, ny), F32),
            pltpu.VMEM(coarse.shape, F32),
            pltpu.SemaphoreType.DMA((nx,)),
            pltpu.SemaphoreType.DMA((3, 2)),
            pltpu.SemaphoreType.DMA,
        ],
    )
    za, zb = swap("gz", sza, szb)
    groups = [[i * RUN + k for k in range(RUN)] for i in range(line // RUN)]
    parts = lax.all_to_all(parts, "gy", 0, 0, tiled=True, axis_index_groups=groups)

    def address(*refs):
        address_kernel(*refs, width=width)

    (send,) = call(address, (parts, za, zb), [(line, part + 2, rows, ny)])
    recv = lax.all_to_all(send, "gy", 0, 0, tiled=True)
    src, rea, sya, syb = call(
        fold_kernel,
        (home, old_field, conduct, source, reaction, coarse, za, zb),
        [block, block, (nz + nx, ny), (nz + nx, ny)],
        smem=1,
    )
    ya, yb = swap("gy", sya, syb)
    start, zhalo, yhalo, own = call(
        place_kernel,
        (home, recv, old_field, za, zb, ya, yb),
        [block, (2, 2, nx, ny), (2, nz + nx, ny), (2, nz, ny)],
        smem=1,
    )
    xa, xb = call(
        edge_kernel,
        (start, conduct, src, rea, zhalo, yhalo, za, zb),
        [(7 * nz + 8, ny)] * 2,
    )
    xa, xb = swap("gx", xa, xb)
    (relaxed,) = call(
        sweeps_kernel,
        (start, conduct, src, rea, zhalo, yhalo, own, za, zb, sya, syb, xa, xb),
        [block],
    )
    return relaxed


def solution(mesh):
    return jax.shard_map(
        on_device,
        mesh=mesh,
        in_specs=(P("gx", "gz", "gy"),) * 6,
        out_specs=P("gx", "gz", "gy"),
        check_vma=False,
    )
```

```python
import jax
import jax.numpy as jnp
from jax import lax
from jax.experimental import pallas as pl
from jax.experimental.pallas import tpu as pltpu
from jax.sharding import PartitionSpec as P

LANES = 128
RUN = 4
VMEM = pl.BlockSpec(memory_space=pltpu.VMEM)
SMEM = pl.BlockSpec(memory_space=pltpu.SMEM)
HBM = pl.BlockSpec(memory_space=pltpu.HBM)
PARAMS = pltpu.CompilerParams(vmem_limit_bytes=24 * 1024 * 1024)
F32 = jnp.float32

PHI1, PHI2, KAP1, KAP2, SRC, REA, HALO = range(7)


def lane_of(shape):
    return lax.broadcasted_iota(jnp.int32, shape, len(shape) - 1)


def row_of(shape):
    return lax.broadcasted_iota(jnp.int32, shape, len(shape) - 2)


def roll_lanes(value, shift):
    shift = shift % LANES
    return pltpu.roll(value, shift, value.ndim - 1) if shift else value


def roll_rows(value, shift):
    return pltpu.roll(value, shift % value.shape[0], 0)


def moved_slot(home_of, slots):
    position = lax.axis_index("gy")
    slot = jnp.int32(0)
    target = jnp.int32(0)
    for j in range(slots):
        home = home_of(j)
        leaves = home != position * slots + j
        slot = jnp.where(leaves, j, slot)
        target = jnp.where(leaves, home, target)
    return slot, target


def edges():
    flags = []
    for axis in ("gx", "gz", "gy"):
        index = lax.axis_index(axis)
        flags.append((index == 0, index == lax.axis_size(axis) - 1))
    return flags


def is_even(axis):
    return lax.rem(lax.axis_index(axis), 2) == 0


def write_pair(axis, first_ref, second_ref, index, low, high):
    even = is_even(axis)
    first_ref[index] = jnp.where(even, high, low)
    second_ref[index] = jnp.where(even, low, high)


def received(axis, first, second):
    even = is_even(axis)
    return jnp.where(even, second, first), jnp.where(even, first, second)


def sent(axis, first, second):
    even = is_even(axis)
    return jnp.where(even, second, first), jnp.where(even, first, second)


def doubler(count):
    half = lax.div(lax.broadcasted_iota(jnp.int32, (count, 2 * count), 1), 2)
    return (half == lax.broadcasted_iota(jnp.int32, (count, 2 * count), 0)).astype(F32)


def exact_dot(left, right):
    return jnp.dot(left, right, precision=lax.Precision.HIGHEST, preferred_element_type=F32)


def refine(coarse_ref):
    cx, cz, cy = coarse_ref.shape
    left, right = doubler(cz).T, doubler(cy)
    return [exact_dot(left, exact_dot(coarse_ref[x], right)) for x in range(cx)]


def split_kernel(home_hbm, old_hbm, parts_ref, home_ref, old_ref, home_sem, sems):
    nx, nz, _ = old_ref.shape
    load_home = pltpu.make_async_copy(home_hbm, home_ref, home_sem)
    loads = [pltpu.make_async_copy(old_hbm.at[x], old_ref.at[x], sems.at[x]) for x in range(nx)]
    load_home.start()
    for load in loads:
        load.start()
    load_home.wait()
    slots = home_ref.shape[2]
    width = LANES // slots
    rows = nz // slots
    slot, target = moved_slot(lambda j: home_ref[0, 0, j], slots)
    device = lax.div(target, slots)
    count, planes = parts_ref.shape[0], parts_ref.shape[1] - 1
    group = lax.div(lane_of((rows, LANES)), width)
    for k in range(count):
        parts_ref[k, planes] = jnp.full((rows, LANES), device, jnp.int32).astype(F32)
    for x in range(nx):
        loads[x].wait()
        box = jnp.zeros((rows, LANES), F32)
        for g in range(slots):
            shift = lax.rem(width * (g - slot) + LANES, LANES)
            rolled = pltpu.roll(old_ref[x, g * rows : (g + 1) * rows, :], shift, 1)
            box = jnp.where(group == g, rolled, box)
        parts_ref[x // planes, x % planes] = box


def fold_kernel(
    home_ref, old_ref, conduct_ref, source_ref, reaction_ref, coarse_ref, after_ref,
    src_ref, rea_ref, ya_ref, yb_ref,
):
    del after_ref
    slots = home_ref.shape[0]
    nx, nz, _ = conduct_ref.shape
    (x_first, x_last), (z_first, z_last), (y_first, y_last) = edges()
    refined = refine(coarse_ref)
    row, lane = row_of((nz, LANES)), lane_of((nz, LANES))
    inner = (
        ((row == 0) & z_first).astype(F32)
        + ((row == nz - 1) & z_last).astype(F32)
        + ((lane == 0) & y_first).astype(F32)
        + ((lane == LANES - 1) & y_last).astype(F32)
    )
    for x in range(nx):
        faces = inner
        if x == 0:
            faces = faces + jnp.where(x_first, 1.0, 0.0)
        if x == nx - 1:
            faces = faces + jnp.where(x_last, 1.0, 0.0)
        weight = faces * conduct_ref[x]
        src_ref[x] = source_ref[x] + weight * refined[x // 2]
        rea_ref[x] = 1.0 + reaction_ref[x] + weight

    low = high = jnp.zeros((nz, LANES), F32)
    for f, (ref, depth) in enumerate(
        ((old_ref, 0), (old_ref, 1), (conduct_ref, 0), (conduct_ref, 1), (src_ref, 0), (rea_ref, 0))
    ):
        for x in range(nx):
            spot = f * nx + x
            low = jnp.where(lane == spot, roll_lanes(ref[x], spot - depth), low)
            high = jnp.where(lane == spot, roll_lanes(ref[x], spot + 1 + depth), high)
    slot, _ = moved_slot(lambda j: home_ref[j], slots)
    note = lane == 6 * nx
    low = jnp.where(note, slot.astype(F32), low)
    high = jnp.where(note, slot.astype(F32), high)
    write_pair("gy", ya_ref, yb_ref, Ellipsis, low, high)


def address_kernel(parts_ref, send_hbm, send_ref, sems, *, width):
    planes = send_ref.shape[1] - 1
    shape = parts_ref.shape[2:]
    column = lax.rem(lane_of(shape), width)
    beside = jnp.where(column < 2, -1.0, jnp.where(column >= width - 2, 1.0, -4096.0))
    count = parts_ref.shape[0]
    columns = [
        (roll_lanes(parts_ref[k, planes] + beside, 4 * i), roll_lanes(parts_ref[k, i], 4 * i))
        for k in range(count)
        for i in range(planes)
    ]
    chunks = sems.shape[0]
    size = send_ref.shape[0] // chunks
    copies = []
    for chunk in range(chunks):
        for device in range(chunk * size, (chunk + 1) * size):
            for i in range(planes):
                value = jnp.zeros(shape, F32)
                for k in range(count):
                    value = jnp.where(parts_ref[k, planes] == device, parts_ref[k, i], value)
                send_ref[device, i] = value
            value = jnp.zeros(shape, F32)
            for spot, source in columns:
                value = jnp.where(spot == device, source, value)
            send_ref[device, planes] = value
        part = pl.ds(chunk * size, size)
        copies.append(pltpu.make_async_copy(send_ref.at[part], send_hbm.at[part], sems.at[chunk]))
        copies[-1].start()
    for copy in copies:
        copy.wait()


def place_kernel(
    home_ref, recv_ref, old_ref, conduct_ref, src_ref, rea_ref, ya_ref, yb_ref,
    start_ref, yhalo_ref, own_ref, xa_ref, xb_ref,
):
    slots = home_ref.shape[0]
    width = LANES // slots
    nx, nz, _ = old_ref.shape
    rows = nz // slots
    slot, _ = moved_slot(lambda j: home_ref[j], slots)
    planes = recv_ref.shape[1] - 1
    run = nx // planes
    count = recv_ref.shape[0]
    here = lax.div(lane_of((rows, LANES)), width) == slot

    def total(first, tile):
        value = recv_ref[first, tile]
        for source in range(first + run, count, run):
            value = value + recv_ref[source, tile]
        return value

    for k in range(run):
        for i in range(planes):
            x = k * planes + i
            arrived = total(k, i)
            for g in range(slots):
                shift = lax.rem(width * (slot - g) + LANES, LANES)
                part = pl.ds(g * rows, rows)
                start_ref[x, part, :] = jnp.where(
                    here, pltpu.roll(arrived, shift, 1), old_ref[x, part, :]
                )

    beside = [total(k, planes) for k in range(run)]
    lane = lane_of((rows, LANES))
    halos = received("gy", ya_ref[...], yb_ref[...])
    for side in range(2):
        outer = width - 1 if side == 0 else 0
        inward = -1 if side == 0 else 1
        touched = float(slots - 1 if side == 0 else 0)
        note = jnp.broadcast_to(halos[side][0:1, 6 * nx : 6 * nx + 1], (rows, LANES)) == touched
        for g in range(slots):
            value = jnp.zeros((rows, LANES), F32)
            for x in range(nx):
                source = beside[x // planes]
                for depth in range(2):
                    at = g * width + outer + inward * depth + 4 * (x % planes)
                    spot = depth * nx + x
                    value = jnp.where(lane == spot, roll_lanes(source, spot - at), value)
            held = halos[side][g * rows : (g + 1) * rows]
            yhalo_ref[side, g * rows : (g + 1) * rows] = jnp.where(
                note & (lane < 2 * nx), value, held
            )

    lane = lane_of((nz, LANES))
    low = high = jnp.zeros((nz, LANES), F32)
    for x in range(nx):
        low = jnp.where(lane == x, roll_lanes(start_ref[x], x), low)
        high = jnp.where(lane == x, roll_lanes(start_ref[x], x + 1), high)
    own_ref[0] = low
    own_ref[1] = high

    for f, (ref, depth) in enumerate(
        ((start_ref, 0), (start_ref, 1), (conduct_ref, 0), (conduct_ref, 1), (src_ref, 0), (rea_ref, 0))
    ):
        write_pair(
            "gx", xa_ref, xb_ref, slice(f * nz, (f + 1) * nz), ref[depth], ref[nx - 1 - depth]
        )
    low = high = jnp.zeros((nz, LANES), F32)
    for side in range(2):
        halo = yhalo_ref[side]
        for f, offset in enumerate((PHI1 * nx, KAP1 * nx)):
            spot = 2 * side + f
            low = jnp.where(lane == spot, roll_lanes(halo, spot - offset), low)
            high = jnp.where(lane == spot, roll_lanes(halo, spot - offset - nx + 1), high)
    write_pair("gx", xa_ref, xb_ref, slice(6 * nz, 7 * nz), low, high)


def rows_kernel(
    start_ref, conduct_ref, src_ref, rea_ref, yhalo_ref, xa_ref, xb_ref,
    za_ref, zb_ref,
):
    _, nz, _ = start_ref.shape
    nx = start_ref.shape[0]
    last = nz - 1
    for f, (ref, depth) in enumerate(
        ((start_ref, 0), (start_ref, 1), (conduct_ref, 0), (conduct_ref, 1), (src_ref, 0), (rea_ref, 0))
    ):
        write_pair("gz", za_ref, zb_ref, f, ref[:, depth, :], ref[:, last - depth, :])
    for f, field in enumerate((PHI1, KAP1)):
        begin = field * nz
        halo = received("gx", xa_ref[begin : begin + nz], xb_ref[begin : begin + nz])
        for side in range(2):
            row = 2 * side + f
            write_pair(
                "gz", za_ref, zb_ref, (HALO, slice(row, row + 1)),
                halo[side][0:1], halo[side][last : last + 1],
            )
            row = 4 + 2 * side + f
            columns = roll_lanes(yhalo_ref[side], -field * nx)
            write_pair(
                "gz", za_ref, zb_ref, (HALO, slice(row, row + 1)),
                columns[0:1], columns[last : last + 1],
            )


def step(numerator, denominator, kappa, sides):
    for phi, beside, outside in sides:
        weight = 0.5 * (kappa + beside)
        if outside is not None:
            weight = jnp.where(outside, 0.0, weight)
        numerator = numerator + weight * phi
        denominator = denominator + weight
    return numerator / denominator


def along_rows(phi, kappa, low, high, flags):
    row = row_of(phi.shape)
    last = phi.shape[0] - 1
    low_edge, high_edge = row == 0, row == last
    return [
        (
            jnp.where(low_edge, low[0], roll_rows(phi, 1)),
            jnp.where(low_edge, low[1], roll_rows(kappa, 1)),
            low_edge & flags[0],
        ),
        (
            jnp.where(high_edge, high[0], roll_rows(phi, last)),
            jnp.where(high_edge, high[1], roll_rows(kappa, last)),
            high_edge & flags[1],
        ),
    ]


def along_lanes(phi, kappa, low, high, flags, last=LANES - 1):
    lane = lane_of(phi.shape)
    low_edge, high_edge = lane == 0, lane == last
    return [
        (
            jnp.where(low_edge, low[0], roll_lanes(phi, 1)),
            jnp.where(low_edge, low[1], roll_lanes(kappa, 1)),
            low_edge & flags[0],
        ),
        (
            jnp.where(high_edge, high[0], roll_lanes(phi, -1)),
            jnp.where(high_edge, high[1], roll_lanes(kappa, -1)),
            high_edge & flags[1],
        ),
    ]


def to_column(row, count):
    shape = (count, LANES)
    picked = jnp.where(lane_of(shape) == row_of(shape), jnp.broadcast_to(row, shape), 0.0)
    return jnp.broadcast_to(jnp.sum(picked, axis=1, keepdims=True), shape)


def sweeps_kernel(
    start_ref, conduct_ref, src_ref, rea_ref, yhalo_ref, own_ref,
    sya_ref, syb_ref, xa_ref, xb_ref, za_ref, zb_ref,
    out_hbm, out_ref, sems,
):
    nx, nz, _ = start_ref.shape
    flags_x, flags_z, flags_y = edges()
    start = [start_ref[x] for x in range(nx)]
    conduct = [conduct_ref[x] for x in range(nx)]

    def part(begin, size):
        return received("gx", xa_ref[begin : begin + size], xb_ref[begin : begin + size])

    xf = [part(f * nz, nz) for f in range(6)]
    xcols = part(6 * nz, nz)
    zf = [received("gz", za_ref[i], zb_ref[i]) for i in range(7)]
    around = zf[HALO]
    yf = [yhalo_ref[side] for side in range(2)]
    sf = sent("gy", sya_ref[...], syb_ref[...])

    def columns(tile, phi_spot, kappa_spot, lane):
        return roll_lanes(tile, lane - phi_spot), roll_lanes(tile, lane - kappa_spot)

    def two_rows(tile, at):
        return tile[at : at + 1], tile[at + 1 : at + 2]

    x_first_sweep = []
    for side in range(2):
        phi, kappa = xf[PHI1][side], xf[KAP1][side]
        me = 0 if side == 0 else nx - 1
        at = 2 * side
        sides = [(xf[PHI2][side], xf[KAP2][side], None), (start[me], conduct[me], None)]
        sides += along_rows(phi, kappa, two_rows(around[0], at), two_rows(around[1], at), flags_z)
        tile = xcols[side]
        sides += along_lanes(
            phi, kappa, columns(tile, 0, 1, 0), columns(tile, 2, 3, LANES - 1), flags_y
        )
        x_first_sweep.append(step(phi + xf[SRC][side], xf[REA][side], kappa, sides))

    z_first_sweep = []
    for side in range(2):
        phi, kappa = zf[PHI1][side], zf[KAP1][side]
        me = 0 if side == 0 else nz - 1
        tile = around[side]
        sides = [
            (zf[PHI2][side], zf[KAP2][side], None),
            (start_ref[:, me, :], conduct_ref[:, me, :], None),
        ]
        sides += along_rows(phi, kappa, two_rows(tile, 0), two_rows(tile, 2), flags_x)
        sides += along_lanes(
            phi,
            kappa,
            tuple(to_column(row, nx) for row in two_rows(tile, 4)),
            tuple(to_column(row, nx) for row in two_rows(tile, 6)),
            flags_y,
        )
        z_first_sweep.append(step(phi + zf[SRC][side], zf[REA][side], kappa, sides))

    y_first_sweep = []
    for side in range(2):
        phi, phi2, kappa, kappa2, src, rea = [roll_lanes(yf[side], -f * nx) for f in range(6)]
        at = 2 * side
        sides = [(phi2, kappa2, None), (own_ref[side], roll_lanes(sf[side], -KAP1 * nx), None)]
        sides += along_rows(
            phi,
            kappa,
            two_rows(around[0], 4 + at),
            two_rows(around[1], 4 + at),
            flags_z,
        )
        sides += along_lanes(
            phi,
            kappa,
            columns(xcols[0], at, at + 1, 0),
            columns(xcols[1], at, at + 1, nx - 1),
            flags_x,
            nx - 1,
        )
        y_first_sweep.append(step(phi + src, rea, kappa, sides))

    copies = []

    def sweep(phis, x_phi, z_phi, y_phi, store=False):
        results = []
        for x in range(nx):
            phi, kappa = phis[x], conduct[x]
            sides = []
            if x:
                sides.append((phis[x - 1], conduct[x - 1], None))
            else:
                sides.append((x_phi[0], xf[KAP1][0], flags_x[0]))
            if x < nx - 1:
                sides.append((phis[x + 1], conduct[x + 1], None))
            else:
                sides.append((x_phi[1], xf[KAP1][1], flags_x[1]))
            sides += along_rows(
                phi,
                kappa,
                (z_phi[0][x : x + 1], zf[KAP1][0][x : x + 1]),
                (z_phi[1][x : x + 1], zf[KAP1][1][x : x + 1]),
                flags_z,
            )
            spot = KAP1 * nx + x
            sides += along_lanes(
                phi,
                kappa,
                (roll_lanes(y_phi[0], -x), roll_lanes(yf[0], -spot)),
                (roll_lanes(y_phi[1], LANES - 1 - x), roll_lanes(yf[1], LANES - 1 - spot)),
                flags_y,
            )
            results.append(step(start[x] + src_ref[x], rea_ref[x], kappa, sides))
            if store:
                out_ref[x] = results[x]
                copies.append(pltpu.make_async_copy(out_ref.at[x], out_hbm.at[x], sems.at[x]))
                copies[x].start()
        return results

    first = sweep(start, xf[PHI1], zf[PHI1], yf)
    sweep(first, x_first_sweep, z_first_sweep, y_first_sweep, store=True)
    for copy in copies:
        copy.wait()


def swap(axis, first, second):
    count = lax.axis_size(axis)
    results = []
    for j, value in ((1, second), (0, first)):
        pairs = []
        for low in range(j, count - 1, 2):
            pairs += [(low, low + 1), (low + 1, low)]
        results.append(lax.ppermute(value, axis, pairs))
    return results[::-1]


def call(kernel, operands, outs, smem=0, hbm=(), out_space=VMEM, scratch=()):
    specs = [SMEM] * smem + [VMEM] * (len(operands) - smem)
    operands = list(operands)
    for i in hbm:
        specs[i] = HBM
        operands[i] = pltpu.with_memory_space_constraint(operands[i], pltpu.HBM)
    return pl.pallas_call(
        kernel,
        out_shape=[jax.ShapeDtypeStruct(shape, F32) for shape in outs],
        in_specs=specs,
        out_specs=[out_space] * len(outs),
        scratch_shapes=scratch,
        compiler_params=PARAMS,
    )(*operands)


def on_device(old_field, new_home, conduct, reaction, source, coarse):
    nx, nz, ny = block = old_field.shape
    home = new_home[0, 0]
    slots = home.shape[0]
    rows, width = nz // slots, ny // slots
    line = lax.axis_size("gy")
    part = nx // RUN

    (parts,) = call(
        split_kernel,
        (new_home, old_field),
        [(RUN, part + 1, rows, ny)],
        hbm=(0, 1),
        scratch=[
            pltpu.SMEM(new_home.shape, jnp.int32),
            pltpu.VMEM(block, F32),
            pltpu.SemaphoreType.DMA,
            pltpu.SemaphoreType.DMA((nx,)),
        ],
    )
    groups = [[i * RUN + k for k in range(RUN)] for i in range(line // RUN)]
    parts = lax.all_to_all(parts, "gy", 0, 0, tiled=True, axis_index_groups=groups)

    def address(*refs):
        address_kernel(*refs, width=width)

    slot_shape = (line, part + 1, rows, ny)
    (send,) = call(
        address,
        (parts,),
        [slot_shape],
        out_space=HBM,
        scratch=[pltpu.VMEM(slot_shape, F32), pltpu.SemaphoreType.DMA((4,))],
    )
    recv = lax.all_to_all(send, "gy", 0, 0, tiled=True)
    src, rea, sya, syb = call(
        fold_kernel,
        (home, old_field, conduct, source, reaction, coarse, parts),
        [block, block, (nz, ny), (nz, ny)],
        smem=1,
    )
    ya, yb = swap("gy", sya, syb)
    start, yhalo, own, xa, xb = call(
        place_kernel,
        (home, recv, old_field, conduct, src, rea, ya, yb),
        [block, (2, nz, ny), (2, nz, ny), (7 * nz, ny), (7 * nz, ny)],
        smem=1,
    )
    xa, xb = swap("gx", xa, xb)
    za, zb = call(
        rows_kernel,
        (start, conduct, src, rea, yhalo, xa, xb),
        [(7, nx, ny), (7, nx, ny)],
    )
    za, zb = swap("gz", za, zb)
    (relaxed,) = call(
        sweeps_kernel,
        (start, conduct, src, rea, yhalo, own, sya, syb, xa, xb, za, zb),
        [block],
        out_space=HBM,
        scratch=[pltpu.VMEM(block, F32), pltpu.SemaphoreType.DMA((nx,))],
    )
    return relaxed


def solution(mesh):
    return jax.shard_map(
        on_device,
        mesh=mesh,
        in_specs=(P("gx", "gz", "gy"),) * 6,
        out_specs=P("gx", "gz", "gy"),
        check_vma=False,
    )
```

```python
import jax
import jax.numpy as jnp
from jax import lax
from jax.experimental import pallas as pl
from jax.experimental.pallas import tpu as pltpu
from jax.sharding import PartitionSpec as P

LANES = 128
RUN = 8
VMEM = pl.BlockSpec(memory_space=pltpu.VMEM)
SMEM = pl.BlockSpec(memory_space=pltpu.SMEM)
HBM = pl.BlockSpec(memory_space=pltpu.HBM)
PARAMS = pltpu.CompilerParams(vmem_limit_bytes=24 * 1024 * 1024)
F32 = jnp.float32

PHI1, PHI2, KAP1, KAP2, SRC, REA, RIM = range(7)


def lane_of(shape):
    return lax.broadcasted_iota(jnp.int32, shape, len(shape) - 1)


def row_of(shape):
    return lax.broadcasted_iota(jnp.int32, shape, len(shape) - 2)


def roll_lanes(value, shift):
    shift = shift % LANES
    return pltpu.roll(value, shift, value.ndim - 1) if shift else value


def roll_rows(value, shift):
    return pltpu.roll(value, shift % value.shape[0], 0)


def moved_slot(home_of, slots):
    position = lax.axis_index("gy")
    slot = jnp.int32(0)
    target = jnp.int32(0)
    for j in range(slots):
        home = home_of(j)
        leaves = home != position * slots + j
        slot = jnp.where(leaves, j, slot)
        target = jnp.where(leaves, home, target)
    return slot, target


def edges():
    flags = []
    for axis in ("gx", "gz", "gy"):
        index = lax.axis_index(axis)
        flags.append((index == 0, index == lax.axis_size(axis) - 1))
    return flags


def is_even(axis):
    return lax.rem(lax.axis_index(axis), 2) == 0


def write_pair(axis, first_ref, second_ref, index, low, high):
    even = is_even(axis)
    first_ref[index] = jnp.where(even, high, low)
    second_ref[index] = jnp.where(even, low, high)


def received(axis, first, second):
    even = is_even(axis)
    return jnp.where(even, second, first), jnp.where(even, first, second)


def sent(axis, first, second):
    even = is_even(axis)
    return jnp.where(even, second, first), jnp.where(even, first, second)


def doubler(count):
    half = lax.div(lax.broadcasted_iota(jnp.int32, (count, 2 * count), 1), 2)
    return (half == lax.broadcasted_iota(jnp.int32, (count, 2 * count), 0)).astype(F32)


def exact_dot(left, right):
    return jnp.dot(left, right, precision=lax.Precision.HIGHEST, preferred_element_type=F32)


def refine(coarse_ref):
    cx, cz, cy = coarse_ref.shape
    left, right = doubler(cz).T, doubler(cy)
    return [exact_dot(left, exact_dot(coarse_ref[x], right)) for x in range(cx)]


def first_kernel(
    home_hbm, old_hbm, conduct_hbm, source_hbm, reaction_hbm, coarse_hbm,
    za_ref, zb_ref, parts_ref, home_ref, old_ref, rows_ref, coarse_ref,
    home_sem, old_sems, sems, coarse_sem,
):
    slots = home_ref.shape[2]
    width = LANES // slots
    nx, nz, _ = old_hbm.shape
    size = rows_ref.shape[3]
    copies = [pltpu.make_async_copy(coarse_hbm, coarse_ref, coarse_sem)]
    loads = [pltpu.make_async_copy(old_hbm.at[x], old_ref.at[x], old_sems.at[x]) for x in range(nx)]
    for i, ref in enumerate((conduct_hbm, source_hbm, reaction_hbm)):
        for side, begin in enumerate((0, nz - size)):
            copies.append(
                pltpu.make_async_copy(
                    ref.at[:, pl.ds(begin, size), :], rows_ref.at[i, side], sems.at[i, side]
                )
            )
    load_home = pltpu.make_async_copy(home_hbm, home_ref, home_sem)
    for copy in [load_home] + loads + copies:
        copy.start()
    load_home.wait()

    slot, target = moved_slot(lambda j: home_ref[0, 0, j], slots)
    device = lax.div(target, slots)
    back = LANES - width * slot
    (x_first, x_last), (z_first, z_last), (y_first, y_last) = edges()
    row, lane = row_of((nx, LANES)), lane_of((nx, LANES))
    note = jnp.where(lane < 3 * width, device, slot).astype(F32)
    inner = (
        ((row == 0) & x_first).astype(F32)
        + ((row == nx - 1) & x_last).astype(F32)
        + ((lane == 0) & y_first).astype(F32)
        + ((lane == LANES - 1) & y_last).astype(F32)
    )
    rows = nz // slots
    count, planes = parts_ref.shape[0], parts_ref.shape[1] - 1
    group = lax.div(lane_of((rows, LANES)), width)
    for x in range(nx):
        loads[x].wait()
        box = jnp.zeros((rows, LANES), F32)
        for g in range(slots):
            shift = lax.rem(width * (g - slot) + LANES, LANES)
            rolled = pltpu.roll(old_ref[x, g * rows : (g + 1) * rows, :], shift, 1)
            box = jnp.where(group == g, rolled, box)
        parts_ref[x // planes, x % planes] = box
    for k in range(count):
        parts_ref[k, planes] = jnp.full((rows, LANES), device, jnp.int32).astype(F32)
    for copy in copies:
        copy.wait()
    cx, cz, cy = coarse_ref.shape
    ends = jnp.concatenate([coarse_ref[:, 0, :], coarse_ref[:, cz - 1, :]], axis=0)
    wide = exact_dot(ends, doubler(cy))

    def rims(first, second):
        near = pltpu.roll(first, lax.rem(back, LANES), 1)
        far = pltpu.roll(second, lax.rem(back + width, LANES), 1)
        return jnp.where(lane < width, near, jnp.where(lane < 2 * width, far, note))

    faces = []
    for side, first, second, edge in ((0, 0, 1, z_first), (1, size - 1, size - 2, z_last)):
        refined = jnp.zeros((nx, LANES), F32)
        for x in range(cx):
            refined = jnp.where(lax.div(row, 2) == x, wide[side * cx + x : side * cx + x + 1], refined)
        top = side * (nz - size)
        old, old2 = old_ref[:, top + first, :], old_ref[:, top + second, :]
        kappa, kappa2 = rows_ref[0, side, :, first, :], rows_ref[0, side, :, second, :]
        weight = (inner + jnp.where(edge, 1.0, 0.0)) * kappa
        src = rows_ref[1, side, :, first, :] + weight * refined
        rea = 1.0 + rows_ref[2, side, :, first, :] + weight
        faces.append([old, old2, kappa, kappa2, src, rea, rims(old, old2)])
    for i in range(7):
        write_pair("gz", za_ref, zb_ref, i, faces[0][i], faces[1][i])


def fold_kernel(
    home_ref, old_ref, conduct_ref, source_ref, reaction_ref, coarse_ref, za_ref, zb_ref,
    src_ref, rea_ref, ya_ref, yb_ref,
):
    slots = home_ref.shape[0]
    width = LANES // slots
    nx, nz, _ = conduct_ref.shape
    (x_first, x_last), (z_first, z_last), (y_first, y_last) = edges()
    refined = refine(coarse_ref)
    row, lane = row_of((nz, LANES)), lane_of((nz, LANES))
    inner = (
        ((row == 0) & z_first).astype(F32)
        + ((row == nz - 1) & z_last).astype(F32)
        + ((lane == 0) & y_first).astype(F32)
        + ((lane == LANES - 1) & y_last).astype(F32)
    )
    for x in range(nx):
        faces = inner
        if x == 0:
            faces = faces + jnp.where(x_first, 1.0, 0.0)
        if x == nx - 1:
            faces = faces + jnp.where(x_last, 1.0, 0.0)
        weight = faces * conduct_ref[x]
        src_ref[x] = source_ref[x] + weight * refined[x // 2]
        rea_ref[x] = 1.0 + reaction_ref[x] + weight

    low = high = jnp.zeros((nz, LANES), F32)
    for f, (ref, depth) in enumerate(
        ((old_ref, 0), (old_ref, 1), (conduct_ref, 0), (conduct_ref, 1), (src_ref, 0), (rea_ref, 0))
    ):
        for x in range(nx):
            spot = f * nx + x
            low = jnp.where(lane == spot, roll_lanes(ref[x], spot - depth), low)
            high = jnp.where(lane == spot, roll_lanes(ref[x], spot + 1 + depth), high)
    write_pair("gy", ya_ref, yb_ref, slice(0, nz), low, high)

    lane = lane_of((nx, LANES))
    slot, _ = moved_slot(lambda j: home_ref[j], slots)
    low = high = jnp.where(lane == 4, slot, 0).astype(F32)
    notes = received("gz", za_ref[RIM], zb_ref[RIM])
    for side in range(2):
        note = jnp.broadcast_to(notes[side][:, 3 * width : 3 * width + 1], (nx, LANES))
        low = jnp.where(lane == 5 + side, note, low)
        high = jnp.where(lane == 5 + side, note, high)
        for f, tile in enumerate((PHI1, KAP1)):
            value = received("gz", za_ref[tile], zb_ref[tile])[side]
            spot = 2 * side + f
            low = jnp.where(lane == spot, roll_lanes(value, spot), low)
            high = jnp.where(lane == spot, roll_lanes(value, spot + 1), high)
    write_pair("gy", ya_ref, yb_ref, slice(nz, nz + nx), low, high)


def address_kernel(parts_ref, za_ref, zb_ref, send_ref, *, width):
    planes = send_ref.shape[1] - 2
    low, high = received("gz", za_ref[RIM], zb_ref[RIM])
    shape = low.shape
    lane = lane_of(shape)
    low_tag = jnp.broadcast_to(low[:, 2 * width : 2 * width + 1], shape)
    high_tag = jnp.broadcast_to(high[:, 2 * width : 2 * width + 1], shape)
    high = roll_lanes(high, 2 * width)
    lower = lane < 2 * width
    rims = jnp.where(lower, low, high)
    tag = jnp.where(lower, low_tag, high_tag)
    column = lax.rem(lane, width)
    beside = jnp.where(column < 2, -1.0, jnp.where(column >= width - 2, 1.0, -4096.0))
    edge = jnp.where(column == 0, -1.0, jnp.where(column == width - 1, 1.0, -4096.0))
    count = parts_ref.shape[0]
    columns = [
        (roll_lanes(parts_ref[k, planes] + beside, 4 * i), roll_lanes(parts_ref[k, i], 4 * i))
        for k in range(count)
        for i in range(planes)
    ]
    columns.append((roll_lanes(tag + edge, 4 * planes), roll_lanes(rims, 4 * planes)))
    for device in range(send_ref.shape[0]):
        for i in range(planes):
            value = jnp.zeros(shape, F32)
            for k in range(count):
                value = jnp.where(parts_ref[k, planes] == device, parts_ref[k, i], value)
            send_ref[device, i] = value
        send_ref[device, planes] = jnp.where(tag == device, rims, 0.0)
        value = jnp.zeros(shape, F32)
        for spot, source in columns:
            value = jnp.where(spot == device, source, value)
        send_ref[device, planes + 1] = value


def spread(tile, offset, width):
    piece = jnp.where(lane_of(tile.shape) < width, roll_lanes(tile, -offset), 0.0)
    result = piece
    for shift in range(width, LANES, width):
        result = result + roll_lanes(piece, shift)
    return result


def place_kernel(
    home_ref, recv_ref, old_ref, za_ref, zb_ref, ya_ref, yb_ref,
    start_ref, zhalo_ref, yhalo_ref, own_ref,
):
    slots = home_ref.shape[0]
    width = LANES // slots
    nx, nz, _ = old_ref.shape
    rows = nz // slots
    slot, _ = moved_slot(lambda j: home_ref[j], slots)
    planes = recv_ref.shape[1] - 2
    run = nx // planes
    count = recv_ref.shape[0]
    here = lax.div(lane_of((rows, LANES)), width) == slot

    def total(first, stride, tile):
        value = recv_ref[first, tile]
        for source in range(first + stride, count, stride):
            value = value + recv_ref[source, tile]
        return value

    for k in range(run):
        for i in range(planes):
            x = k * planes + i
            arrived = total(k, run, i)
            for g in range(slots):
                shift = lax.rem(width * (slot - g) + LANES, LANES)
                part = pl.ds(g * rows, rows)
                start_ref[x, part, :] = jnp.where(
                    here, pltpu.roll(arrived, shift, 1), old_ref[x, part, :]
                )

    rims = total(0, 1, planes)
    faces = [received("gz", za_ref[i], zb_ref[i]) for i in range(7)]
    group = lax.div(lane_of((nx, LANES)), width).astype(F32)
    for side in range(2):
        note = faces[RIM][side]
        there = jnp.broadcast_to(note[:, 3 * width : 3 * width + 1], note.shape) == group
        for depth in range(2):
            moved = spread(rims, (2 * side + depth) * width, width)
            zhalo_ref[side, depth] = jnp.where(there, moved, faces[depth][side])

    beside = [total(k, run, planes + 1) for k in range(run)]
    every = beside[0]
    for k in range(1, run):
        every = every + beside[k]
    lane = lane_of((rows, LANES))
    corner_lane = lane_of((nx, LANES))
    halos = received("gy", ya_ref[:nz], yb_ref[:nz])
    corners = received("gy", ya_ref[nz : nz + nx], yb_ref[nz : nz + nx])
    for side in range(2):
        outer = width - 1 if side == 0 else 0
        inward = -1 if side == 0 else 1
        touched = float(slots - 1 if side == 0 else 0)
        note = jnp.broadcast_to(corners[side][0:1, 4:5], (rows, LANES)) == touched
        for g in range(slots):
            value = jnp.zeros((rows, LANES), F32)
            for x in range(nx):
                source = beside[x // planes]
                for depth in range(2):
                    at = g * width + outer + inward * depth + 4 * (x % planes)
                    spot = depth * nx + x
                    value = jnp.where(lane == spot, roll_lanes(source, spot - at), value)
            held = halos[side][g * rows : (g + 1) * rows]
            yhalo_ref[side, g * rows : (g + 1) * rows] = jnp.where(
                note & (lane < 2 * nx), value, held
            )
        corner = corners[side]
        for z_side in range(2):
            note = jnp.broadcast_to(corner[:, 5 + z_side : 6 + z_side], (nx, LANES)) == touched
            at = 2 * width * z_side + outer + 4 * planes
            spot = 2 * z_side
            corner = jnp.where(
                note & (corner_lane == spot), roll_lanes(every, spot - at), corner
            )
        yhalo_ref[side, nz : nz + nx] = corner

    lane = lane_of((nz, LANES))
    low = high = jnp.zeros((nz, LANES), F32)
    for x in range(nx):
        low = jnp.where(lane == x, roll_lanes(start_ref[x], x), low)
        high = jnp.where(lane == x, roll_lanes(start_ref[x], x + 1), high)
    own_ref[0] = low
    own_ref[1] = high


def edge_kernel(
    start_ref, conduct_ref, src_ref, rea_ref, zhalo_ref, yhalo_ref, za_ref, zb_ref,
    xa_ref, xb_ref,
):
    nx, nz, _ = start_ref.shape
    for f, (ref, depth) in enumerate(
        ((start_ref, 0), (start_ref, 1), (conduct_ref, 0), (conduct_ref, 1), (src_ref, 0), (rea_ref, 0))
    ):
        write_pair(
            "gx", xa_ref, xb_ref, slice(f * nz, (f + 1) * nz), ref[depth], ref[nx - 1 - depth]
        )
    base = 6 * nz
    kappas = received("gz", za_ref[KAP1], zb_ref[KAP1])
    xa_ref[base : base + 8] = jnp.zeros((8, LANES), F32)
    xb_ref[base : base + 8] = jnp.zeros((8, LANES), F32)
    for side in range(2):
        for f, tile in enumerate((zhalo_ref[side, 0], kappas[side])):
            spot = base + 2 * side + f
            write_pair(
                "gx", xa_ref, xb_ref, slice(spot, spot + 1), tile[0:1], tile[nx - 1 : nx]
            )
    lane = lane_of((nz, LANES))
    low = high = jnp.zeros((nz, LANES), F32)
    for side in range(2):
        halo = yhalo_ref[side, :nz]
        for f, offset in enumerate((PHI1 * nx, KAP1 * nx)):
            spot = 2 * side + f
            low = jnp.where(lane == spot, roll_lanes(halo, spot - offset), low)
            high = jnp.where(lane == spot, roll_lanes(halo, spot - offset - nx + 1), high)
    write_pair("gx", xa_ref, xb_ref, slice(base + 8, base + 8 + nz), low, high)


def step(numerator, denominator, kappa, sides):
    for phi, beside, outside in sides:
        weight = 0.5 * (kappa + beside)
        if outside is not None:
            weight = jnp.where(outside, 0.0, weight)
        numerator = numerator + weight * phi
        denominator = denominator + weight
    return numerator / denominator


def along_rows(phi, kappa, low, high, flags):
    row = row_of(phi.shape)
    last = phi.shape[0] - 1
    low_edge, high_edge = row == 0, row == last
    return [
        (
            jnp.where(low_edge, low[0], roll_rows(phi, 1)),
            jnp.where(low_edge, low[1], roll_rows(kappa, 1)),
            low_edge & flags[0],
        ),
        (
            jnp.where(high_edge, high[0], roll_rows(phi, last)),
            jnp.where(high_edge, high[1], roll_rows(kappa, last)),
            high_edge & flags[1],
        ),
    ]


def along_lanes(phi, kappa, low, high, flags, last=LANES - 1):
    lane = lane_of(phi.shape)
    low_edge, high_edge = lane == 0, lane == last
    return [
        (
            jnp.where(low_edge, low[0], roll_lanes(phi, 1)),
            jnp.where(low_edge, low[1], roll_lanes(kappa, 1)),
            low_edge & flags[0],
        ),
        (
            jnp.where(high_edge, high[0], roll_lanes(phi, -1)),
            jnp.where(high_edge, high[1], roll_lanes(kappa, -1)),
            high_edge & flags[1],
        ),
    ]


def to_row(tile, spot):
    column = jnp.broadcast_to(tile[:, spot : spot + 1], tile.shape)
    return jnp.sum(
        jnp.where(lane_of(tile.shape) == row_of(tile.shape), column, 0.0), axis=0, keepdims=True
    )


def sweeps_kernel(
    start_ref, conduct_ref, src_ref, rea_ref, zhalo_ref, yhalo_ref, own_ref,
    za_ref, zb_ref, sya_ref, syb_ref, xa_ref, xb_ref,
    out_ref,
):
    nx, nz, _ = start_ref.shape
    flags_x, flags_z, flags_y = edges()
    start = [start_ref[x] for x in range(nx)]
    conduct = [conduct_ref[x] for x in range(nx)]
    base = 6 * nz

    def part(axis, a_ref, b_ref, begin, size):
        return received(axis, a_ref[begin : begin + size], b_ref[begin : begin + size])

    xf = [part("gx", xa_ref, xb_ref, f * nz, nz) for f in range(6)]
    xrows = part("gx", xa_ref, xb_ref, base, 8)
    xcols = part("gx", xa_ref, xb_ref, base + 8, nz)
    zf = [received("gz", za_ref[i], zb_ref[i]) for i in range(6)]
    yf = [yhalo_ref[side, :nz] for side in range(2)]
    yt = [yhalo_ref[side, nz : nz + nx] for side in range(2)]
    sf = sent("gy", sya_ref[:nz], syb_ref[:nz])

    def columns(tile, phi_spot, kappa_spot, lane):
        return roll_lanes(tile, lane - phi_spot), roll_lanes(tile, lane - kappa_spot)

    x_first_sweep = []
    for side in range(2):
        phi, kappa = xf[PHI1][side], xf[KAP1][side]
        me = 0 if side == 0 else nx - 1
        rows = xrows[side]
        sides = [(xf[PHI2][side], xf[KAP2][side], None), (start[me], conduct[me], None)]
        sides += along_rows(phi, kappa, (rows[0:1], rows[1:2]), (rows[2:3], rows[3:4]), flags_z)
        tile = xcols[side]
        sides += along_lanes(
            phi, kappa, columns(tile, 0, 1, 0), columns(tile, 2, 3, LANES - 1), flags_y
        )
        x_first_sweep.append(step(phi + xf[SRC][side], xf[REA][side], kappa, sides))

    z_first_sweep = []
    for side in range(2):
        phi, kappa = zhalo_ref[side, 0], zf[KAP1][side]
        me = 0 if side == 0 else nz - 1
        at = 2 * side
        sides = [
            (zhalo_ref[side, 1], zf[KAP2][side], None),
            (start_ref[:, me, :], conduct_ref[:, me, :], None),
        ]
        sides += along_rows(
            phi,
            kappa,
            (xrows[0][at : at + 1], xrows[0][at + 1 : at + 2]),
            (xrows[1][at : at + 1], xrows[1][at + 1 : at + 2]),
            flags_x,
        )
        sides += along_lanes(
            phi,
            kappa,
            columns(yt[0], at, at + 1, 0),
            columns(yt[1], at, at + 1, LANES - 1),
            flags_y,
        )
        z_first_sweep.append(step(phi + zf[SRC][side], zf[REA][side], kappa, sides))

    y_first_sweep = []
    for side in range(2):
        phi, phi2, kappa, kappa2, src, rea = [roll_lanes(yf[side], -f * nx) for f in range(6)]
        at = 2 * side
        sides = [(phi2, kappa2, None), (own_ref[side], roll_lanes(sf[side], -KAP1 * nx), None)]
        sides += along_rows(
            phi,
            kappa,
            (to_row(yt[side], 0), to_row(yt[side], 1)),
            (to_row(yt[side], 2), to_row(yt[side], 3)),
            flags_z,
        )
        sides += along_lanes(
            phi,
            kappa,
            columns(xcols[0], at, at + 1, 0),
            columns(xcols[1], at, at + 1, nx - 1),
            flags_x,
            nx - 1,
        )
        y_first_sweep.append(step(phi + src, rea, kappa, sides))

    def sweep(phis, x_phi, z_phi, y_phi):
        results = []
        for x in range(nx):
            phi, kappa = phis[x], conduct[x]
            sides = []
            if x:
                sides.append((phis[x - 1], conduct[x - 1], None))
            else:
                sides.append((x_phi[0], xf[KAP1][0], flags_x[0]))
            if x < nx - 1:
                sides.append((phis[x + 1], conduct[x + 1], None))
            else:
                sides.append((x_phi[1], xf[KAP1][1], flags_x[1]))
            sides += along_rows(
                phi,
                kappa,
                (z_phi[0][x : x + 1], zf[KAP1][0][x : x + 1]),
                (z_phi[1][x : x + 1], zf[KAP1][1][x : x + 1]),
                flags_z,
            )
            spot = KAP1 * nx + x
            sides += along_lanes(
                phi,
                kappa,
                (roll_lanes(y_phi[0], -x), roll_lanes(yf[0], -spot)),
                (roll_lanes(y_phi[1], LANES - 1 - x), roll_lanes(yf[1], LANES - 1 - spot)),
                flags_y,
            )
            results.append(step(start[x] + src_ref[x], rea_ref[x], kappa, sides))
        return results

    first = sweep(start, xf[PHI1], (zhalo_ref[0, 0], zhalo_ref[1, 0]), yf)
    second = sweep(first, x_first_sweep, z_first_sweep, y_first_sweep)
    for x in range(nx):
        out_ref[x] = second[x]


def swap(axis, first, second):
    count = lax.axis_size(axis)
    results = []
    for j, value in ((1, second), (0, first)):
        pairs = []
        for low in range(j, count - 1, 2):
            pairs += [(low, low + 1), (low + 1, low)]
        results.append(lax.ppermute(value, axis, pairs))
    return results[::-1]


def call(kernel, operands, outs, smem=0, hbm=(), scratch=()):
    specs = [SMEM] * smem + [VMEM] * (len(operands) - smem)
    operands = list(operands)
    for i in hbm:
        specs[i] = HBM
        operands[i] = pltpu.with_memory_space_constraint(operands[i], pltpu.HBM)
    return pl.pallas_call(
        kernel,
        out_shape=[jax.ShapeDtypeStruct(shape, F32) for shape in outs],
        in_specs=specs,
        out_specs=[VMEM] * len(outs),
        scratch_shapes=scratch,
        compiler_params=PARAMS,
    )(*operands)


def on_device(old_field, new_home, conduct, reaction, source, coarse):
    nx, nz, ny = block = old_field.shape
    home = new_home[0, 0]
    slots = home.shape[0]
    rows, width = nz // slots, ny // slots
    line = lax.axis_size("gy")
    part = nx // RUN

    sza, szb, parts = call(
        first_kernel,
        (new_home, old_field, conduct, source, reaction, coarse),
        [(7, nx, ny), (7, nx, ny), (RUN, part + 1, rows, ny)],
        hbm=(0, 1, 2, 3, 4, 5),
        scratch=[
            pltpu.SMEM(new_home.shape, jnp.int32),
            pltpu.VMEM(block, F32),
            pltpu.VMEM((3, 2, nx, 8, ny), F32),
            pltpu.VMEM(coarse.shape, F32),
            pltpu.SemaphoreType.DMA,
            pltpu.SemaphoreType.DMA((nx,)),
            pltpu.SemaphoreType.DMA((3, 2)),
            pltpu.SemaphoreType.DMA,
        ],
    )
    za, zb = swap("gz", sza, szb)
    groups = [[i * RUN + k for k in range(RUN)] for i in range(line // RUN)]
    parts = lax.all_to_all(parts, "gy", 0, 0, tiled=True, axis_index_groups=groups)

    def address(*refs):
        address_kernel(*refs, width=width)

    (send,) = call(address, (parts, za, zb), [(line, part + 2, rows, ny)])
    recv = lax.all_to_all(send, "gy", 0, 0, tiled=True)
    src, rea, sya, syb = call(
        fold_kernel,
        (home, old_field, conduct, source, reaction, coarse, za, zb),
        [block, block, (nz + nx, ny), (nz + nx, ny)],
        smem=1,
    )
    ya, yb = swap("gy", sya, syb)
    start, zhalo, yhalo, own = call(
        place_kernel,
        (home, recv, old_field, za, zb, ya, yb),
        [block, (2, 2, nx, ny), (2, nz + nx, ny), (2, nz, ny)],
        smem=1,
    )
    xa, xb = call(
        edge_kernel,
        (start, conduct, src, rea, zhalo, yhalo, za, zb),
        [(7 * nz + 8, ny)] * 2,
    )
    xa, xb = swap("gx", xa, xb)
    (relaxed,) = call(
        sweeps_kernel,
        (start, conduct, src, rea, zhalo, yhalo, own, za, zb, sya, syb, xa, xb),
        [block],
    )
    return relaxed


def solution(mesh):
    return jax.shard_map(
        on_device,
        mesh=mesh,
        in_specs=(P("gx", "gz", "gy"),) * 6,
        out_specs=P("gx", "gz", "gy"),
        check_vma=False,
    )
```

```python
import jax
import jax.numpy as jnp
from jax import lax
from jax.experimental import pallas as pl
from jax.experimental.pallas import tpu as pltpu
from jax.sharding import PartitionSpec as P

LANES = 128
RUN = 8
VMEM = pl.BlockSpec(memory_space=pltpu.VMEM)
SMEM = pl.BlockSpec(memory_space=pltpu.SMEM)
HBM = pl.BlockSpec(memory_space=pltpu.HBM)
PARAMS = pltpu.CompilerParams(vmem_limit_bytes=24 * 1024 * 1024)
F32 = jnp.float32

PHI1, PHI2, KAP1, KAP2, SRC, REA, RIM = range(7)


def lane_of(shape):
    return lax.broadcasted_iota(jnp.int32, shape, len(shape) - 1)


def row_of(shape):
    return lax.broadcasted_iota(jnp.int32, shape, len(shape) - 2)


def roll_lanes(value, shift):
    shift = shift % LANES
    return pltpu.roll(value, shift, value.ndim - 1) if shift else value


def roll_rows(value, shift):
    return pltpu.roll(value, shift % value.shape[0], 0)


def moved_slot(home_of, slots):
    position = lax.axis_index("gy")
    slot = jnp.int32(0)
    target = jnp.int32(0)
    for j in range(slots):
        home = home_of(j)
        leaves = home != position * slots + j
        slot = jnp.where(leaves, j, slot)
        target = jnp.where(leaves, home, target)
    return slot, target


def edges():
    flags = []
    for axis in ("gx", "gz", "gy"):
        index = lax.axis_index(axis)
        flags.append((index == 0, index == lax.axis_size(axis) - 1))
    return flags


def is_even(axis):
    return lax.rem(lax.axis_index(axis), 2) == 0


def write_pair(axis, first_ref, second_ref, index, low, high):
    even = is_even(axis)
    first_ref[index] = jnp.where(even, high, low)
    second_ref[index] = jnp.where(even, low, high)


def received(axis, first, second):
    even = is_even(axis)
    return jnp.where(even, second, first), jnp.where(even, first, second)


def sent(axis, first, second):
    even = is_even(axis)
    return jnp.where(even, second, first), jnp.where(even, first, second)


def doubler(count):
    half = lax.div(lax.broadcasted_iota(jnp.int32, (count, 2 * count), 1), 2)
    return (half == lax.broadcasted_iota(jnp.int32, (count, 2 * count), 0)).astype(F32)


def exact_dot(left, right):
    return jnp.dot(left, right, precision=lax.Precision.HIGHEST, preferred_element_type=F32)


def refine(coarse_ref):
    cx, cz, cy = coarse_ref.shape
    left, right = doubler(cz).T, doubler(cy)
    return [exact_dot(left, exact_dot(coarse_ref[x], right)) for x in range(cx)]


def first_kernel(
    home_hbm, old_hbm, conduct_hbm, source_hbm, reaction_hbm, coarse_hbm,
    za_ref, zb_ref, parts_ref, home_ref, old_ref, rows_ref, coarse_ref,
    home_sem, old_sems, sems, coarse_sem,
):
    slots = home_ref.shape[2]
    width = LANES // slots
    nx, nz, _ = old_hbm.shape
    size = rows_ref.shape[3]
    copies = [pltpu.make_async_copy(coarse_hbm, coarse_ref, coarse_sem)]
    loads = [pltpu.make_async_copy(old_hbm.at[x], old_ref.at[x], old_sems.at[x]) for x in range(nx)]
    for i, ref in enumerate((conduct_hbm, source_hbm, reaction_hbm)):
        for side, begin in enumerate((0, nz - size)):
            copies.append(
                pltpu.make_async_copy(
                    ref.at[:, pl.ds(begin, size), :], rows_ref.at[i, side], sems.at[i, side]
                )
            )
    load_home = pltpu.make_async_copy(home_hbm, home_ref, home_sem)
    for copy in [load_home] + loads + copies:
        copy.start()
    load_home.wait()

    slot, target = moved_slot(lambda j: home_ref[0, 0, j], slots)
    device = lax.div(target, slots)
    back = LANES - width * slot
    (x_first, x_last), (z_first, z_last), (y_first, y_last) = edges()
    row, lane = row_of((nx, LANES)), lane_of((nx, LANES))
    note = jnp.where(lane < 3 * width, device, slot).astype(F32)
    inner = (
        ((row == 0) & x_first).astype(F32)
        + ((row == nx - 1) & x_last).astype(F32)
        + ((lane == 0) & y_first).astype(F32)
        + ((lane == LANES - 1) & y_last).astype(F32)
    )
    rows = nz // slots
    count, planes = parts_ref.shape[0], parts_ref.shape[1] - 1
    group = lax.div(lane_of((rows, LANES)), width)
    for x in range(nx):
        loads[x].wait()
        box = jnp.zeros((rows, LANES), F32)
        for g in range(slots):
            shift = lax.rem(width * (g - slot) + LANES, LANES)
            rolled = pltpu.roll(old_ref[x, g * rows : (g + 1) * rows, :], shift, 1)
            box = jnp.where(group == g, rolled, box)
        parts_ref[x // planes, x % planes] = box
    for k in range(count):
        parts_ref[k, planes] = jnp.full((rows, LANES), device, jnp.int32).astype(F32)
    for copy in copies:
        copy.wait()
    cx, cz, cy = coarse_ref.shape
    ends = jnp.concatenate([coarse_ref[:, 0, :], coarse_ref[:, cz - 1, :]], axis=0)
    wide = exact_dot(ends, doubler(cy))

    def rims(first, second):
        near = pltpu.roll(first, lax.rem(back, LANES), 1)
        far = pltpu.roll(second, lax.rem(back + width, LANES), 1)
        return jnp.where(lane < width, near, jnp.where(lane < 2 * width, far, note))

    faces = []
    for side, first, second, edge in ((0, 0, 1, z_first), (1, size - 1, size - 2, z_last)):
        refined = jnp.zeros((nx, LANES), F32)
        for x in range(cx):
            refined = jnp.where(lax.div(row, 2) == x, wide[side * cx + x : side * cx + x + 1], refined)
        top = side * (nz - size)
        old, old2 = old_ref[:, top + first, :], old_ref[:, top + second, :]
        kappa, kappa2 = rows_ref[0, side, :, first, :], rows_ref[0, side, :, second, :]
        weight = (inner + jnp.where(edge, 1.0, 0.0)) * kappa
        src = rows_ref[1, side, :, first, :] + weight * refined
        rea = 1.0 + rows_ref[2, side, :, first, :] + weight
        faces.append([old, old2, kappa, kappa2, src, rea, rims(old, old2)])
    for i in range(7):
        write_pair("gz", za_ref, zb_ref, i, faces[0][i], faces[1][i])


def columns_kernel(
    sent_ref, old_ref, conduct_ref, source_ref, reaction_ref, coarse_ref, za_ref, zb_ref,
    ya_ref, yb_ref, *, width,
):
    nx, nz, _ = conduct_ref.shape
    cx, cz, cy = coarse_ref.shape
    (x_first, x_last), (z_first, z_last), _ = edges()
    lane = lane_of((cz, LANES))
    ends = jnp.zeros((cz, LANES), F32)
    for x in range(cx):
        plane = coarse_ref[x]
        for side, at in ((0, 0), (1, cy - 1)):
            column = jnp.broadcast_to(plane[:, at : at + 1], (cz, LANES))
            ends = jnp.where(lax.div(lane, 2) == side * cx + x, column, ends)
    refined = exact_dot(doubler(cz).T, ends)

    row, lane = row_of((nz, LANES)), lane_of((nz, LANES))
    low = high = jnp.zeros((nz, LANES), F32)
    for f, (ref, depth) in enumerate(
        ((old_ref, 0), (old_ref, 1), (conduct_ref, 0), (conduct_ref, 1), (source_ref, 0), (reaction_ref, 0))
    ):
        for x in range(nx):
            spot = f * nx + x
            low = jnp.where(lane == spot, roll_lanes(ref[x], spot - depth), low)
            high = jnp.where(lane == spot, roll_lanes(ref[x], spot + 1 + depth), high)
    field, x_at = lax.div(lane, nx), lax.rem(lane, nx)
    outside = (
        ((row == 0) & z_first).astype(F32)
        + ((row == nz - 1) & z_last).astype(F32)
        + ((x_at == 0) & x_first).astype(F32)
        + ((x_at == nx - 1) & x_last).astype(F32)
    )

    def fold(tile, at):
        src = tile + outside * roll_lanes(tile, (SRC - KAP1) * nx) * roll_lanes(refined, SRC * nx - at)
        rea = 1.0 + tile + outside * roll_lanes(tile, (REA - KAP1) * nx)
        return jnp.where(field == SRC, src, jnp.where(field == REA, rea, tile))

    write_pair("gy", ya_ref, yb_ref, slice(0, nz), fold(low, 0), fold(high, nx))

    lane = lane_of((nx, LANES))
    spot = slice(3 * width, 3 * width + 1)
    own = jnp.broadcast_to(sent_ref[RIM][:, spot], (nx, LANES))
    low = high = jnp.where(lane == 4, own, 0.0)
    notes = received("gz", za_ref[RIM], zb_ref[RIM])
    for side in range(2):
        note = jnp.broadcast_to(notes[side][:, spot], (nx, LANES))
        low = jnp.where(lane == 5 + side, note, low)
        high = jnp.where(lane == 5 + side, note, high)
        for f, tile in enumerate((PHI1, KAP1)):
            value = received("gz", za_ref[tile], zb_ref[tile])[side]
            at = 2 * side + f
            low = jnp.where(lane == at, roll_lanes(value, at), low)
            high = jnp.where(lane == at, roll_lanes(value, at + 1), high)
    write_pair("gy", ya_ref, yb_ref, slice(nz, nz + nx), low, high)


def fold_kernel(conduct_ref, source_ref, reaction_ref, coarse_ref, after_ref, src_ref, rea_ref):
    del after_ref
    nx, nz, _ = conduct_ref.shape
    (x_first, x_last), (z_first, z_last), (y_first, y_last) = edges()
    refined = refine(coarse_ref)
    row, lane = row_of((nz, LANES)), lane_of((nz, LANES))
    inner = (
        ((row == 0) & z_first).astype(F32)
        + ((row == nz - 1) & z_last).astype(F32)
        + ((lane == 0) & y_first).astype(F32)
        + ((lane == LANES - 1) & y_last).astype(F32)
    )
    for x in range(nx):
        faces = inner
        if x == 0:
            faces = faces + jnp.where(x_first, 1.0, 0.0)
        if x == nx - 1:
            faces = faces + jnp.where(x_last, 1.0, 0.0)
        weight = faces * conduct_ref[x]
        src_ref[x] = source_ref[x] + weight * refined[x // 2]
        rea_ref[x] = 1.0 + reaction_ref[x] + weight


def address_kernel(parts_ref, za_ref, zb_ref, send_ref, *, width):
    planes = send_ref.shape[1] - 2
    low, high = received("gz", za_ref[RIM], zb_ref[RIM])
    shape = low.shape
    lane = lane_of(shape)
    low_tag = jnp.broadcast_to(low[:, 2 * width : 2 * width + 1], shape)
    high_tag = jnp.broadcast_to(high[:, 2 * width : 2 * width + 1], shape)
    high = roll_lanes(high, 2 * width)
    lower = lane < 2 * width
    rims = jnp.where(lower, low, high)
    tag = jnp.where(lower, low_tag, high_tag)
    column = lax.rem(lane, width)
    beside = jnp.where(column < 2, -1.0, jnp.where(column >= width - 2, 1.0, -4096.0))
    edge = jnp.where(column == 0, -1.0, jnp.where(column == width - 1, 1.0, -4096.0))
    count = parts_ref.shape[0]
    columns = [
        (roll_lanes(parts_ref[k, planes] + beside, 4 * i), roll_lanes(parts_ref[k, i], 4 * i))
        for k in range(count)
        for i in range(planes)
    ]
    columns.append((roll_lanes(tag + edge, 4 * planes), roll_lanes(rims, 4 * planes)))
    for device in range(send_ref.shape[0]):
        for i in range(planes):
            value = jnp.zeros(shape, F32)
            for k in range(count):
                value = jnp.where(parts_ref[k, planes] == device, parts_ref[k, i], value)
            send_ref[device, i] = value
        send_ref[device, planes] = jnp.where(tag == device, rims, 0.0)
        value = jnp.zeros(shape, F32)
        for spot, source in columns:
            value = jnp.where(spot == device, source, value)
        send_ref[device, planes + 1] = value


def spread(tile, offset, width):
    piece = jnp.where(lane_of(tile.shape) < width, roll_lanes(tile, -offset), 0.0)
    result = piece
    for shift in range(width, LANES, width):
        result = result + roll_lanes(piece, shift)
    return result


def place_kernel(
    home_ref, recv_ref, old_ref, za_ref, zb_ref, ya_ref, yb_ref,
    start_ref, zhalo_ref, yhalo_ref, own_ref,
):
    slots = home_ref.shape[0]
    width = LANES // slots
    nx, nz, _ = old_ref.shape
    rows = nz // slots
    slot, _ = moved_slot(lambda j: home_ref[j], slots)
    planes = recv_ref.shape[1] - 2
    run = nx // planes
    count = recv_ref.shape[0]
    here = lax.div(lane_of((rows, LANES)), width) == slot

    def total(first, stride, tile):
        value = recv_ref[first, tile]
        for source in range(first + stride, count, stride):
            value = value + recv_ref[source, tile]
        return value

    for k in range(run):
        for i in range(planes):
            x = k * planes + i
            arrived = total(k, run, i)
            for g in range(slots):
                shift = lax.rem(width * (slot - g) + LANES, LANES)
                part = pl.ds(g * rows, rows)
                start_ref[x, part, :] = jnp.where(
                    here, pltpu.roll(arrived, shift, 1), old_ref[x, part, :]
                )

    rims = total(0, 1, planes)
    faces = [received("gz", za_ref[i], zb_ref[i]) for i in range(7)]
    group = lax.div(lane_of((nx, LANES)), width).astype(F32)
    for side in range(2):
        note = faces[RIM][side]
        there = jnp.broadcast_to(note[:, 3 * width : 3 * width + 1], note.shape) == group
        for depth in range(2):
            moved = spread(rims, (2 * side + depth) * width, width)
            zhalo_ref[side, depth] = jnp.where(there, moved, faces[depth][side])

    beside = [total(k, run, planes + 1) for k in range(run)]
    every = beside[0]
    for k in range(1, run):
        every = every + beside[k]
    lane = lane_of((rows, LANES))
    corner_lane = lane_of((nx, LANES))
    halos = received("gy", ya_ref[:nz], yb_ref[:nz])
    corners = received("gy", ya_ref[nz : nz + nx], yb_ref[nz : nz + nx])
    for side in range(2):
        outer = width - 1 if side == 0 else 0
        inward = -1 if side == 0 else 1
        touched = float(slots - 1 if side == 0 else 0)
        note = jnp.broadcast_to(corners[side][0:1, 4:5], (rows, LANES)) == touched
        for g in range(slots):
            value = jnp.zeros((rows, LANES), F32)
            for x in range(nx):
                source = beside[x // planes]
                for depth in range(2):
                    at = g * width + outer + inward * depth + 4 * (x % planes)
                    spot = depth * nx + x
                    value = jnp.where(lane == spot, roll_lanes(source, spot - at), value)
            held = halos[side][g * rows : (g + 1) * rows]
            yhalo_ref[side, g * rows : (g + 1) * rows] = jnp.where(
                note & (lane < 2 * nx), value, held
            )
        corner = corners[side]
        for z_side in range(2):
            note = jnp.broadcast_to(corner[:, 5 + z_side : 6 + z_side], (nx, LANES)) == touched
            at = 2 * width * z_side + outer + 4 * planes
            spot = 2 * z_side
            corner = jnp.where(
                note & (corner_lane == spot), roll_lanes(every, spot - at), corner
            )
        yhalo_ref[side, nz : nz + nx] = corner

    lane = lane_of((nz, LANES))
    low = high = jnp.zeros((nz, LANES), F32)
    for x in range(nx):
        low = jnp.where(lane == x, roll_lanes(start_ref[x], x), low)
        high = jnp.where(lane == x, roll_lanes(start_ref[x], x + 1), high)
    own_ref[0] = low
    own_ref[1] = high


def edge_kernel(
    start_ref, conduct_ref, src_ref, rea_ref, zhalo_ref, yhalo_ref, za_ref, zb_ref,
    xa_ref, xb_ref,
):
    nx, nz, _ = start_ref.shape
    for f, (ref, depth) in enumerate(
        ((start_ref, 0), (start_ref, 1), (conduct_ref, 0), (conduct_ref, 1), (src_ref, 0), (rea_ref, 0))
    ):
        write_pair(
            "gx", xa_ref, xb_ref, slice(f * nz, (f + 1) * nz), ref[depth], ref[nx - 1 - depth]
        )
    base = 6 * nz
    kappas = received("gz", za_ref[KAP1], zb_ref[KAP1])
    xa_ref[base : base + 8] = jnp.zeros((8, LANES), F32)
    xb_ref[base : base + 8] = jnp.zeros((8, LANES), F32)
    for side in range(2):
        for f, tile in enumerate((zhalo_ref[side, 0], kappas[side])):
            spot = base + 2 * side + f
            write_pair(
                "gx", xa_ref, xb_ref, slice(spot, spot + 1), tile[0:1], tile[nx - 1 : nx]
            )
    lane = lane_of((nz, LANES))
    low = high = jnp.zeros((nz, LANES), F32)
    for side in range(2):
        halo = yhalo_ref[side, :nz]
        for f, offset in enumerate((PHI1 * nx, KAP1 * nx)):
            spot = 2 * side + f
            low = jnp.where(lane == spot, roll_lanes(halo, spot - offset), low)
            high = jnp.where(lane == spot, roll_lanes(halo, spot - offset - nx + 1), high)
    write_pair("gx", xa_ref, xb_ref, slice(base + 8, base + 8 + nz), low, high)


def step(numerator, denominator, kappa, sides):
    for phi, beside, outside in sides:
        weight = 0.5 * (kappa + beside)
        if outside is not None:
            weight = jnp.where(outside, 0.0, weight)
        numerator = numerator + weight * phi
        denominator = denominator + weight
    return numerator / denominator


def along_rows(phi, kappa, low, high, flags):
    row = row_of(phi.shape)
    last = phi.shape[0] - 1
    low_edge, high_edge = row == 0, row == last
    return [
        (
            jnp.where(low_edge, low[0], roll_rows(phi, 1)),
            jnp.where(low_edge, low[1], roll_rows(kappa, 1)),
            low_edge & flags[0],
        ),
        (
            jnp.where(high_edge, high[0], roll_rows(phi, last)),
            jnp.where(high_edge, high[1], roll_rows(kappa, last)),
            high_edge & flags[1],
        ),
    ]


def along_lanes(phi, kappa, low, high, flags, last=LANES - 1):
    lane = lane_of(phi.shape)
    low_edge, high_edge = lane == 0, lane == last
    return [
        (
            jnp.where(low_edge, low[0], roll_lanes(phi, 1)),
            jnp.where(low_edge, low[1], roll_lanes(kappa, 1)),
            low_edge & flags[0],
        ),
        (
            jnp.where(high_edge, high[0], roll_lanes(phi, -1)),
            jnp.where(high_edge, high[1], roll_lanes(kappa, -1)),
            high_edge & flags[1],
        ),
    ]


def to_row(tile, spot):
    column = jnp.broadcast_to(tile[:, spot : spot + 1], tile.shape)
    return jnp.sum(
        jnp.where(lane_of(tile.shape) == row_of(tile.shape), column, 0.0), axis=0, keepdims=True
    )


def sweep_plane(x, phi, kappa, numerator, denominator, sides, z_phi, z_kappa, y_phi, y_kappa, flags_z, flags_y):
    sides = sides + along_rows(
        phi,
        kappa,
        (z_phi[0][x : x + 1], z_kappa[0][x : x + 1]),
        (z_phi[1][x : x + 1], z_kappa[1][x : x + 1]),
        flags_z,
    )
    spot = KAP1 * z_phi[0].shape[0] + x
    sides += along_lanes(
        phi,
        kappa,
        (roll_lanes(y_phi[0], -x), roll_lanes(y_kappa[0], -spot)),
        (roll_lanes(y_phi[1], LANES - 1 - x), roll_lanes(y_kappa[1], LANES - 1 - spot)),
        flags_y,
    )
    return step(numerator, denominator, kappa, sides)


def inner_kernel(
    start_ref, conduct_ref, src_ref, rea_ref, zhalo_ref, yhalo_ref, za_ref, zb_ref, after_ref,
    first_ref,
):
    del after_ref
    nx, nz, _ = start_ref.shape
    _, flags_z, flags_y = edges()
    z_kappa = received("gz", za_ref[KAP1], zb_ref[KAP1])
    z_phi = (zhalo_ref[0, 0], zhalo_ref[1, 0])
    yf = [yhalo_ref[side, :nz] for side in range(2)]
    first_ref[0] = start_ref[0]
    first_ref[nx - 1] = start_ref[nx - 1]
    for x in range(1, nx - 1):
        sides = [(start_ref[i], conduct_ref[i], None) for i in (x - 1, x + 1)]
        first_ref[x] = sweep_plane(
            x, start_ref[x], conduct_ref[x], start_ref[x] + src_ref[x], rea_ref[x],
            sides, z_phi, z_kappa, yf, yf, flags_z, flags_y,
        )


def sweeps_kernel(
    start_ref, conduct_ref, src_ref, rea_ref, zhalo_ref, yhalo_ref, own_ref,
    za_ref, zb_ref, sya_ref, syb_ref, xa_ref, xb_ref, first_ref,
    out_ref,
):
    nx, nz, _ = start_ref.shape
    flags_x, flags_z, flags_y = edges()
    start = [start_ref[x] for x in range(nx)]
    conduct = [conduct_ref[x] for x in range(nx)]
    base = 6 * nz

    def part(axis, a_ref, b_ref, begin, size):
        return received(axis, a_ref[begin : begin + size], b_ref[begin : begin + size])

    xf = [part("gx", xa_ref, xb_ref, f * nz, nz) for f in range(6)]
    xrows = part("gx", xa_ref, xb_ref, base, 8)
    xcols = part("gx", xa_ref, xb_ref, base + 8, nz)
    zf = [received("gz", za_ref[i], zb_ref[i]) for i in range(6)]
    yf = [yhalo_ref[side, :nz] for side in range(2)]
    yt = [yhalo_ref[side, nz : nz + nx] for side in range(2)]
    sf = sent("gy", sya_ref[:nz], syb_ref[:nz])

    def columns(tile, phi_spot, kappa_spot, lane):
        return roll_lanes(tile, lane - phi_spot), roll_lanes(tile, lane - kappa_spot)

    x_first_sweep = []
    for side in range(2):
        phi, kappa = xf[PHI1][side], xf[KAP1][side]
        me = 0 if side == 0 else nx - 1
        rows = xrows[side]
        sides = [(xf[PHI2][side], xf[KAP2][side], None), (start[me], conduct[me], None)]
        sides += along_rows(phi, kappa, (rows[0:1], rows[1:2]), (rows[2:3], rows[3:4]), flags_z)
        tile = xcols[side]
        sides += along_lanes(
            phi, kappa, columns(tile, 0, 1, 0), columns(tile, 2, 3, LANES - 1), flags_y
        )
        x_first_sweep.append(step(phi + xf[SRC][side], xf[REA][side], kappa, sides))

    z_first_sweep = []
    for side in range(2):
        phi, kappa = zhalo_ref[side, 0], zf[KAP1][side]
        me = 0 if side == 0 else nz - 1
        at = 2 * side
        sides = [
            (zhalo_ref[side, 1], zf[KAP2][side], None),
            (start_ref[:, me, :], conduct_ref[:, me, :], None),
        ]
        sides += along_rows(
            phi,
            kappa,
            (xrows[0][at : at + 1], xrows[0][at + 1 : at + 2]),
            (xrows[1][at : at + 1], xrows[1][at + 1 : at + 2]),
            flags_x,
        )
        sides += along_lanes(
            phi,
            kappa,
            columns(yt[0], at, at + 1, 0),
            columns(yt[1], at, at + 1, LANES - 1),
            flags_y,
        )
        z_first_sweep.append(step(phi + zf[SRC][side], zf[REA][side], kappa, sides))

    y_first_sweep = []
    for side in range(2):
        phi, phi2, kappa, kappa2, src, rea = [roll_lanes(yf[side], -f * nx) for f in range(6)]
        at = 2 * side
        sides = [(phi2, kappa2, None), (own_ref[side], roll_lanes(sf[side], -KAP1 * nx), None)]
        sides += along_rows(
            phi,
            kappa,
            (to_row(yt[side], 0), to_row(yt[side], 1)),
            (to_row(yt[side], 2), to_row(yt[side], 3)),
            flags_z,
        )
        sides += along_lanes(
            phi,
            kappa,
            columns(xcols[0], at, at + 1, 0),
            columns(xcols[1], at, at + 1, nx - 1),
            flags_x,
            nx - 1,
        )
        y_first_sweep.append(step(phi + src, rea, kappa, sides))

    def sweep(phis, x_phi, z_phi, y_phi, planes):
        below = [(x_phi[0], xf[KAP1][0], flags_x[0])] + [(phis[x], conduct[x], None) for x in range(nx - 1)]
        above = [(phis[x], conduct[x], None) for x in range(1, nx)] + [(x_phi[1], xf[KAP1][1], flags_x[1])]
        return [
            sweep_plane(
                x, phis[x], conduct[x], start[x] + src_ref[x], rea_ref[x],
                [below[x], above[x]], z_phi, zf[KAP1], y_phi, yf, flags_z, flags_y,
            )
            for x in planes
        ]

    ends = sweep(start, xf[PHI1], (zhalo_ref[0, 0], zhalo_ref[1, 0]), yf, (0, nx - 1))
    first = [ends[0]] + [first_ref[x] for x in range(1, nx - 1)] + [ends[1]]
    second = sweep(first, x_first_sweep, z_first_sweep, y_first_sweep, range(nx))
    for x in range(nx):
        out_ref[x] = second[x]


def swap(axis, first, second):
    count = lax.axis_size(axis)
    results = []
    for j, value in ((1, second), (0, first)):
        pairs = []
        for low in range(j, count - 1, 2):
            pairs += [(low, low + 1), (low + 1, low)]
        results.append(lax.ppermute(value, axis, pairs))
    return results[::-1]


def call(kernel, operands, outs, smem=0, hbm=(), scratch=()):
    specs = [SMEM] * smem + [VMEM] * (len(operands) - smem)
    operands = list(operands)
    for i in hbm:
        specs[i] = HBM
        operands[i] = pltpu.with_memory_space_constraint(operands[i], pltpu.HBM)
    return pl.pallas_call(
        kernel,
        out_shape=[jax.ShapeDtypeStruct(shape, F32) for shape in outs],
        in_specs=specs,
        out_specs=[VMEM] * len(outs),
        scratch_shapes=scratch,
        compiler_params=PARAMS,
    )(*operands)


def on_device(old_field, new_home, conduct, reaction, source, coarse):
    nx, nz, ny = block = old_field.shape
    home = new_home[0, 0]
    slots = home.shape[0]
    rows, width = nz // slots, ny // slots
    line = lax.axis_size("gy")
    part = nx // RUN

    sza, szb, parts = call(
        first_kernel,
        (new_home, old_field, conduct, source, reaction, coarse),
        [(7, nx, ny), (7, nx, ny), (RUN, part + 1, rows, ny)],
        hbm=(0, 1, 2, 3, 4, 5),
        scratch=[
            pltpu.SMEM(new_home.shape, jnp.int32),
            pltpu.VMEM(block, F32),
            pltpu.VMEM((3, 2, nx, 8, ny), F32),
            pltpu.VMEM(coarse.shape, F32),
            pltpu.SemaphoreType.DMA,
            pltpu.SemaphoreType.DMA((nx,)),
            pltpu.SemaphoreType.DMA((3, 2)),
            pltpu.SemaphoreType.DMA,
        ],
    )
    za, zb = swap("gz", sza, szb)
    groups = [[i * RUN + k for k in range(RUN)] for i in range(line // RUN)]
    parts = lax.all_to_all(parts, "gy", 0, 0, tiled=True, axis_index_groups=groups)

    def address(*refs):
        address_kernel(*refs, width=width)

    (send,) = call(address, (parts, za, zb), [(line, part + 2, rows, ny)])
    recv = lax.all_to_all(send, "gy", 0, 0, tiled=True)

    def columns(*refs):
        columns_kernel(*refs, width=width)

    sya, syb = call(
        columns, (sza, old_field, conduct, source, reaction, coarse, za, zb), [(nz + nx, ny)] * 2
    )
    ya, yb = swap("gy", sya, syb)
    src, rea = call(fold_kernel, (conduct, source, reaction, coarse, sya), [block, block])
    start, zhalo, yhalo, own = call(
        place_kernel,
        (home, recv, old_field, za, zb, ya, yb),
        [block, (2, 2, nx, ny), (2, nz + nx, ny), (2, nz, ny)],
        smem=1,
    )
    xa, xb = call(
        edge_kernel,
        (start, conduct, src, rea, zhalo, yhalo, za, zb),
        [(7 * nz + 8, ny)] * 2,
    )
    (first,) = call(
        inner_kernel, (start, conduct, src, rea, zhalo, yhalo, za, zb, xa), [block]
    )
    xa, xb = swap("gx", xa, xb)
    (relaxed,) = call(
        sweeps_kernel,
        (start, conduct, src, rea, zhalo, yhalo, own, za, zb, sya, syb, xa, xb, first),
        [block],
    )
    return relaxed


def solution(mesh):
    return jax.shard_map(
        on_device,
        mesh=mesh,
        in_specs=(P("gx", "gz", "gy"),) * 6,
        out_specs=P("gx", "gz", "gy"),
        check_vma=False,
    )
```

```python
import jax
import jax.numpy as jnp
from jax import lax
from jax.experimental import pallas as pl
from jax.experimental.pallas import tpu as pltpu
from jax.sharding import PartitionSpec as P

LANES = 128
RUN = 4
VMEM = pl.BlockSpec(memory_space=pltpu.VMEM)
SMEM = pl.BlockSpec(memory_space=pltpu.SMEM)
HBM = pl.BlockSpec(memory_space=pltpu.HBM)
PARAMS = pltpu.CompilerParams(vmem_limit_bytes=24 * 1024 * 1024)
F32 = jnp.float32

PHI1, PHI2, KAP1, KAP2, SRC, REA, RIM = range(7)


def lane_of(shape):
    return lax.broadcasted_iota(jnp.int32, shape, len(shape) - 1)


def row_of(shape):
    return lax.broadcasted_iota(jnp.int32, shape, len(shape) - 2)


def roll_lanes(value, shift):
    shift = shift % LANES
    return pltpu.roll(value, shift, value.ndim - 1) if shift else value


def roll_rows(value, shift):
    return pltpu.roll(value, shift % value.shape[0], 0)


def moved_slot(home_of, slots):
    position = lax.axis_index("gy")
    slot = jnp.int32(0)
    target = jnp.int32(0)
    for j in range(slots):
        home = home_of(j)
        leaves = home != position * slots + j
        slot = jnp.where(leaves, j, slot)
        target = jnp.where(leaves, home, target)
    return slot, target


def edges():
    flags = []
    for axis in ("gx", "gz", "gy"):
        index = lax.axis_index(axis)
        flags.append((index == 0, index == lax.axis_size(axis) - 1))
    return flags


def is_even(axis):
    return lax.rem(lax.axis_index(axis), 2) == 0


def write_pair(axis, first_ref, second_ref, index, low, high):
    even = is_even(axis)
    first_ref[index] = jnp.where(even, high, low)
    second_ref[index] = jnp.where(even, low, high)


def received(axis, first, second):
    even = is_even(axis)
    return jnp.where(even, second, first), jnp.where(even, first, second)


def sent(axis, first, second):
    even = is_even(axis)
    return jnp.where(even, second, first), jnp.where(even, first, second)


def doubler(count):
    half = lax.div(lax.broadcasted_iota(jnp.int32, (count, 2 * count), 1), 2)
    return (half == lax.broadcasted_iota(jnp.int32, (count, 2 * count), 0)).astype(F32)


def exact_dot(left, right):
    return jnp.dot(left, right, precision=lax.Precision.HIGHEST, preferred_element_type=F32)


def refine(coarse_ref):
    cx, cz, cy = coarse_ref.shape
    left, right = doubler(cz).T, doubler(cy)
    return [exact_dot(left, exact_dot(coarse_ref[x], right)) for x in range(cx)]


def first_kernel(
    home_hbm, old_hbm, conduct_hbm, source_hbm, reaction_hbm, coarse_hbm,
    za_ref, zb_ref, parts_ref, home_ref, old_ref, rows_ref, coarse_ref,
    home_sem, old_sems, sems, coarse_sem,
):
    slots = home_ref.shape[2]
    width = LANES // slots
    nx, nz, _ = old_hbm.shape
    size = rows_ref.shape[3]
    copies = [pltpu.make_async_copy(coarse_hbm, coarse_ref, coarse_sem)]
    loads = [pltpu.make_async_copy(old_hbm.at[x], old_ref.at[x], old_sems.at[x]) for x in range(nx)]
    for i, ref in enumerate((conduct_hbm, source_hbm, reaction_hbm)):
        for side, begin in enumerate((0, nz - size)):
            copies.append(
                pltpu.make_async_copy(
                    ref.at[:, pl.ds(begin, size), :], rows_ref.at[i, side], sems.at[i, side]
                )
            )
    load_home = pltpu.make_async_copy(home_hbm, home_ref, home_sem)
    for copy in [load_home] + loads + copies:
        copy.start()
    load_home.wait()

    slot, target = moved_slot(lambda j: home_ref[0, 0, j], slots)
    device = lax.div(target, slots)
    back = LANES - width * slot
    (x_first, x_last), (z_first, z_last), (y_first, y_last) = edges()
    row, lane = row_of((nx, LANES)), lane_of((nx, LANES))
    note = jnp.where(lane < 3 * width, device, slot).astype(F32)
    inner = (
        ((row == 0) & x_first).astype(F32)
        + ((row == nx - 1) & x_last).astype(F32)
        + ((lane == 0) & y_first).astype(F32)
        + ((lane == LANES - 1) & y_last).astype(F32)
    )
    rows = nz // slots
    count, planes = parts_ref.shape[0], parts_ref.shape[1] - 1
    group = lax.div(lane_of((rows, LANES)), width)
    for x in range(nx):
        loads[x].wait()
        box = jnp.zeros((rows, LANES), F32)
        for g in range(slots):
            shift = lax.rem(width * (g - slot) + LANES, LANES)
            rolled = pltpu.roll(old_ref[x, g * rows : (g + 1) * rows, :], shift, 1)
            box = jnp.where(group == g, rolled, box)
        parts_ref[x // planes, x % planes] = box
    for k in range(count):
        parts_ref[k, planes] = jnp.full((rows, LANES), device, jnp.int32).astype(F32)
    for copy in copies:
        copy.wait()
    cx, cz, cy = coarse_ref.shape
    ends = jnp.concatenate([coarse_ref[:, 0, :], coarse_ref[:, cz - 1, :]], axis=0)
    wide = exact_dot(ends, doubler(cy))

    def rims(first, second):
        near = pltpu.roll(first, lax.rem(back, LANES), 1)
        far = pltpu.roll(second, lax.rem(back + width, LANES), 1)
        return jnp.where(lane < width, near, jnp.where(lane < 2 * width, far, note))

    faces = []
    for side, first, second, edge in ((0, 0, 1, z_first), (1, size - 1, size - 2, z_last)):
        refined = jnp.zeros((nx, LANES), F32)
        for x in range(cx):
            refined = jnp.where(lax.div(row, 2) == x, wide[side * cx + x : side * cx + x + 1], refined)
        top = side * (nz - size)
        old, old2 = old_ref[:, top + first, :], old_ref[:, top + second, :]
        kappa, kappa2 = rows_ref[0, side, :, first, :], rows_ref[0, side, :, second, :]
        weight = (inner + jnp.where(edge, 1.0, 0.0)) * kappa
        src = rows_ref[1, side, :, first, :] + weight * refined
        rea = 1.0 + rows_ref[2, side, :, first, :] + weight
        faces.append([old, old2, kappa, kappa2, src, rea, rims(old, old2)])
    for i in range(7):
        write_pair("gz", za_ref, zb_ref, i, faces[0][i], faces[1][i])


def columns_kernel(
    sent_ref, old_ref, conduct_ref, source_ref, reaction_ref, coarse_ref, za_ref, zb_ref,
    ya_ref, yb_ref, *, width,
):
    nx, nz, _ = conduct_ref.shape
    cx, cz, cy = coarse_ref.shape
    (x_first, x_last), (z_first, z_last), _ = edges()
    lane = lane_of((cz, LANES))
    ends = jnp.zeros((cz, LANES), F32)
    for x in range(cx):
        plane = coarse_ref[x]
        for side, at in ((0, 0), (1, cy - 1)):
            column = jnp.broadcast_to(plane[:, at : at + 1], (cz, LANES))
            ends = jnp.where(lax.div(lane, 2) == side * cx + x, column, ends)
    refined = exact_dot(doubler(cz).T, ends)

    row, lane = row_of((nz, LANES)), lane_of((nz, LANES))
    low = high = jnp.zeros((nz, LANES), F32)
    for f, (ref, depth) in enumerate(
        ((old_ref, 0), (old_ref, 1), (conduct_ref, 0), (conduct_ref, 1), (source_ref, 0), (reaction_ref, 0))
    ):
        for x in range(nx):
            spot = f * nx + x
            low = jnp.where(lane == spot, roll_lanes(ref[x], spot - depth), low)
            high = jnp.where(lane == spot, roll_lanes(ref[x], spot + 1 + depth), high)
    field, x_at = lax.div(lane, nx), lax.rem(lane, nx)
    outside = (
        ((row == 0) & z_first).astype(F32)
        + ((row == nz - 1) & z_last).astype(F32)
        + ((x_at == 0) & x_first).astype(F32)
        + ((x_at == nx - 1) & x_last).astype(F32)
    )

    def fold(tile, at):
        src = tile + outside * roll_lanes(tile, (SRC - KAP1) * nx) * roll_lanes(refined, SRC * nx - at)
        rea = 1.0 + tile + outside * roll_lanes(tile, (REA - KAP1) * nx)
        return jnp.where(field == SRC, src, jnp.where(field == REA, rea, tile))

    write_pair("gy", ya_ref, yb_ref, slice(0, nz), fold(low, 0), fold(high, nx))

    lane = lane_of((nx, LANES))
    spot = slice(3 * width, 3 * width + 1)
    own = jnp.broadcast_to(sent_ref[RIM][:, spot], (nx, LANES))
    low = high = jnp.where(lane == 4, own, 0.0)
    notes = received("gz", za_ref[RIM], zb_ref[RIM])
    for side in range(2):
        note = jnp.broadcast_to(notes[side][:, spot], (nx, LANES))
        low = jnp.where(lane == 5 + side, note, low)
        high = jnp.where(lane == 5 + side, note, high)
        for f, tile in enumerate((PHI1, KAP1)):
            value = received("gz", za_ref[tile], zb_ref[tile])[side]
            at = 2 * side + f
            low = jnp.where(lane == at, roll_lanes(value, at), low)
            high = jnp.where(lane == at, roll_lanes(value, at + 1), high)
    write_pair("gy", ya_ref, yb_ref, slice(nz, nz + nx), low, high)


def fold_kernel(conduct_ref, source_ref, reaction_ref, coarse_ref, after_ref, src_ref, rea_ref):
    del after_ref
    nx, nz, _ = conduct_ref.shape
    (x_first, x_last), (z_first, z_last), (y_first, y_last) = edges()
    refined = refine(coarse_ref)
    row, lane = row_of((nz, LANES)), lane_of((nz, LANES))
    inner = (
        ((row == 0) & z_first).astype(F32)
        + ((row == nz - 1) & z_last).astype(F32)
        + ((lane == 0) & y_first).astype(F32)
        + ((lane == LANES - 1) & y_last).astype(F32)
    )
    for x in range(nx):
        faces = inner
        if x == 0:
            faces = faces + jnp.where(x_first, 1.0, 0.0)
        if x == nx - 1:
            faces = faces + jnp.where(x_last, 1.0, 0.0)
        weight = faces * conduct_ref[x]
        src_ref[x] = source_ref[x] + weight * refined[x // 2]
        rea_ref[x] = 1.0 + reaction_ref[x] + weight


def address_kernel(parts_ref, za_ref, zb_ref, send_ref, *, width):
    planes = send_ref.shape[1] - 2
    low, high = received("gz", za_ref[RIM], zb_ref[RIM])
    shape = low.shape
    lane = lane_of(shape)
    low_tag = jnp.broadcast_to(low[:, 2 * width : 2 * width + 1], shape)
    high_tag = jnp.broadcast_to(high[:, 2 * width : 2 * width + 1], shape)
    high = roll_lanes(high, 2 * width)
    lower = lane < 2 * width
    rims = jnp.where(lower, low, high)
    tag = jnp.where(lower, low_tag, high_tag)
    column = lax.rem(lane, width)
    beside = jnp.where(column < 2, -1.0, jnp.where(column >= width - 2, 1.0, -4096.0))
    edge = jnp.where(column == 0, -1.0, jnp.where(column == width - 1, 1.0, -4096.0))
    count = parts_ref.shape[0]
    columns = [
        (roll_lanes(parts_ref[k, planes] + beside, 4 * i), roll_lanes(parts_ref[k, i], 4 * i))
        for k in range(count)
        for i in range(planes)
    ]
    columns.append((roll_lanes(tag + edge, 4 * planes), roll_lanes(rims, 4 * planes)))
    for device in range(send_ref.shape[0]):
        for i in range(planes):
            value = jnp.zeros(shape, F32)
            for k in range(count):
                value = jnp.where(parts_ref[k, planes] == device, parts_ref[k, i], value)
            send_ref[device, i] = value
        send_ref[device, planes] = jnp.where(tag == device, rims, 0.0)
        value = jnp.zeros(shape, F32)
        for spot, source in columns:
            value = jnp.where(spot == device, source, value)
        send_ref[device, planes + 1] = value


def spread(tile, offset, width):
    piece = jnp.where(lane_of(tile.shape) < width, roll_lanes(tile, -offset), 0.0)
    result = piece
    for shift in range(width, LANES, width):
        result = result + roll_lanes(piece, shift)
    return result


def place_kernel(
    home_ref, recv_ref, old_ref, za_ref, zb_ref, ya_ref, yb_ref,
    start_ref, zhalo_ref, yhalo_ref,
):
    slots = home_ref.shape[0]
    width = LANES // slots
    nx, nz, _ = old_ref.shape
    rows = nz // slots
    slot, _ = moved_slot(lambda j: home_ref[j], slots)
    planes = recv_ref.shape[1] - 2
    run = nx // planes
    count = recv_ref.shape[0]
    here = lax.div(lane_of((rows, LANES)), width) == slot

    def total(first, stride, tile):
        value = recv_ref[first, tile]
        for source in range(first + stride, count, stride):
            value = value + recv_ref[source, tile]
        return value

    for k in range(run):
        for i in range(planes):
            x = k * planes + i
            arrived = total(k, run, i)
            for g in range(slots):
                shift = lax.rem(width * (slot - g) + LANES, LANES)
                part = pl.ds(g * rows, rows)
                start_ref[x, part, :] = jnp.where(
                    here, pltpu.roll(arrived, shift, 1), old_ref[x, part, :]
                )

    rims = total(0, 1, planes)
    faces = [received("gz", za_ref[i], zb_ref[i]) for i in range(7)]
    group = lax.div(lane_of((nx, LANES)), width).astype(F32)
    for side in range(2):
        note = faces[RIM][side]
        there = jnp.broadcast_to(note[:, 3 * width : 3 * width + 1], note.shape) == group
        for depth in range(2):
            moved = spread(rims, (2 * side + depth) * width, width)
            zhalo_ref[side, depth] = jnp.where(there, moved, faces[depth][side])

    beside = [total(k, run, planes + 1) for k in range(run)]
    every = beside[0]
    for k in range(1, run):
        every = every + beside[k]
    lane = lane_of((rows, LANES))
    corner_lane = lane_of((nx, LANES))
    halos = received("gy", ya_ref[:nz], yb_ref[:nz])
    corners = received("gy", ya_ref[nz : nz + nx], yb_ref[nz : nz + nx])
    for side in range(2):
        outer = width - 1 if side == 0 else 0
        inward = -1 if side == 0 else 1
        touched = float(slots - 1 if side == 0 else 0)
        note = jnp.broadcast_to(corners[side][0:1, 4:5], (rows, LANES)) == touched
        for g in range(slots):
            value = jnp.zeros((rows, LANES), F32)
            for x in range(nx):
                source = beside[x // planes]
                for depth in range(2):
                    at = g * width + outer + inward * depth + 4 * (x % planes)
                    spot = depth * nx + x
                    value = jnp.where(lane == spot, roll_lanes(source, spot - at), value)
            held = halos[side][g * rows : (g + 1) * rows]
            yhalo_ref[side, g * rows : (g + 1) * rows] = jnp.where(
                note & (lane < 2 * nx), value, held
            )
        corner = corners[side]
        for z_side in range(2):
            note = jnp.broadcast_to(corner[:, 5 + z_side : 6 + z_side], (nx, LANES)) == touched
            at = 2 * width * z_side + outer + 4 * planes
            spot = 2 * z_side
            corner = jnp.where(
                note & (corner_lane == spot), roll_lanes(every, spot - at), corner
            )
        yhalo_ref[side, nz : nz + nx] = corner


def edge_kernel(
    start_ref, conduct_ref, src_ref, rea_ref, zhalo_ref, yhalo_ref, za_ref, zb_ref,
    xa_ref, xb_ref,
):
    nx, nz, _ = start_ref.shape
    for f, (ref, depth) in enumerate(
        ((start_ref, 0), (start_ref, 1), (conduct_ref, 0), (conduct_ref, 1), (src_ref, 0), (rea_ref, 0))
    ):
        write_pair(
            "gx", xa_ref, xb_ref, slice(f * nz, (f + 1) * nz), ref[depth], ref[nx - 1 - depth]
        )
    base = 6 * nz
    kappas = received("gz", za_ref[KAP1], zb_ref[KAP1])
    xa_ref[base : base + 8] = jnp.zeros((8, LANES), F32)
    xb_ref[base : base + 8] = jnp.zeros((8, LANES), F32)
    for side in range(2):
        for f, tile in enumerate((zhalo_ref[side, 0], kappas[side])):
            spot = base + 2 * side + f
            write_pair(
                "gx", xa_ref, xb_ref, slice(spot, spot + 1), tile[0:1], tile[nx - 1 : nx]
            )
    lane = lane_of((nz, LANES))
    low = high = jnp.zeros((nz, LANES), F32)
    for side in range(2):
        halo = yhalo_ref[side, :nz]
        for f, offset in enumerate((PHI1 * nx, KAP1 * nx)):
            spot = 2 * side + f
            low = jnp.where(lane == spot, roll_lanes(halo, spot - offset), low)
            high = jnp.where(lane == spot, roll_lanes(halo, spot - offset - nx + 1), high)
    write_pair("gx", xa_ref, xb_ref, slice(base + 8, base + 8 + nz), low, high)


def step(numerator, denominator, kappa, sides):
    for phi, beside, outside in sides:
        weight = 0.5 * (kappa + beside)
        if outside is not None:
            weight = jnp.where(outside, 0.0, weight)
        numerator = numerator + weight * phi
        denominator = denominator + weight
    return numerator / denominator


def along_rows(phi, kappa, low, high, flags):
    row = row_of(phi.shape)
    last = phi.shape[0] - 1
    low_edge, high_edge = row == 0, row == last
    return [
        (
            jnp.where(low_edge, low[0], roll_rows(phi, 1)),
            jnp.where(low_edge, low[1], roll_rows(kappa, 1)),
            low_edge & flags[0],
        ),
        (
            jnp.where(high_edge, high[0], roll_rows(phi, last)),
            jnp.where(high_edge, high[1], roll_rows(kappa, last)),
            high_edge & flags[1],
        ),
    ]


def along_lanes(phi, kappa, low, high, flags, last=LANES - 1):
    lane = lane_of(phi.shape)
    low_edge, high_edge = lane == 0, lane == last
    return [
        (
            jnp.where(low_edge, low[0], roll_lanes(phi, 1)),
            jnp.where(low_edge, low[1], roll_lanes(kappa, 1)),
            low_edge & flags[0],
        ),
        (
            jnp.where(high_edge, high[0], roll_lanes(phi, -1)),
            jnp.where(high_edge, high[1], roll_lanes(kappa, -1)),
            high_edge & flags[1],
        ),
    ]


def to_row(tile, spot):
    column = jnp.broadcast_to(tile[:, spot : spot + 1], tile.shape)
    return jnp.sum(
        jnp.where(lane_of(tile.shape) == row_of(tile.shape), column, 0.0), axis=0, keepdims=True
    )


def sweep_plane(x, phi, kappa, numerator, denominator, sides, z_phi, z_kappa, y_phi, y_kappa, flags_z, flags_y):
    sides = sides + along_rows(
        phi,
        kappa,
        (z_phi[0][x : x + 1], z_kappa[0][x : x + 1]),
        (z_phi[1][x : x + 1], z_kappa[1][x : x + 1]),
        flags_z,
    )
    spot = KAP1 * z_phi[0].shape[0] + x
    sides += along_lanes(
        phi,
        kappa,
        (roll_lanes(y_phi[0], -x), roll_lanes(y_kappa[0], -spot)),
        (roll_lanes(y_phi[1], LANES - 1 - x), roll_lanes(y_kappa[1], LANES - 1 - spot)),
        flags_y,
    )
    return step(numerator, denominator, kappa, sides)


def inner_kernel(
    start_ref, conduct_ref, src_ref, rea_ref, zhalo_ref, yhalo_ref, za_ref, zb_ref, after_ref,
    first_ref, own_ref,
):
    del after_ref
    nx, nz, _ = start_ref.shape
    _, flags_z, flags_y = edges()
    z_kappa = received("gz", za_ref[KAP1], zb_ref[KAP1])
    z_phi = (zhalo_ref[0, 0], zhalo_ref[1, 0])
    yf = [yhalo_ref[side, :nz] for side in range(2)]
    first_ref[0] = start_ref[0]
    first_ref[nx - 1] = start_ref[nx - 1]
    for x in range(1, nx - 1):
        sides = [(start_ref[i], conduct_ref[i], None) for i in (x - 1, x + 1)]
        first_ref[x] = sweep_plane(
            x, start_ref[x], conduct_ref[x], start_ref[x] + src_ref[x], rea_ref[x],
            sides, z_phi, z_kappa, yf, yf, flags_z, flags_y,
        )

    lane = lane_of((nz, LANES))
    low = high = jnp.zeros((nz, LANES), F32)
    for x in range(nx):
        low = jnp.where(lane == x, roll_lanes(start_ref[x], x), low)
        high = jnp.where(lane == x, roll_lanes(start_ref[x], x + 1), high)
    own_ref[0] = low
    own_ref[1] = high


def sweeps_kernel(
    start_ref, conduct_ref, src_ref, rea_ref, zhalo_ref, yhalo_ref, own_ref,
    za_ref, zb_ref, sya_ref, syb_ref, xa_ref, xb_ref, first_ref,
    out_ref,
):
    nx, nz, _ = start_ref.shape
    flags_x, flags_z, flags_y = edges()
    start = [start_ref[x] for x in range(nx)]
    conduct = [conduct_ref[x] for x in range(nx)]
    base = 6 * nz

    def part(axis, a_ref, b_ref, begin, size):
        return received(axis, a_ref[begin : begin + size], b_ref[begin : begin + size])

    xf = [part("gx", xa_ref, xb_ref, f * nz, nz) for f in range(6)]
    xrows = part("gx", xa_ref, xb_ref, base, 8)
    xcols = part("gx", xa_ref, xb_ref, base + 8, nz)
    zf = [received("gz", za_ref[i], zb_ref[i]) for i in range(6)]
    yf = [yhalo_ref[side, :nz] for side in range(2)]
    yt = [yhalo_ref[side, nz : nz + nx] for side in range(2)]
    sf = sent("gy", sya_ref[:nz], syb_ref[:nz])

    def columns(tile, phi_spot, kappa_spot, lane):
        return roll_lanes(tile, lane - phi_spot), roll_lanes(tile, lane - kappa_spot)

    x_first_sweep = []
    for side in range(2):
        phi, kappa = xf[PHI1][side], xf[KAP1][side]
        me = 0 if side == 0 else nx - 1
        rows = xrows[side]
        sides = [(xf[PHI2][side], xf[KAP2][side], None), (start[me], conduct[me], None)]
        sides += along_rows(phi, kappa, (rows[0:1], rows[1:2]), (rows[2:3], rows[3:4]), flags_z)
        tile = xcols[side]
        sides += along_lanes(
            phi, kappa, columns(tile, 0, 1, 0), columns(tile, 2, 3, LANES - 1), flags_y
        )
        x_first_sweep.append(step(phi + xf[SRC][side], xf[REA][side], kappa, sides))

    z_first_sweep = []
    for side in range(2):
        phi, kappa = zhalo_ref[side, 0], zf[KAP1][side]
        me = 0 if side == 0 else nz - 1
        at = 2 * side
        sides = [
            (zhalo_ref[side, 1], zf[KAP2][side], None),
            (start_ref[:, me, :], conduct_ref[:, me, :], None),
        ]
        sides += along_rows(
            phi,
            kappa,
            (xrows[0][at : at + 1], xrows[0][at + 1 : at + 2]),
            (xrows[1][at : at + 1], xrows[1][at + 1 : at + 2]),
            flags_x,
        )
        sides += along_lanes(
            phi,
            kappa,
            columns(yt[0], at, at + 1, 0),
            columns(yt[1], at, at + 1, LANES - 1),
            flags_y,
        )
        z_first_sweep.append(step(phi + zf[SRC][side], zf[REA][side], kappa, sides))

    y_first_sweep = []
    for side in range(2):
        phi, phi2, kappa, kappa2, src, rea = [roll_lanes(yf[side], -f * nx) for f in range(6)]
        at = 2 * side
        sides = [(phi2, kappa2, None), (own_ref[side], roll_lanes(sf[side], -KAP1 * nx), None)]
        sides += along_rows(
            phi,
            kappa,
            (to_row(yt[side], 0), to_row(yt[side], 1)),
            (to_row(yt[side], 2), to_row(yt[side], 3)),
            flags_z,
        )
        sides += along_lanes(
            phi,
            kappa,
            columns(xcols[0], at, at + 1, 0),
            columns(xcols[1], at, at + 1, nx - 1),
            flags_x,
            nx - 1,
        )
        y_first_sweep.append(step(phi + src, rea, kappa, sides))

    def sweep(phis, x_phi, z_phi, y_phi, planes):
        below = [(x_phi[0], xf[KAP1][0], flags_x[0])] + [(phis[x], conduct[x], None) for x in range(nx - 1)]
        above = [(phis[x], conduct[x], None) for x in range(1, nx)] + [(x_phi[1], xf[KAP1][1], flags_x[1])]
        return [
            sweep_plane(
                x, phis[x], conduct[x], start[x] + src_ref[x], rea_ref[x],
                [below[x], above[x]], z_phi, zf[KAP1], y_phi, yf, flags_z, flags_y,
            )
            for x in planes
        ]

    ends = sweep(start, xf[PHI1], (zhalo_ref[0, 0], zhalo_ref[1, 0]), yf, (0, nx - 1))
    first = [ends[0]] + [first_ref[x] for x in range(1, nx - 1)] + [ends[1]]
    second = sweep(first, x_first_sweep, z_first_sweep, y_first_sweep, range(nx))
    for x in range(nx):
        out_ref[x] = second[x]


def swap(axis, first, second):
    count = lax.axis_size(axis)
    results = []
    for j, value in ((1, second), (0, first)):
        pairs = []
        for low in range(j, count - 1, 2):
            pairs += [(low, low + 1), (low + 1, low)]
        results.append(lax.ppermute(value, axis, pairs))
    return results[::-1]


def call(kernel, operands, outs, smem=0, hbm=(), scratch=()):
    specs = [SMEM] * smem + [VMEM] * (len(operands) - smem)
    operands = list(operands)
    for i in hbm:
        specs[i] = HBM
        operands[i] = pltpu.with_memory_space_constraint(operands[i], pltpu.HBM)
    return pl.pallas_call(
        kernel,
        out_shape=[jax.ShapeDtypeStruct(shape, F32) for shape in outs],
        in_specs=specs,
        out_specs=[VMEM] * len(outs),
        scratch_shapes=scratch,
        compiler_params=PARAMS,
    )(*operands)


def on_device(old_field, new_home, conduct, reaction, source, coarse):
    nx, nz, ny = block = old_field.shape
    home = new_home[0, 0]
    slots = home.shape[0]
    rows, width = nz // slots, ny // slots
    line = lax.axis_size("gy")
    part = nx // RUN

    sza, szb, parts = call(
        first_kernel,
        (new_home, old_field, conduct, source, reaction, coarse),
        [(7, nx, ny), (7, nx, ny), (RUN, part + 1, rows, ny)],
        hbm=(0, 1, 2, 3, 4, 5),
        scratch=[
            pltpu.SMEM(new_home.shape, jnp.int32),
            pltpu.VMEM(block, F32),
            pltpu.VMEM((3, 2, nx, 8, ny), F32),
            pltpu.VMEM(coarse.shape, F32),
            pltpu.SemaphoreType.DMA,
            pltpu.SemaphoreType.DMA((nx,)),
            pltpu.SemaphoreType.DMA((3, 2)),
            pltpu.SemaphoreType.DMA,
        ],
    )
    za, zb = swap("gz", sza, szb)
    groups = [[i * RUN + k for k in range(RUN)] for i in range(line // RUN)]
    parts = lax.all_to_all(parts, "gy", 0, 0, tiled=True, axis_index_groups=groups)

    def address(*refs):
        address_kernel(*refs, width=width)

    (send,) = call(address, (parts, za, zb), [(line, part + 2, rows, ny)])
    recv = lax.all_to_all(send, "gy", 0, 0, tiled=True)

    def columns(*refs):
        columns_kernel(*refs, width=width)

    sya, syb = call(
        columns, (sza, old_field, conduct, source, reaction, coarse, za, zb), [(nz + nx, ny)] * 2
    )
    ya, yb = swap("gy", sya, syb)
    src, rea = call(fold_kernel, (conduct, source, reaction, coarse, sya), [block, block])
    start, zhalo, yhalo = call(
        place_kernel,
        (home, recv, old_field, za, zb, ya, yb),
        [block, (2, 2, nx, ny), (2, nz + nx, ny)],
        smem=1,
    )
    xa, xb = call(
        edge_kernel,
        (start, conduct, src, rea, zhalo, yhalo, za, zb),
        [(7 * nz + 8, ny)] * 2,
    )
    first, own = call(
        inner_kernel,
        (start, conduct, src, rea, zhalo, yhalo, za, zb, xa),
        [block, (2, nz, ny)],
    )
    xa, xb = swap("gx", xa, xb)
    (relaxed,) = call(
        sweeps_kernel,
        (start, conduct, src, rea, zhalo, yhalo, own, za, zb, sya, syb, xa, xb, first),
        [block],
    )
    return relaxed


def solution(mesh):
    return jax.shard_map(
        on_device,
        mesh=mesh,
        in_specs=(P("gx", "gz", "gy"),) * 6,
        out_specs=P("gx", "gz", "gy"),
        check_vma=False,
    )
```

```python
import jax
import jax.numpy as jnp
from jax import lax
from jax.experimental import pallas as pl
from jax.experimental.pallas import tpu as pltpu
from jax.sharding import PartitionSpec as P

LANES = 128
RUN = 8
VMEM = pl.BlockSpec(memory_space=pltpu.VMEM)
SMEM = pl.BlockSpec(memory_space=pltpu.SMEM)
HBM = pl.BlockSpec(memory_space=pltpu.HBM)
PARAMS = pltpu.CompilerParams(vmem_limit_bytes=24 * 1024 * 1024)
F32 = jnp.float32

PHI1, PHI2, KAP1, KAP2, SRC, REA, RIM = range(7)


def lane_of(shape):
    return lax.broadcasted_iota(jnp.int32, shape, len(shape) - 1)


def row_of(shape):
    return lax.broadcasted_iota(jnp.int32, shape, len(shape) - 2)


def roll_lanes(value, shift):
    shift = shift % LANES
    return pltpu.roll(value, shift, value.ndim - 1) if shift else value


def roll_rows(value, shift):
    return pltpu.roll(value, shift % value.shape[0], 0)


def moved_slot(home_of, slots):
    position = lax.axis_index("gy")
    slot = jnp.int32(0)
    target = jnp.int32(0)
    for j in range(slots):
        home = home_of(j)
        leaves = home != position * slots + j
        slot = jnp.where(leaves, j, slot)
        target = jnp.where(leaves, home, target)
    return slot, target


def edges():
    flags = []
    for axis in ("gx", "gz", "gy"):
        index = lax.axis_index(axis)
        flags.append((index == 0, index == lax.axis_size(axis) - 1))
    return flags


def is_even(axis):
    return lax.rem(lax.axis_index(axis), 2) == 0


def write_pair(axis, first_ref, second_ref, index, low, high):
    even = is_even(axis)
    first_ref[index] = jnp.where(even, high, low)
    second_ref[index] = jnp.where(even, low, high)


def received(axis, first, second):
    even = is_even(axis)
    return jnp.where(even, second, first), jnp.where(even, first, second)


def sent(axis, first, second):
    even = is_even(axis)
    return jnp.where(even, second, first), jnp.where(even, first, second)


def doubler(count):
    half = lax.div(lax.broadcasted_iota(jnp.int32, (count, 2 * count), 1), 2)
    return (half == lax.broadcasted_iota(jnp.int32, (count, 2 * count), 0)).astype(F32)


def exact_dot(left, right):
    return jnp.dot(left, right, precision=lax.Precision.HIGHEST, preferred_element_type=F32)


def refine(coarse_ref):
    cx, cz, cy = coarse_ref.shape
    left, right = doubler(cz).T, doubler(cy)
    return [exact_dot(left, exact_dot(coarse_ref[x], right)) for x in range(cx)]


def first_kernel(
    home_hbm, old_hbm, conduct_hbm, source_hbm, reaction_hbm, coarse_hbm,
    za_ref, zb_ref, parts_hbm, parts_ref, home_ref, old_ref, rows_ref, coarse_ref,
    home_sem, old_sems, sems, coarse_sem, part_sems,
):
    slots = home_ref.shape[2]
    width = LANES // slots
    nx, nz, _ = old_hbm.shape
    size = rows_ref.shape[3]
    copies = [pltpu.make_async_copy(coarse_hbm, coarse_ref, coarse_sem)]
    loads = [pltpu.make_async_copy(old_hbm.at[x], old_ref.at[x], old_sems.at[x]) for x in range(nx)]
    for i, ref in enumerate((conduct_hbm, source_hbm, reaction_hbm)):
        for side, begin in enumerate((0, nz - size)):
            copies.append(
                pltpu.make_async_copy(
                    ref.at[:, pl.ds(begin, size), :], rows_ref.at[i, side], sems.at[i, side]
                )
            )
    load_home = pltpu.make_async_copy(home_hbm, home_ref, home_sem)
    for copy in [load_home] + loads + copies:
        copy.start()
    load_home.wait()

    slot, target = moved_slot(lambda j: home_ref[0, 0, j], slots)
    device = lax.div(target, slots)
    back = LANES - width * slot
    (x_first, x_last), (z_first, z_last), (y_first, y_last) = edges()
    row, lane = row_of((nx, LANES)), lane_of((nx, LANES))
    note = jnp.where(lane < 3 * width, device, slot).astype(F32)
    inner = (
        ((row == 0) & x_first).astype(F32)
        + ((row == nx - 1) & x_last).astype(F32)
        + ((lane == 0) & y_first).astype(F32)
        + ((lane == LANES - 1) & y_last).astype(F32)
    )
    rows = nz // slots
    planes = parts_ref.shape[1] - 1
    stores = []
    group = lax.div(lane_of((rows, LANES)), width)
    for x in range(nx):
        loads[x].wait()
        box = jnp.zeros((rows, LANES), F32)
        for g in range(slots):
            shift = lax.rem(width * (g - slot) + LANES, LANES)
            rolled = pltpu.roll(old_ref[x, g * rows : (g + 1) * rows, :], shift, 1)
            box = jnp.where(group == g, rolled, box)
        k = x // planes
        parts_ref[k, x % planes] = box
        if x % planes == planes - 1:
            parts_ref[k, planes] = jnp.full((rows, LANES), device, jnp.int32).astype(F32)
            stores.append(pltpu.make_async_copy(parts_ref.at[k], parts_hbm.at[k], part_sems.at[k]))
            stores[k].start()
    for copy in copies:
        copy.wait()
    cx, cz, cy = coarse_ref.shape
    ends = jnp.concatenate([coarse_ref[:, 0, :], coarse_ref[:, cz - 1, :]], axis=0)
    wide = exact_dot(ends, doubler(cy))

    def rims(first, second):
        near = pltpu.roll(first, lax.rem(back, LANES), 1)
        far = pltpu.roll(second, lax.rem(back + width, LANES), 1)
        return jnp.where(lane < width, near, jnp.where(lane < 2 * width, far, note))

    faces = []
    for side, first, second, edge in ((0, 0, 1, z_first), (1, size - 1, size - 2, z_last)):
        refined = jnp.zeros((nx, LANES), F32)
        for x in range(cx):
            refined = jnp.where(lax.div(row, 2) == x, wide[side * cx + x : side * cx + x + 1], refined)
        top = side * (nz - size)
        old, old2 = old_ref[:, top + first, :], old_ref[:, top + second, :]
        kappa, kappa2 = rows_ref[0, side, :, first, :], rows_ref[0, side, :, second, :]
        weight = (inner + jnp.where(edge, 1.0, 0.0)) * kappa
        src = rows_ref[1, side, :, first, :] + weight * refined
        rea = 1.0 + rows_ref[2, side, :, first, :] + weight
        faces.append([old, old2, kappa, kappa2, src, rea, rims(old, old2)])
    for i in range(7):
        write_pair("gz", za_ref, zb_ref, i, faces[0][i], faces[1][i])
    for store in stores:
        store.wait()


def columns_kernel(
    sent_ref, old_ref, conduct_ref, source_ref, reaction_ref, coarse_ref, za_ref, zb_ref,
    ya_ref, yb_ref, *, width,
):
    nx, nz, _ = conduct_ref.shape
    cx, cz, cy = coarse_ref.shape
    (x_first, x_last), (z_first, z_last), _ = edges()
    lane = lane_of((cz, LANES))
    ends = jnp.zeros((cz, LANES), F32)
    for x in range(cx):
        plane = coarse_ref[x]
        for side, at in ((0, 0), (1, cy - 1)):
            column = jnp.broadcast_to(plane[:, at : at + 1], (cz, LANES))
            ends = jnp.where(lax.div(lane, 2) == side * cx + x, column, ends)
    refined = exact_dot(doubler(cz).T, ends)

    row, lane = row_of((nz, LANES)), lane_of((nz, LANES))
    low = high = jnp.zeros((nz, LANES), F32)
    for f, (ref, depth) in enumerate(
        ((old_ref, 0), (old_ref, 1), (conduct_ref, 0), (conduct_ref, 1), (source_ref, 0), (reaction_ref, 0))
    ):
        for x in range(nx):
            spot = f * nx + x
            low = jnp.where(lane == spot, roll_lanes(ref[x], spot - depth), low)
            high = jnp.where(lane == spot, roll_lanes(ref[x], spot + 1 + depth), high)
    field, x_at = lax.div(lane, nx), lax.rem(lane, nx)
    outside = (
        ((row == 0) & z_first).astype(F32)
        + ((row == nz - 1) & z_last).astype(F32)
        + ((x_at == 0) & x_first).astype(F32)
        + ((x_at == nx - 1) & x_last).astype(F32)
    )

    def fold(tile, at):
        src = tile + outside * roll_lanes(tile, (SRC - KAP1) * nx) * roll_lanes(refined, SRC * nx - at)
        rea = 1.0 + tile + outside * roll_lanes(tile, (REA - KAP1) * nx)
        return jnp.where(field == SRC, src, jnp.where(field == REA, rea, tile))

    write_pair("gy", ya_ref, yb_ref, slice(0, nz), fold(low, 0), fold(high, nx))

    lane = lane_of((nx, LANES))
    spot = slice(3 * width, 3 * width + 1)
    own = jnp.broadcast_to(sent_ref[RIM][:, spot], (nx, LANES))
    low = high = jnp.where(lane == 4, own, 0.0)
    notes = received("gz", za_ref[RIM], zb_ref[RIM])
    for side in range(2):
        note = jnp.broadcast_to(notes[side][:, spot], (nx, LANES))
        low = jnp.where(lane == 5 + side, note, low)
        high = jnp.where(lane == 5 + side, note, high)
        for f, tile in enumerate((PHI1, KAP1)):
            value = received("gz", za_ref[tile], zb_ref[tile])[side]
            at = 2 * side + f
            low = jnp.where(lane == at, roll_lanes(value, at), low)
            high = jnp.where(lane == at, roll_lanes(value, at + 1), high)
    write_pair("gy", ya_ref, yb_ref, slice(nz, nz + nx), low, high)


def fold_kernel(conduct_ref, source_ref, reaction_ref, coarse_ref, after_ref, src_ref, rea_ref):
    del after_ref
    nx, nz, _ = conduct_ref.shape
    (x_first, x_last), (z_first, z_last), (y_first, y_last) = edges()
    refined = refine(coarse_ref)
    row, lane = row_of((nz, LANES)), lane_of((nz, LANES))
    inner = (
        ((row == 0) & z_first).astype(F32)
        + ((row == nz - 1) & z_last).astype(F32)
        + ((lane == 0) & y_first).astype(F32)
        + ((lane == LANES - 1) & y_last).astype(F32)
    )
    for x in range(nx):
        faces = inner
        if x == 0:
            faces = faces + jnp.where(x_first, 1.0, 0.0)
        if x == nx - 1:
            faces = faces + jnp.where(x_last, 1.0, 0.0)
        weight = faces * conduct_ref[x]
        src_ref[x] = source_ref[x] + weight * refined[x // 2]
        rea_ref[x] = 1.0 + reaction_ref[x] + weight


def address_kernel(parts_ref, za_ref, zb_ref, send_ref, *, width):
    planes = send_ref.shape[1] - 2
    low, high = received("gz", za_ref[RIM], zb_ref[RIM])
    shape = low.shape
    lane = lane_of(shape)
    low_tag = jnp.broadcast_to(low[:, 2 * width : 2 * width + 1], shape)
    high_tag = jnp.broadcast_to(high[:, 2 * width : 2 * width + 1], shape)
    high = roll_lanes(high, 2 * width)
    lower = lane < 2 * width
    rims = jnp.where(lower, low, high)
    tag = jnp.where(lower, low_tag, high_tag)
    column = lax.rem(lane, width)
    beside = jnp.where(column < 2, -1.0, jnp.where(column >= width - 2, 1.0, -4096.0))
    edge = jnp.where(column == 0, -1.0, jnp.where(column == width - 1, 1.0, -4096.0))
    count = parts_ref.shape[0]
    columns = [
        (roll_lanes(parts_ref[k, planes] + beside, 4 * i), roll_lanes(parts_ref[k, i], 4 * i))
        for k in range(count)
        for i in range(planes)
    ]
    columns.append((roll_lanes(tag + edge, 4 * planes), roll_lanes(rims, 4 * planes)))
    for device in range(send_ref.shape[0]):
        for i in range(planes):
            value = jnp.zeros(shape, F32)
            for k in range(count):
                value = jnp.where(parts_ref[k, planes] == device, parts_ref[k, i], value)
            send_ref[device, i] = value
        send_ref[device, planes] = jnp.where(tag == device, rims, 0.0)
        value = jnp.zeros(shape, F32)
        for spot, source in columns:
            value = jnp.where(spot == device, source, value)
        send_ref[device, planes + 1] = value


def spread(tile, offset, width):
    piece = jnp.where(lane_of(tile.shape) < width, roll_lanes(tile, -offset), 0.0)
    result = piece
    for shift in range(width, LANES, width):
        result = result + roll_lanes(piece, shift)
    return result


def place_kernel(
    home_ref, recv_ref, old_ref, za_ref, zb_ref, ya_ref, yb_ref,
    start_ref, zhalo_ref, yhalo_ref,
):
    slots = home_ref.shape[0]
    width = LANES // slots
    nx, nz, _ = old_ref.shape
    rows = nz // slots
    slot, _ = moved_slot(lambda j: home_ref[j], slots)
    planes = recv_ref.shape[1] - 2
    run = nx // planes
    count = recv_ref.shape[0]
    here = lax.div(lane_of((rows, LANES)), width) == slot

    def total(first, stride, tile):
        value = recv_ref[first, tile]
        for source in range(first + stride, count, stride):
            value = value + recv_ref[source, tile]
        return value

    for k in range(run):
        for i in range(planes):
            x = k * planes + i
            arrived = total(k, run, i)
            for g in range(slots):
                shift = lax.rem(width * (slot - g) + LANES, LANES)
                part = pl.ds(g * rows, rows)
                start_ref[x, part, :] = jnp.where(
                    here, pltpu.roll(arrived, shift, 1), old_ref[x, part, :]
                )

    rims = total(0, 1, planes)
    faces = [received("gz", za_ref[i], zb_ref[i]) for i in range(7)]
    group = lax.div(lane_of((nx, LANES)), width).astype(F32)
    for side in range(2):
        note = faces[RIM][side]
        there = jnp.broadcast_to(note[:, 3 * width : 3 * width + 1], note.shape) == group
        for depth in range(2):
            moved = spread(rims, (2 * side + depth) * width, width)
            zhalo_ref[side, depth] = jnp.where(there, moved, faces[depth][side])

    beside = [total(k, run, planes + 1) for k in range(run)]
    every = beside[0]
    for k in range(1, run):
        every = every + beside[k]
    lane = lane_of((rows, LANES))
    corner_lane = lane_of((nx, LANES))
    halos = received("gy", ya_ref[:nz], yb_ref[:nz])
    corners = received("gy", ya_ref[nz : nz + nx], yb_ref[nz : nz + nx])
    for side in range(2):
        outer = width - 1 if side == 0 else 0
        inward = -1 if side == 0 else 1
        touched = float(slots - 1 if side == 0 else 0)
        note = jnp.broadcast_to(corners[side][0:1, 4:5], (rows, LANES)) == touched
        for g in range(slots):
            value = jnp.zeros((rows, LANES), F32)
            for x in range(nx):
                source = beside[x // planes]
                for depth in range(2):
                    at = g * width + outer + inward * depth + 4 * (x % planes)
                    spot = depth * nx + x
                    value = jnp.where(lane == spot, roll_lanes(source, spot - at), value)
            held = halos[side][g * rows : (g + 1) * rows]
            yhalo_ref[side, g * rows : (g + 1) * rows] = jnp.where(
                note & (lane < 2 * nx), value, held
            )
        corner = corners[side]
        for z_side in range(2):
            note = jnp.broadcast_to(corner[:, 5 + z_side : 6 + z_side], (nx, LANES)) == touched
            at = 2 * width * z_side + outer + 4 * planes
            spot = 2 * z_side
            corner = jnp.where(
                note & (corner_lane == spot), roll_lanes(every, spot - at), corner
            )
        yhalo_ref[side, nz : nz + nx] = corner


def edge_kernel(
    start_ref, conduct_ref, src_ref, rea_ref, zhalo_ref, yhalo_ref, za_ref, zb_ref,
    xa_ref, xb_ref,
):
    nx, nz, _ = start_ref.shape
    for f, (ref, depth) in enumerate(
        ((start_ref, 0), (start_ref, 1), (conduct_ref, 0), (conduct_ref, 1), (src_ref, 0), (rea_ref, 0))
    ):
        write_pair(
            "gx", xa_ref, xb_ref, slice(f * nz, (f + 1) * nz), ref[depth], ref[nx - 1 - depth]
        )
    base = 6 * nz
    kappas = received("gz", za_ref[KAP1], zb_ref[KAP1])
    xa_ref[base : base + 8] = jnp.zeros((8, LANES), F32)
    xb_ref[base : base + 8] = jnp.zeros((8, LANES), F32)
    for side in range(2):
        for f, tile in enumerate((zhalo_ref[side, 0], kappas[side])):
            spot = base + 2 * side + f
            write_pair(
                "gx", xa_ref, xb_ref, slice(spot, spot + 1), tile[0:1], tile[nx - 1 : nx]
            )
    lane = lane_of((nz, LANES))
    low = high = jnp.zeros((nz, LANES), F32)
    for side in range(2):
        halo = yhalo_ref[side, :nz]
        for f, offset in enumerate((PHI1 * nx, KAP1 * nx)):
            spot = 2 * side + f
            low = jnp.where(lane == spot, roll_lanes(halo, spot - offset), low)
            high = jnp.where(lane == spot, roll_lanes(halo, spot - offset - nx + 1), high)
    write_pair("gx", xa_ref, xb_ref, slice(base + 8, base + 8 + nz), low, high)


def step(numerator, denominator, kappa, sides):
    for phi, beside, outside in sides:
        weight = 0.5 * (kappa + beside)
        if outside is not None:
            weight = jnp.where(outside, 0.0, weight)
        numerator = numerator + weight * phi
        denominator = denominator + weight
    return numerator / denominator


def along_rows(phi, kappa, low, high, flags):
    row = row_of(phi.shape)
    last = phi.shape[0] - 1
    low_edge, high_edge = row == 0, row == last
    return [
        (
            jnp.where(low_edge, low[0], roll_rows(phi, 1)),
            jnp.where(low_edge, low[1], roll_rows(kappa, 1)),
            low_edge & flags[0],
        ),
        (
            jnp.where(high_edge, high[0], roll_rows(phi, last)),
            jnp.where(high_edge, high[1], roll_rows(kappa, last)),
            high_edge & flags[1],
        ),
    ]


def along_lanes(phi, kappa, low, high, flags, last=LANES - 1):
    lane = lane_of(phi.shape)
    low_edge, high_edge = lane == 0, lane == last
    return [
        (
            jnp.where(low_edge, low[0], roll_lanes(phi, 1)),
            jnp.where(low_edge, low[1], roll_lanes(kappa, 1)),
            low_edge & flags[0],
        ),
        (
            jnp.where(high_edge, high[0], roll_lanes(phi, -1)),
            jnp.where(high_edge, high[1], roll_lanes(kappa, -1)),
            high_edge & flags[1],
        ),
    ]


def to_row(tile, spot):
    column = jnp.broadcast_to(tile[:, spot : spot + 1], tile.shape)
    return jnp.sum(
        jnp.where(lane_of(tile.shape) == row_of(tile.shape), column, 0.0), axis=0, keepdims=True
    )


def sweep_plane(x, phi, kappa, numerator, denominator, sides, z_phi, z_kappa, y_phi, y_kappa, flags_z, flags_y):
    sides = sides + along_rows(
        phi,
        kappa,
        (z_phi[0][x : x + 1], z_kappa[0][x : x + 1]),
        (z_phi[1][x : x + 1], z_kappa[1][x : x + 1]),
        flags_z,
    )
    spot = KAP1 * z_phi[0].shape[0] + x
    sides += along_lanes(
        phi,
        kappa,
        (roll_lanes(y_phi[0], -x), roll_lanes(y_kappa[0], -spot)),
        (roll_lanes(y_phi[1], LANES - 1 - x), roll_lanes(y_kappa[1], LANES - 1 - spot)),
        flags_y,
    )
    return step(numerator, denominator, kappa, sides)


def inner_kernel(
    start_ref, conduct_ref, src_ref, rea_ref, zhalo_ref, yhalo_ref, za_ref, zb_ref, after_ref,
    first_ref, own_ref,
):
    del after_ref
    nx, nz, _ = start_ref.shape
    _, flags_z, flags_y = edges()
    z_kappa = received("gz", za_ref[KAP1], zb_ref[KAP1])
    z_phi = (zhalo_ref[0, 0], zhalo_ref[1, 0])
    yf = [yhalo_ref[side, :nz] for side in range(2)]
    first_ref[0] = start_ref[0]
    first_ref[nx - 1] = start_ref[nx - 1]
    for x in range(1, nx - 1):
        sides = [(start_ref[i], conduct_ref[i], None) for i in (x - 1, x + 1)]
        first_ref[x] = sweep_plane(
            x, start_ref[x], conduct_ref[x], start_ref[x] + src_ref[x], rea_ref[x],
            sides, z_phi, z_kappa, yf, yf, flags_z, flags_y,
        )

    lane = lane_of((nz, LANES))
    low = high = jnp.zeros((nz, LANES), F32)
    for x in range(nx):
        low = jnp.where(lane == x, roll_lanes(start_ref[x], x), low)
        high = jnp.where(lane == x, roll_lanes(start_ref[x], x + 1), high)
    own_ref[0] = low
    own_ref[1] = high


def sweeps_kernel(
    start_ref, conduct_ref, src_ref, rea_ref, zhalo_ref, yhalo_ref, own_ref,
    za_ref, zb_ref, sya_ref, syb_ref, xa_ref, xb_ref, first_ref,
    out_ref,
):
    nx, nz, _ = start_ref.shape
    flags_x, flags_z, flags_y = edges()
    start = [start_ref[x] for x in range(nx)]
    conduct = [conduct_ref[x] for x in range(nx)]
    base = 6 * nz

    def part(axis, a_ref, b_ref, begin, size):
        return received(axis, a_ref[begin : begin + size], b_ref[begin : begin + size])

    xf = [part("gx", xa_ref, xb_ref, f * nz, nz) for f in range(6)]
    xrows = part("gx", xa_ref, xb_ref, base, 8)
    xcols = part("gx", xa_ref, xb_ref, base + 8, nz)
    zf = [received("gz", za_ref[i], zb_ref[i]) for i in range(6)]
    yf = [yhalo_ref[side, :nz] for side in range(2)]
    yt = [yhalo_ref[side, nz : nz + nx] for side in range(2)]
    sf = sent("gy", sya_ref[:nz], syb_ref[:nz])

    def columns(tile, phi_spot, kappa_spot, lane):
        return roll_lanes(tile, lane - phi_spot), roll_lanes(tile, lane - kappa_spot)

    x_first_sweep = []
    for side in range(2):
        phi, kappa = xf[PHI1][side], xf[KAP1][side]
        me = 0 if side == 0 else nx - 1
        rows = xrows[side]
        sides = [(xf[PHI2][side], xf[KAP2][side], None), (start[me], conduct[me], None)]
        sides += along_rows(phi, kappa, (rows[0:1], rows[1:2]), (rows[2:3], rows[3:4]), flags_z)
        tile = xcols[side]
        sides += along_lanes(
            phi, kappa, columns(tile, 0, 1, 0), columns(tile, 2, 3, LANES - 1), flags_y
        )
        x_first_sweep.append(step(phi + xf[SRC][side], xf[REA][side], kappa, sides))

    z_first_sweep = []
    for side in range(2):
        phi, kappa = zhalo_ref[side, 0], zf[KAP1][side]
        me = 0 if side == 0 else nz - 1
        at = 2 * side
        sides = [
            (zhalo_ref[side, 1], zf[KAP2][side], None),
            (start_ref[:, me, :], conduct_ref[:, me, :], None),
        ]
        sides += along_rows(
            phi,
            kappa,
            (xrows[0][at : at + 1], xrows[0][at + 1 : at + 2]),
            (xrows[1][at : at + 1], xrows[1][at + 1 : at + 2]),
            flags_x,
        )
        sides += along_lanes(
            phi,
            kappa,
            columns(yt[0], at, at + 1, 0),
            columns(yt[1], at, at + 1, LANES - 1),
            flags_y,
        )
        z_first_sweep.append(step(phi + zf[SRC][side], zf[REA][side], kappa, sides))

    y_first_sweep = []
    for side in range(2):
        phi, phi2, kappa, kappa2, src, rea = [roll_lanes(yf[side], -f * nx) for f in range(6)]
        at = 2 * side
        sides = [(phi2, kappa2, None), (own_ref[side], roll_lanes(sf[side], -KAP1 * nx), None)]
        sides += along_rows(
            phi,
            kappa,
            (to_row(yt[side], 0), to_row(yt[side], 1)),
            (to_row(yt[side], 2), to_row(yt[side], 3)),
            flags_z,
        )
        sides += along_lanes(
            phi,
            kappa,
            columns(xcols[0], at, at + 1, 0),
            columns(xcols[1], at, at + 1, nx - 1),
            flags_x,
            nx - 1,
        )
        y_first_sweep.append(step(phi + src, rea, kappa, sides))

    def sweep(phis, x_phi, z_phi, y_phi, planes):
        below = [(x_phi[0], xf[KAP1][0], flags_x[0])] + [(phis[x], conduct[x], None) for x in range(nx - 1)]
        above = [(phis[x], conduct[x], None) for x in range(1, nx)] + [(x_phi[1], xf[KAP1][1], flags_x[1])]
        return [
            sweep_plane(
                x, phis[x], conduct[x], start[x] + src_ref[x], rea_ref[x],
                [below[x], above[x]], z_phi, zf[KAP1], y_phi, yf, flags_z, flags_y,
            )
            for x in planes
        ]

    ends = sweep(start, xf[PHI1], (zhalo_ref[0, 0], zhalo_ref[1, 0]), yf, (0, nx - 1))
    first = [ends[0]] + [first_ref[x] for x in range(1, nx - 1)] + [ends[1]]
    second = sweep(first, x_first_sweep, z_first_sweep, y_first_sweep, range(nx))
    for x in range(nx):
        out_ref[x] = second[x]


def swap(axis, first, second):
    count = lax.axis_size(axis)
    results = []
    for j, value in ((1, second), (0, first)):
        pairs = []
        for low in range(j, count - 1, 2):
            pairs += [(low, low + 1), (low + 1, low)]
        results.append(lax.ppermute(value, axis, pairs))
    return results[::-1]


def call(kernel, operands, outs, smem=0, hbm=(), hbm_outs=(), scratch=()):
    specs = [SMEM] * smem + [VMEM] * (len(operands) - smem)
    operands = list(operands)
    for i in hbm:
        specs[i] = HBM
        operands[i] = pltpu.with_memory_space_constraint(operands[i], pltpu.HBM)
    return pl.pallas_call(
        kernel,
        out_shape=[jax.ShapeDtypeStruct(shape, F32) for shape in outs],
        in_specs=specs,
        out_specs=[HBM if i in hbm_outs else VMEM for i in range(len(outs))],
        scratch_shapes=scratch,
        compiler_params=PARAMS,
    )(*operands)


def on_device(old_field, new_home, conduct, reaction, source, coarse):
    nx, nz, ny = block = old_field.shape
    home = new_home[0, 0]
    slots = home.shape[0]
    rows, width = nz // slots, ny // slots
    line = lax.axis_size("gy")
    part = nx // RUN

    sza, szb, parts = call(
        first_kernel,
        (new_home, old_field, conduct, source, reaction, coarse),
        [(7, nx, ny), (7, nx, ny), (RUN, part + 1, rows, ny)],
        hbm=(0, 1, 2, 3, 4, 5),
        hbm_outs=(2,),
        scratch=[
            pltpu.VMEM((RUN, part + 1, rows, ny), F32),
            pltpu.SMEM(new_home.shape, jnp.int32),
            pltpu.VMEM(block, F32),
            pltpu.VMEM((3, 2, nx, 8, ny), F32),
            pltpu.VMEM(coarse.shape, F32),
            pltpu.SemaphoreType.DMA,
            pltpu.SemaphoreType.DMA((nx,)),
            pltpu.SemaphoreType.DMA((3, 2)),
            pltpu.SemaphoreType.DMA,
            pltpu.SemaphoreType.DMA((RUN,)),
        ],
    )
    za, zb = swap("gz", sza, szb)
    groups = [[i * RUN + k for k in range(RUN)] for i in range(line // RUN)]
    parts = lax.all_to_all(parts, "gy", 0, 0, tiled=True, axis_index_groups=groups)

    def address(*refs):
        address_kernel(*refs, width=width)

    (send,) = call(address, (parts, za, zb), [(line, part + 2, rows, ny)])
    recv = lax.all_to_all(send, "gy", 0, 0, tiled=True)

    def columns(*refs):
        columns_kernel(*refs, width=width)

    sya, syb = call(
        columns, (sza, old_field, conduct, source, reaction, coarse, za, zb), [(nz + nx, ny)] * 2
    )
    ya, yb = swap("gy", sya, syb)
    src, rea = call(fold_kernel, (conduct, source, reaction, coarse, sya), [block, block])
    start, zhalo, yhalo = call(
        place_kernel,
        (home, recv, old_field, za, zb, ya, yb),
        [block, (2, 2, nx, ny), (2, nz + nx, ny)],
        smem=1,
    )
    xa, xb = call(
        edge_kernel,
        (start, conduct, src, rea, zhalo, yhalo, za, zb),
        [(7 * nz + 8, ny)] * 2,
    )
    first, own = call(
        inner_kernel,
        (start, conduct, src, rea, zhalo, yhalo, za, zb, xa),
        [block, (2, nz, ny)],
    )
    xa, xb = swap("gx", xa, xb)
    (relaxed,) = call(
        sweeps_kernel,
        (start, conduct, src, rea, zhalo, yhalo, own, za, zb, sya, syb, xa, xb, first),
        [block],
    )
    return relaxed


def solution(mesh):
    return jax.shard_map(
        on_device,
        mesh=mesh,
        in_specs=(P("gx", "gz", "gy"),) * 6,
        out_specs=P("gx", "gz", "gy"),
        check_vma=False,
    )
```

```python
import jax
import jax.numpy as jnp
from jax import lax
from jax.experimental import pallas as pl
from jax.experimental.pallas import tpu as pltpu
from jax.sharding import PartitionSpec as P

LANES = 128
RUN = 8
VMEM = pl.BlockSpec(memory_space=pltpu.VMEM)
SMEM = pl.BlockSpec(memory_space=pltpu.SMEM)
HBM = pl.BlockSpec(memory_space=pltpu.HBM)
PARAMS = pltpu.CompilerParams(vmem_limit_bytes=24 * 1024 * 1024)
F32 = jnp.float32

PHI1, PHI2, KAP1, KAP2, SRC, REA, RIM = range(7)
XPHI, XKAP, XNUM, XDEN = range(4)


def lane_of(shape):
    return lax.broadcasted_iota(jnp.int32, shape, len(shape) - 1)


def row_of(shape):
    return lax.broadcasted_iota(jnp.int32, shape, len(shape) - 2)


def roll_lanes(value, shift):
    shift = shift % LANES
    return pltpu.roll(value, shift, value.ndim - 1) if shift else value


def roll_rows(value, shift):
    return pltpu.roll(value, shift % value.shape[0], 0)


def moved_slot(home_of, slots):
    position = lax.axis_index("gy")
    slot = jnp.int32(0)
    target = jnp.int32(0)
    for j in range(slots):
        home = home_of(j)
        leaves = home != position * slots + j
        slot = jnp.where(leaves, j, slot)
        target = jnp.where(leaves, home, target)
    return slot, target


def edges():
    flags = []
    for axis in ("gx", "gz", "gy"):
        index = lax.axis_index(axis)
        flags.append((index == 0, index == lax.axis_size(axis) - 1))
    return flags


def is_even(axis):
    return lax.rem(lax.axis_index(axis), 2) == 0


def write_pair(axis, first_ref, second_ref, index, low, high):
    even = is_even(axis)
    first_ref[index] = jnp.where(even, high, low)
    second_ref[index] = jnp.where(even, low, high)


def received(axis, first, second):
    even = is_even(axis)
    return jnp.where(even, second, first), jnp.where(even, first, second)


def sent(axis, first, second):
    even = is_even(axis)
    return jnp.where(even, second, first), jnp.where(even, first, second)


def doubler(count):
    half = lax.div(lax.broadcasted_iota(jnp.int32, (count, 2 * count), 1), 2)
    return (half == lax.broadcasted_iota(jnp.int32, (count, 2 * count), 0)).astype(F32)


def exact_dot(left, right):
    return jnp.dot(left, right, precision=lax.Precision.HIGHEST, preferred_element_type=F32)


def refine(coarse_ref):
    cx, cz, cy = coarse_ref.shape
    left, right = doubler(cz).T, doubler(cy)
    return [exact_dot(left, exact_dot(coarse_ref[x], right)) for x in range(cx)]


def first_kernel(
    home_hbm, old_hbm, conduct_hbm, source_hbm, reaction_hbm, coarse_hbm,
    za_ref, zb_ref, parts_hbm, parts_ref, home_ref, old_ref, rows_ref, coarse_ref,
    home_sem, old_sems, sems, coarse_sem, part_sems,
):
    slots = home_ref.shape[2]
    width = LANES // slots
    nx, nz, _ = old_hbm.shape
    size = rows_ref.shape[3]
    copies = [pltpu.make_async_copy(coarse_hbm, coarse_ref, coarse_sem)]
    loads = [pltpu.make_async_copy(old_hbm.at[x], old_ref.at[x], old_sems.at[x]) for x in range(nx)]
    for i, ref in enumerate((conduct_hbm, source_hbm, reaction_hbm)):
        for side, begin in enumerate((0, nz - size)):
            copies.append(
                pltpu.make_async_copy(
                    ref.at[:, pl.ds(begin, size), :], rows_ref.at[i, side], sems.at[i, side]
                )
            )
    load_home = pltpu.make_async_copy(home_hbm, home_ref, home_sem)
    for copy in [load_home] + loads + copies:
        copy.start()
    load_home.wait()

    slot, target = moved_slot(lambda j: home_ref[0, 0, j], slots)
    device = lax.div(target, slots)
    back = LANES - width * slot
    (x_first, x_last), (z_first, z_last), (y_first, y_last) = edges()
    row, lane = row_of((nx, LANES)), lane_of((nx, LANES))
    note = jnp.where(lane < 3 * width, device, slot).astype(F32)
    inner = (
        ((row == 0) & x_first).astype(F32)
        + ((row == nx - 1) & x_last).astype(F32)
        + ((lane == 0) & y_first).astype(F32)
        + ((lane == LANES - 1) & y_last).astype(F32)
    )
    rows = nz // slots
    planes = parts_ref.shape[1] - 1
    stores = []
    group = lax.div(lane_of((rows, LANES)), width)
    for x in range(nx):
        loads[x].wait()
        box = jnp.zeros((rows, LANES), F32)
        for g in range(slots):
            shift = lax.rem(width * (g - slot) + LANES, LANES)
            rolled = pltpu.roll(old_ref[x, g * rows : (g + 1) * rows, :], shift, 1)
            box = jnp.where(group == g, rolled, box)
        k = x // planes
        parts_ref[k, x % planes] = box
        if x % planes == planes - 1:
            parts_ref[k, planes] = jnp.full((rows, LANES), device, jnp.int32).astype(F32)
            stores.append(pltpu.make_async_copy(parts_ref.at[k], parts_hbm.at[k], part_sems.at[k]))
            stores[k].start()
    for copy in copies:
        copy.wait()
    cx, cz, cy = coarse_ref.shape
    ends = jnp.concatenate([coarse_ref[:, 0, :], coarse_ref[:, cz - 1, :]], axis=0)
    wide = exact_dot(ends, doubler(cy))

    def rims(first, second):
        near = pltpu.roll(first, lax.rem(back, LANES), 1)
        far = pltpu.roll(second, lax.rem(back + width, LANES), 1)
        return jnp.where(lane < width, near, jnp.where(lane < 2 * width, far, note))

    faces = []
    for side, first, second, edge in ((0, 0, 1, z_first), (1, size - 1, size - 2, z_last)):
        refined = jnp.zeros((nx, LANES), F32)
        for x in range(cx):
            refined = jnp.where(lax.div(row, 2) == x, wide[side * cx + x : side * cx + x + 1], refined)
        top = side * (nz - size)
        old, old2 = old_ref[:, top + first, :], old_ref[:, top + second, :]
        kappa, kappa2 = rows_ref[0, side, :, first, :], rows_ref[0, side, :, second, :]
        weight = (inner + jnp.where(edge, 1.0, 0.0)) * kappa
        src = rows_ref[1, side, :, first, :] + weight * refined
        rea = 1.0 + rows_ref[2, side, :, first, :] + weight
        faces.append([old, old2, kappa, kappa2, src, rea, rims(old, old2)])
    for i in range(7):
        write_pair("gz", za_ref, zb_ref, i, faces[0][i], faces[1][i])
    for store in stores:
        store.wait()


def columns_kernel(
    sent_ref, old_ref, conduct_ref, source_ref, reaction_ref, coarse_ref, za_ref, zb_ref,
    ya_ref, yb_ref, *, width,
):
    nx, nz, _ = conduct_ref.shape
    cx, cz, cy = coarse_ref.shape
    (x_first, x_last), (z_first, z_last), _ = edges()
    lane = lane_of((cz, LANES))
    ends = jnp.zeros((cz, LANES), F32)
    for x in range(cx):
        plane = coarse_ref[x]
        for side, at in ((0, 0), (1, cy - 1)):
            column = jnp.broadcast_to(plane[:, at : at + 1], (cz, LANES))
            ends = jnp.where(lax.div(lane, 2) == side * cx + x, column, ends)
    refined = exact_dot(doubler(cz).T, ends)

    row, lane = row_of((nz, LANES)), lane_of((nz, LANES))
    low = high = jnp.zeros((nz, LANES), F32)
    for f, (ref, depth) in enumerate(
        ((old_ref, 0), (old_ref, 1), (conduct_ref, 0), (conduct_ref, 1), (source_ref, 0), (reaction_ref, 0))
    ):
        for x in range(nx):
            spot = f * nx + x
            low = jnp.where(lane == spot, roll_lanes(ref[x], spot - depth), low)
            high = jnp.where(lane == spot, roll_lanes(ref[x], spot + 1 + depth), high)
    field, x_at = lax.div(lane, nx), lax.rem(lane, nx)
    outside = (
        ((row == 0) & z_first).astype(F32)
        + ((row == nz - 1) & z_last).astype(F32)
        + ((x_at == 0) & x_first).astype(F32)
        + ((x_at == nx - 1) & x_last).astype(F32)
    )

    def fold(tile, at):
        src = tile + outside * roll_lanes(tile, (SRC - KAP1) * nx) * roll_lanes(refined, SRC * nx - at)
        rea = 1.0 + tile + outside * roll_lanes(tile, (REA - KAP1) * nx)
        return jnp.where(field == SRC, src, jnp.where(field == REA, rea, tile))

    write_pair("gy", ya_ref, yb_ref, slice(0, nz), fold(low, 0), fold(high, nx))

    lane = lane_of((nx, LANES))
    spot = slice(3 * width, 3 * width + 1)
    own = jnp.broadcast_to(sent_ref[RIM][:, spot], (nx, LANES))
    low = high = jnp.where(lane == 4, own, 0.0)
    notes = received("gz", za_ref[RIM], zb_ref[RIM])
    for side in range(2):
        note = jnp.broadcast_to(notes[side][:, spot], (nx, LANES))
        low = jnp.where(lane == 5 + side, note, low)
        high = jnp.where(lane == 5 + side, note, high)
        for f, tile in enumerate((PHI1, KAP1)):
            value = received("gz", za_ref[tile], zb_ref[tile])[side]
            at = 2 * side + f
            low = jnp.where(lane == at, roll_lanes(value, at), low)
            high = jnp.where(lane == at, roll_lanes(value, at + 1), high)
    write_pair("gy", ya_ref, yb_ref, slice(nz, nz + nx), low, high)


def fold_kernel(conduct_ref, source_ref, reaction_ref, coarse_ref, after_ref, src_ref, rea_ref):
    del after_ref
    nx, nz, _ = conduct_ref.shape
    (x_first, x_last), (z_first, z_last), (y_first, y_last) = edges()
    refined = refine(coarse_ref)
    row, lane = row_of((nz, LANES)), lane_of((nz, LANES))
    inner = (
        ((row == 0) & z_first).astype(F32)
        + ((row == nz - 1) & z_last).astype(F32)
        + ((lane == 0) & y_first).astype(F32)
        + ((lane == LANES - 1) & y_last).astype(F32)
    )
    for x in range(nx):
        faces = inner
        if x == 0:
            faces = faces + jnp.where(x_first, 1.0, 0.0)
        if x == nx - 1:
            faces = faces + jnp.where(x_last, 1.0, 0.0)
        weight = faces * conduct_ref[x]
        src_ref[x] = source_ref[x] + weight * refined[x // 2]
        rea_ref[x] = 1.0 + reaction_ref[x] + weight


def address_kernel(parts_ref, za_ref, zb_ref, send_ref, *, width):
    planes = send_ref.shape[1] - 2
    low, high = received("gz", za_ref[RIM], zb_ref[RIM])
    shape = low.shape
    lane = lane_of(shape)
    low_tag = jnp.broadcast_to(low[:, 2 * width : 2 * width + 1], shape)
    high_tag = jnp.broadcast_to(high[:, 2 * width : 2 * width + 1], shape)
    high = roll_lanes(high, 2 * width)
    lower = lane < 2 * width
    rims = jnp.where(lower, low, high)
    tag = jnp.where(lower, low_tag, high_tag)
    column = lax.rem(lane, width)
    beside = jnp.where(column < 2, -1.0, jnp.where(column >= width - 2, 1.0, -4096.0))
    edge = jnp.where(column == 0, -1.0, jnp.where(column == width - 1, 1.0, -4096.0))
    count = parts_ref.shape[0]
    columns = [
        (roll_lanes(parts_ref[k, planes] + beside, 4 * i), roll_lanes(parts_ref[k, i], 4 * i))
        for k in range(count)
        for i in range(planes)
    ]
    columns.append((roll_lanes(tag + edge, 4 * planes), roll_lanes(rims, 4 * planes)))
    for device in range(send_ref.shape[0]):
        for i in range(planes):
            value = jnp.zeros(shape, F32)
            for k in range(count):
                value = jnp.where(parts_ref[k, planes] == device, parts_ref[k, i], value)
            send_ref[device, i] = value
        send_ref[device, planes] = jnp.where(tag == device, rims, 0.0)
        value = jnp.zeros(shape, F32)
        for spot, source in columns:
            value = jnp.where(spot == device, source, value)
        send_ref[device, planes + 1] = value


def spread(tile, offset, width):
    piece = jnp.where(lane_of(tile.shape) < width, roll_lanes(tile, -offset), 0.0)
    result = piece
    for shift in range(width, LANES, width):
        result = result + roll_lanes(piece, shift)
    return result


def place_kernel(
    home_ref, recv_ref, old_ref, za_ref, zb_ref, ya_ref, yb_ref,
    start_ref, zhalo_ref, yhalo_ref,
):
    slots = home_ref.shape[0]
    width = LANES // slots
    nx, nz, _ = old_ref.shape
    rows = nz // slots
    slot, _ = moved_slot(lambda j: home_ref[j], slots)
    planes = recv_ref.shape[1] - 2
    run = nx // planes
    count = recv_ref.shape[0]
    here = lax.div(lane_of((rows, LANES)), width) == slot

    def total(first, stride, tile):
        value = recv_ref[first, tile]
        for source in range(first + stride, count, stride):
            value = value + recv_ref[source, tile]
        return value

    for k in range(run):
        for i in range(planes):
            x = k * planes + i
            arrived = total(k, run, i)
            for g in range(slots):
                shift = lax.rem(width * (slot - g) + LANES, LANES)
                part = pl.ds(g * rows, rows)
                start_ref[x, part, :] = jnp.where(
                    here, pltpu.roll(arrived, shift, 1), old_ref[x, part, :]
                )

    rims = total(0, 1, planes)
    faces = [received("gz", za_ref[i], zb_ref[i]) for i in range(7)]
    group = lax.div(lane_of((nx, LANES)), width).astype(F32)
    for side in range(2):
        note = faces[RIM][side]
        there = jnp.broadcast_to(note[:, 3 * width : 3 * width + 1], note.shape) == group
        for depth in range(2):
            moved = spread(rims, (2 * side + depth) * width, width)
            zhalo_ref[side, depth] = jnp.where(there, moved, faces[depth][side])

    beside = [total(k, run, planes + 1) for k in range(run)]
    every = beside[0]
    for k in range(1, run):
        every = every + beside[k]
    lane = lane_of((rows, LANES))
    corner_lane = lane_of((nx, LANES))
    halos = received("gy", ya_ref[:nz], yb_ref[:nz])
    corners = received("gy", ya_ref[nz : nz + nx], yb_ref[nz : nz + nx])
    for side in range(2):
        outer = width - 1 if side == 0 else 0
        inward = -1 if side == 0 else 1
        touched = float(slots - 1 if side == 0 else 0)
        note = jnp.broadcast_to(corners[side][0:1, 4:5], (rows, LANES)) == touched
        for g in range(slots):
            value = jnp.zeros((rows, LANES), F32)
            for x in range(nx):
                source = beside[x // planes]
                for depth in range(2):
                    at = g * width + outer + inward * depth + 4 * (x % planes)
                    spot = depth * nx + x
                    value = jnp.where(lane == spot, roll_lanes(source, spot - at), value)
            held = halos[side][g * rows : (g + 1) * rows]
            yhalo_ref[side, g * rows : (g + 1) * rows] = jnp.where(
                note & (lane < 2 * nx), value, held
            )
        corner = corners[side]
        for z_side in range(2):
            note = jnp.broadcast_to(corner[:, 5 + z_side : 6 + z_side], (nx, LANES)) == touched
            at = 2 * width * z_side + outer + 4 * planes
            spot = 2 * z_side
            corner = jnp.where(
                note & (corner_lane == spot), roll_lanes(every, spot - at), corner
            )
        yhalo_ref[side, nz : nz + nx] = corner


def edge_kernel(
    start_ref, conduct_ref, src_ref, rea_ref, zhalo_ref, yhalo_ref, za_ref, zb_ref,
    xa_ref, xb_ref,
):
    nx, nz, _ = start_ref.shape
    _, flags_z, flags_y = edges()
    z_kappa = received("gz", za_ref[KAP1], zb_ref[KAP1])
    z_phi = (zhalo_ref[0, 0], zhalo_ref[1, 0])
    yf = [yhalo_ref[side, :nz] for side in range(2)]
    faces = []
    for me, inner in ((0, 1), (nx - 1, nx - 2)):
        sides = plane_sides(
            me, start_ref[me], conduct_ref[me], [(start_ref[inner], conduct_ref[inner], None)],
            z_phi, z_kappa, yf, yf, flags_z, flags_y,
        )
        sums = gather(start_ref[me] + src_ref[me], rea_ref[me], conduct_ref[me], sides)
        faces.append((start_ref[me], conduct_ref[me], *sums))
    for f in range(4):
        write_pair("gx", xa_ref, xb_ref, slice(f * nz, (f + 1) * nz), faces[0][f], faces[1][f])
    base = 4 * nz
    kappas = received("gz", za_ref[KAP1], zb_ref[KAP1])
    xa_ref[base : base + 8] = jnp.zeros((8, LANES), F32)
    xb_ref[base : base + 8] = jnp.zeros((8, LANES), F32)
    for side in range(2):
        for f, tile in enumerate((zhalo_ref[side, 0], kappas[side])):
            spot = base + 2 * side + f
            write_pair(
                "gx", xa_ref, xb_ref, slice(spot, spot + 1), tile[0:1], tile[nx - 1 : nx]
            )
    lane = lane_of((nz, LANES))
    low = high = jnp.zeros((nz, LANES), F32)
    for side in range(2):
        halo = yhalo_ref[side, :nz]
        for f, offset in enumerate((PHI1 * nx, KAP1 * nx)):
            spot = 2 * side + f
            low = jnp.where(lane == spot, roll_lanes(halo, spot - offset), low)
            high = jnp.where(lane == spot, roll_lanes(halo, spot - offset - nx + 1), high)
    write_pair("gx", xa_ref, xb_ref, slice(base + 8, base + 8 + nz), low, high)


def gather(numerator, denominator, kappa, sides):
    for phi, beside, outside in sides:
        weight = 0.5 * (kappa + beside)
        if outside is not None:
            weight = jnp.where(outside, 0.0, weight)
        numerator = numerator + weight * phi
        denominator = denominator + weight
    return numerator, denominator


def step(numerator, denominator, kappa, sides):
    numerator, denominator = gather(numerator, denominator, kappa, sides)
    return numerator / denominator


def along_rows(phi, kappa, low, high, flags):
    row = row_of(phi.shape)
    last = phi.shape[0] - 1
    low_edge, high_edge = row == 0, row == last
    return [
        (
            jnp.where(low_edge, low[0], roll_rows(phi, 1)),
            jnp.where(low_edge, low[1], roll_rows(kappa, 1)),
            low_edge & flags[0],
        ),
        (
            jnp.where(high_edge, high[0], roll_rows(phi, last)),
            jnp.where(high_edge, high[1], roll_rows(kappa, last)),
            high_edge & flags[1],
        ),
    ]


def along_lanes(phi, kappa, low, high, flags, last=LANES - 1):
    lane = lane_of(phi.shape)
    low_edge, high_edge = lane == 0, lane == last
    return [
        (
            jnp.where(low_edge, low[0], roll_lanes(phi, 1)),
            jnp.where(low_edge, low[1], roll_lanes(kappa, 1)),
            low_edge & flags[0],
        ),
        (
            jnp.where(high_edge, high[0], roll_lanes(phi, -1)),
            jnp.where(high_edge, high[1], roll_lanes(kappa, -1)),
            high_edge & flags[1],
        ),
    ]


def to_row(tile, spot):
    column = jnp.broadcast_to(tile[:, spot : spot + 1], tile.shape)
    return jnp.sum(
        jnp.where(lane_of(tile.shape) == row_of(tile.shape), column, 0.0), axis=0, keepdims=True
    )


def plane_sides(x, phi, kappa, sides, z_phi, z_kappa, y_phi, y_kappa, flags_z, flags_y):
    sides = sides + along_rows(
        phi,
        kappa,
        (z_phi[0][x : x + 1], z_kappa[0][x : x + 1]),
        (z_phi[1][x : x + 1], z_kappa[1][x : x + 1]),
        flags_z,
    )
    spot = KAP1 * z_phi[0].shape[0] + x
    sides += along_lanes(
        phi,
        kappa,
        (roll_lanes(y_phi[0], -x), roll_lanes(y_kappa[0], -spot)),
        (roll_lanes(y_phi[1], LANES - 1 - x), roll_lanes(y_kappa[1], LANES - 1 - spot)),
        flags_y,
    )
    return sides


def inner_kernel(
    start_ref, conduct_ref, src_ref, rea_ref, zhalo_ref, yhalo_ref, za_ref, zb_ref, after_ref,
    first_ref, own_ref,
):
    del after_ref
    nx, nz, _ = start_ref.shape
    _, flags_z, flags_y = edges()
    z_kappa = received("gz", za_ref[KAP1], zb_ref[KAP1])
    z_phi = (zhalo_ref[0, 0], zhalo_ref[1, 0])
    yf = [yhalo_ref[side, :nz] for side in range(2)]
    first_ref[0] = start_ref[0]
    first_ref[nx - 1] = start_ref[nx - 1]
    for x in range(1, nx - 1):
        sides = [(start_ref[i], conduct_ref[i], None) for i in (x - 1, x + 1)]
        sides = plane_sides(
            x, start_ref[x], conduct_ref[x], sides, z_phi, z_kappa, yf, yf, flags_z, flags_y
        )
        first_ref[x] = step(start_ref[x] + src_ref[x], rea_ref[x], conduct_ref[x], sides)

    lane = lane_of((nz, LANES))
    low = high = jnp.zeros((nz, LANES), F32)
    for x in range(nx):
        low = jnp.where(lane == x, roll_lanes(start_ref[x], x), low)
        high = jnp.where(lane == x, roll_lanes(start_ref[x], x + 1), high)
    own_ref[0] = low
    own_ref[1] = high


def sweeps_kernel(
    start_ref, conduct_ref, src_ref, rea_ref, zhalo_ref, yhalo_ref, own_ref,
    za_ref, zb_ref, sya_ref, syb_ref, sxa_ref, sxb_ref, xa_ref, xb_ref, first_ref,
    out_ref,
):
    nx, nz, _ = start_ref.shape
    flags_x, flags_z, flags_y = edges()
    start = [start_ref[x] for x in range(nx)]
    conduct = [conduct_ref[x] for x in range(nx)]
    base = 4 * nz

    def part(axis, a_ref, b_ref, begin, size):
        return received(axis, a_ref[begin : begin + size], b_ref[begin : begin + size])

    xf = [part("gx", xa_ref, xb_ref, f * nz, nz) for f in range(4)]
    num, den = [
        sent("gx", sxa_ref[f * nz : (f + 1) * nz], sxb_ref[f * nz : (f + 1) * nz]) for f in (XNUM, XDEN)
    ]
    xrows = part("gx", xa_ref, xb_ref, base, 8)
    xcols = part("gx", xa_ref, xb_ref, base + 8, nz)
    zf = [received("gz", za_ref[i], zb_ref[i]) for i in range(6)]
    yf = [yhalo_ref[side, :nz] for side in range(2)]
    yt = [yhalo_ref[side, nz : nz + nx] for side in range(2)]
    sf = sent("gy", sya_ref[:nz], syb_ref[:nz])

    def columns(tile, phi_spot, kappa_spot, lane):
        return roll_lanes(tile, lane - phi_spot), roll_lanes(tile, lane - kappa_spot)

    x_first_sweep, ends = [], []
    for side, me in ((0, 0), (1, nx - 1)):
        kappa = xf[XKAP][side]
        sides = [(start[me], conduct[me], None)]
        x_first_sweep.append(step(xf[XNUM][side], xf[XDEN][side], kappa, sides))
        sides = [(xf[XPHI][side], kappa, flags_x[side])]
        ends.append(step(num[side], den[side], conduct[me], sides))

    z_first_sweep = []
    for side in range(2):
        phi, kappa = zhalo_ref[side, 0], zf[KAP1][side]
        me = 0 if side == 0 else nz - 1
        at = 2 * side
        sides = [
            (zhalo_ref[side, 1], zf[KAP2][side], None),
            (start_ref[:, me, :], conduct_ref[:, me, :], None),
        ]
        sides += along_rows(
            phi,
            kappa,
            (xrows[0][at : at + 1], xrows[0][at + 1 : at + 2]),
            (xrows[1][at : at + 1], xrows[1][at + 1 : at + 2]),
            flags_x,
        )
        sides += along_lanes(
            phi,
            kappa,
            columns(yt[0], at, at + 1, 0),
            columns(yt[1], at, at + 1, LANES - 1),
            flags_y,
        )
        z_first_sweep.append(step(phi + zf[SRC][side], zf[REA][side], kappa, sides))

    y_first_sweep = []
    for side in range(2):
        phi, phi2, kappa, kappa2, src, rea = [roll_lanes(yf[side], -f * nx) for f in range(6)]
        at = 2 * side
        sides = [(phi2, kappa2, None), (own_ref[side], roll_lanes(sf[side], -KAP1 * nx), None)]
        sides += along_rows(
            phi,
            kappa,
            (to_row(yt[side], 0), to_row(yt[side], 1)),
            (to_row(yt[side], 2), to_row(yt[side], 3)),
            flags_z,
        )
        sides += along_lanes(
            phi,
            kappa,
            columns(xcols[0], at, at + 1, 0),
            columns(xcols[1], at, at + 1, nx - 1),
            flags_x,
            nx - 1,
        )
        y_first_sweep.append(step(phi + src, rea, kappa, sides))

    first = [ends[0]] + [first_ref[x] for x in range(1, nx - 1)] + [ends[1]]
    for x in range(nx):
        below = (first[x - 1], conduct[x - 1], None)
        if x == 0:
            below = (x_first_sweep[0], xf[XKAP][0], flags_x[0])
        if x == nx - 1:
            above = (x_first_sweep[1], xf[XKAP][1], flags_x[1])
        else:
            above = (first[x + 1], conduct[x + 1], None)
        sides = plane_sides(
            x, first[x], conduct[x], [below, above],
            z_first_sweep, zf[KAP1], y_first_sweep, yf, flags_z, flags_y,
        )
        out_ref[x] = step(start[x] + src_ref[x], rea_ref[x], conduct[x], sides)


def swap(axis, first, second):
    count = lax.axis_size(axis)
    results = []
    for j, value in ((1, second), (0, first)):
        pairs = []
        for low in range(j, count - 1, 2):
            pairs += [(low, low + 1), (low + 1, low)]
        results.append(lax.ppermute(value, axis, pairs))
    return results[::-1]


def call(kernel, operands, outs, smem=0, hbm=(), hbm_outs=(), scratch=()):
    specs = [SMEM] * smem + [VMEM] * (len(operands) - smem)
    operands = list(operands)
    for i in hbm:
        specs[i] = HBM
        operands[i] = pltpu.with_memory_space_constraint(operands[i], pltpu.HBM)
    return pl.pallas_call(
        kernel,
        out_shape=[jax.ShapeDtypeStruct(shape, F32) for shape in outs],
        in_specs=specs,
        out_specs=[HBM if i in hbm_outs else VMEM for i in range(len(outs))],
        scratch_shapes=scratch,
        compiler_params=PARAMS,
    )(*operands)


def on_device(old_field, new_home, conduct, reaction, source, coarse):
    nx, nz, ny = block = old_field.shape
    home = new_home[0, 0]
    slots = home.shape[0]
    rows, width = nz // slots, ny // slots
    line = lax.axis_size("gy")
    part = nx // RUN

    sza, szb, parts = call(
        first_kernel,
        (new_home, old_field, conduct, source, reaction, coarse),
        [(7, nx, ny), (7, nx, ny), (RUN, part + 1, rows, ny)],
        hbm=(0, 1, 2, 3, 4, 5),
        hbm_outs=(2,),
        scratch=[
            pltpu.VMEM((RUN, part + 1, rows, ny), F32),
            pltpu.SMEM(new_home.shape, jnp.int32),
            pltpu.VMEM(block, F32),
            pltpu.VMEM((3, 2, nx, 8, ny), F32),
            pltpu.VMEM(coarse.shape, F32),
            pltpu.SemaphoreType.DMA,
            pltpu.SemaphoreType.DMA((nx,)),
            pltpu.SemaphoreType.DMA((3, 2)),
            pltpu.SemaphoreType.DMA,
            pltpu.SemaphoreType.DMA((RUN,)),
        ],
    )
    za, zb = swap("gz", sza, szb)
    groups = [[i * RUN + k for k in range(RUN)] for i in range(line // RUN)]
    parts = lax.all_to_all(parts, "gy", 0, 0, tiled=True, axis_index_groups=groups)

    def address(*refs):
        address_kernel(*refs, width=width)

    (send,) = call(address, (parts, za, zb), [(line, part + 2, rows, ny)])
    recv = lax.all_to_all(send, "gy", 0, 0, tiled=True)

    def columns(*refs):
        columns_kernel(*refs, width=width)

    sya, syb = call(
        columns, (sza, old_field, conduct, source, reaction, coarse, za, zb), [(nz + nx, ny)] * 2
    )
    ya, yb = swap("gy", sya, syb)
    src, rea = call(fold_kernel, (conduct, source, reaction, coarse, sya), [block, block])
    start, zhalo, yhalo = call(
        place_kernel,
        (home, recv, old_field, za, zb, ya, yb),
        [block, (2, 2, nx, ny), (2, nz + nx, ny)],
        smem=1,
    )
    sxa, sxb = call(
        edge_kernel,
        (start, conduct, src, rea, zhalo, yhalo, za, zb),
        [(5 * nz + 8, ny)] * 2,
    )
    first, own = call(
        inner_kernel,
        (start, conduct, src, rea, zhalo, yhalo, za, zb, sxa),
        [block, (2, nz, ny)],
    )
    xa, xb = swap("gx", sxa, sxb)
    (relaxed,) = call(
        sweeps_kernel,
        (start, conduct, src, rea, zhalo, yhalo, own, za, zb, sya, syb, sxa, sxb, xa, xb, first),
        [block],
    )
    return relaxed


def solution(mesh):
    return jax.shard_map(
        on_device,
        mesh=mesh,
        in_specs=(P("gx", "gz", "gy"),) * 6,
        out_specs=P("gx", "gz", "gy"),
        check_vma=False,
    )
```

```python
import jax
import jax.numpy as jnp
from jax import lax
from jax.experimental import pallas as pl
from jax.experimental.pallas import tpu as pltpu
from jax.sharding import PartitionSpec as P

LANES = 128
RUN = 8
VMEM = pl.BlockSpec(memory_space=pltpu.VMEM)
SMEM = pl.BlockSpec(memory_space=pltpu.SMEM)
HBM = pl.BlockSpec(memory_space=pltpu.HBM)
PARAMS = pltpu.CompilerParams(vmem_limit_bytes=24 * 1024 * 1024)
F32 = jnp.float32

PHI1, PHI2, KAP1, KAP2, SRC, REA, RIM = range(7)
XPHI, XKAP, XNUM, XDEN = range(4)


def lane_of(shape):
    return lax.broadcasted_iota(jnp.int32, shape, len(shape) - 1)


def row_of(shape):
    return lax.broadcasted_iota(jnp.int32, shape, len(shape) - 2)


def roll_lanes(value, shift):
    shift = shift % LANES
    return pltpu.roll(value, shift, value.ndim - 1) if shift else value


def roll_rows(value, shift):
    return pltpu.roll(value, shift % value.shape[0], 0)


def moved_slot(home_of, slots):
    position = lax.axis_index("gy")
    slot = jnp.int32(0)
    target = jnp.int32(0)
    for j in range(slots):
        home = home_of(j)
        leaves = home != position * slots + j
        slot = jnp.where(leaves, j, slot)
        target = jnp.where(leaves, home, target)
    return slot, target


def edges():
    flags = []
    for axis in ("gx", "gz", "gy"):
        index = lax.axis_index(axis)
        flags.append((index == 0, index == lax.axis_size(axis) - 1))
    return flags


def is_even(axis):
    return lax.rem(lax.axis_index(axis), 2) == 0


def write_pair(axis, first_ref, second_ref, index, low, high):
    even = is_even(axis)
    first_ref[index] = jnp.where(even, high, low)
    second_ref[index] = jnp.where(even, low, high)


def received(axis, first, second):
    even = is_even(axis)
    return jnp.where(even, second, first), jnp.where(even, first, second)


def sent(axis, first, second):
    even = is_even(axis)
    return jnp.where(even, second, first), jnp.where(even, first, second)


def doubler(count):
    half = lax.div(lax.broadcasted_iota(jnp.int32, (count, 2 * count), 1), 2)
    return (half == lax.broadcasted_iota(jnp.int32, (count, 2 * count), 0)).astype(F32)


def exact_dot(left, right):
    return jnp.dot(left, right, precision=lax.Precision.HIGHEST, preferred_element_type=F32)


def refine(coarse_ref):
    cx, cz, cy = coarse_ref.shape
    left, right = doubler(cz).T, doubler(cy)
    return [exact_dot(left, exact_dot(coarse_ref[x], right)) for x in range(cx)]


def first_kernel(
    home_hbm, old_hbm, conduct_hbm, source_hbm, reaction_hbm, coarse_hbm,
    za_ref, zb_ref, parts_hbm, parts_ref, home_ref, old_ref, rows_ref, coarse_ref,
    home_sem, old_sems, sems, coarse_sem, part_sems,
):
    slots = home_ref.shape[2]
    width = LANES // slots
    nx, nz, _ = old_hbm.shape
    size = rows_ref.shape[3]
    copies = [pltpu.make_async_copy(coarse_hbm, coarse_ref, coarse_sem)]
    loads = [pltpu.make_async_copy(old_hbm.at[x], old_ref.at[x], old_sems.at[x]) for x in range(nx)]
    for i, ref in enumerate((conduct_hbm, source_hbm, reaction_hbm)):
        for side, begin in enumerate((0, nz - size)):
            copies.append(
                pltpu.make_async_copy(
                    ref.at[:, pl.ds(begin, size), :], rows_ref.at[i, side], sems.at[i, side]
                )
            )
    load_home = pltpu.make_async_copy(home_hbm, home_ref, home_sem)
    for copy in [load_home] + loads + copies:
        copy.start()
    load_home.wait()

    slot, target = moved_slot(lambda j: home_ref[0, 0, j], slots)
    device = lax.div(target, slots)
    back = LANES - width * slot
    (x_first, x_last), (z_first, z_last), (y_first, y_last) = edges()
    row, lane = row_of((nx, LANES)), lane_of((nx, LANES))
    note = jnp.where(lane < 3 * width, device, slot).astype(F32)
    inner = (
        ((row == 0) & x_first).astype(F32)
        + ((row == nx - 1) & x_last).astype(F32)
        + ((lane == 0) & y_first).astype(F32)
        + ((lane == LANES - 1) & y_last).astype(F32)
    )
    rows = nz // slots
    planes = parts_ref.shape[1] - 1
    stores = []
    group = lax.div(lane_of((rows, LANES)), width)
    for x in range(nx):
        loads[x].wait()
        box = jnp.zeros((rows, LANES), F32)
        for g in range(slots):
            shift = lax.rem(width * (g - slot) + LANES, LANES)
            rolled = pltpu.roll(old_ref[x, g * rows : (g + 1) * rows, :], shift, 1)
            box = jnp.where(group == g, rolled, box)
        k = x // planes
        parts_ref[k, x % planes] = box
        if x % planes == planes - 1:
            parts_ref[k, planes] = jnp.full((rows, LANES), device, jnp.int32).astype(F32)
            stores.append(pltpu.make_async_copy(parts_ref.at[k], parts_hbm.at[k], part_sems.at[k]))
            stores[k].start()
    for copy in copies:
        copy.wait()
    cx, cz, cy = coarse_ref.shape
    ends = jnp.concatenate([coarse_ref[:, 0, :], coarse_ref[:, cz - 1, :]], axis=0)
    wide = exact_dot(ends, doubler(cy))

    def rims(first, second):
        near = pltpu.roll(first, lax.rem(back, LANES), 1)
        far = pltpu.roll(second, lax.rem(back + width, LANES), 1)
        return jnp.where(lane < width, near, jnp.where(lane < 2 * width, far, note))

    faces = []
    for side, first, second, edge in ((0, 0, 1, z_first), (1, size - 1, size - 2, z_last)):
        refined = jnp.zeros((nx, LANES), F32)
        for x in range(cx):
            refined = jnp.where(lax.div(row, 2) == x, wide[side * cx + x : side * cx + x + 1], refined)
        top = side * (nz - size)
        old, old2 = old_ref[:, top + first, :], old_ref[:, top + second, :]
        kappa, kappa2 = rows_ref[0, side, :, first, :], rows_ref[0, side, :, second, :]
        weight = (inner + jnp.where(edge, 1.0, 0.0)) * kappa
        src = rows_ref[1, side, :, first, :] + weight * refined
        rea = 1.0 + rows_ref[2, side, :, first, :] + weight
        faces.append([old, old2, kappa, kappa2, src, rea, rims(old, old2)])
    for i in range(7):
        write_pair("gz", za_ref, zb_ref, i, faces[0][i], faces[1][i])
    for store in stores:
        store.wait()


def columns_kernel(
    sent_ref, old_ref, conduct_ref, source_ref, reaction_ref, coarse_ref, za_ref, zb_ref,
    ya_ref, yb_ref, *, width,
):
    nx, nz, _ = conduct_ref.shape
    cx, cz, cy = coarse_ref.shape
    (x_first, x_last), (z_first, z_last), _ = edges()
    lane = lane_of((cz, LANES))
    ends = jnp.zeros((cz, LANES), F32)
    for x in range(cx):
        plane = coarse_ref[x]
        for side, at in ((0, 0), (1, cy - 1)):
            column = jnp.broadcast_to(plane[:, at : at + 1], (cz, LANES))
            ends = jnp.where(lax.div(lane, 2) == side * cx + x, column, ends)
    refined = exact_dot(doubler(cz).T, ends)

    row, lane = row_of((nz, LANES)), lane_of((nz, LANES))
    low = high = jnp.zeros((nz, LANES), F32)
    for f, (ref, depth) in enumerate(
        ((old_ref, 0), (old_ref, 1), (conduct_ref, 0), (conduct_ref, 1), (source_ref, 0), (reaction_ref, 0))
    ):
        for x in range(nx):
            spot = f * nx + x
            low = jnp.where(lane == spot, roll_lanes(ref[x], spot - depth), low)
            high = jnp.where(lane == spot, roll_lanes(ref[x], spot + 1 + depth), high)
    field, x_at = lax.div(lane, nx), lax.rem(lane, nx)
    outside = (
        ((row == 0) & z_first).astype(F32)
        + ((row == nz - 1) & z_last).astype(F32)
        + ((x_at == 0) & x_first).astype(F32)
        + ((x_at == nx - 1) & x_last).astype(F32)
    )

    def fold(tile, at):
        src = tile + outside * roll_lanes(tile, (SRC - KAP1) * nx) * roll_lanes(refined, SRC * nx - at)
        rea = 1.0 + tile + outside * roll_lanes(tile, (REA - KAP1) * nx)
        return jnp.where(field == SRC, src, jnp.where(field == REA, rea, tile))

    write_pair("gy", ya_ref, yb_ref, slice(0, nz), fold(low, 0), fold(high, nx))

    lane = lane_of((nx, LANES))
    spot = slice(3 * width, 3 * width + 1)
    own = jnp.broadcast_to(sent_ref[RIM][:, spot], (nx, LANES))
    low = high = jnp.where(lane == 4, own, 0.0)
    notes = received("gz", za_ref[RIM], zb_ref[RIM])
    for side in range(2):
        note = jnp.broadcast_to(notes[side][:, spot], (nx, LANES))
        low = jnp.where(lane == 5 + side, note, low)
        high = jnp.where(lane == 5 + side, note, high)
        for f, tile in enumerate((PHI1, KAP1)):
            value = received("gz", za_ref[tile], zb_ref[tile])[side]
            at = 2 * side + f
            low = jnp.where(lane == at, roll_lanes(value, at), low)
            high = jnp.where(lane == at, roll_lanes(value, at + 1), high)
    write_pair("gy", ya_ref, yb_ref, slice(nz, nz + nx), low, high)


def fold_kernel(conduct_ref, source_ref, reaction_ref, coarse_ref, after_ref, src_ref, rea_ref):
    del after_ref
    nx, nz, _ = conduct_ref.shape
    (x_first, x_last), (z_first, z_last), (y_first, y_last) = edges()
    refined = refine(coarse_ref)
    row, lane = row_of((nz, LANES)), lane_of((nz, LANES))
    inner = (
        ((row == 0) & z_first).astype(F32)
        + ((row == nz - 1) & z_last).astype(F32)
        + ((lane == 0) & y_first).astype(F32)
        + ((lane == LANES - 1) & y_last).astype(F32)
    )
    for x in range(nx):
        faces = inner
        if x == 0:
            faces = faces + jnp.where(x_first, 1.0, 0.0)
        if x == nx - 1:
            faces = faces + jnp.where(x_last, 1.0, 0.0)
        weight = faces * conduct_ref[x]
        src_ref[x] = source_ref[x] + weight * refined[x // 2]
        rea_ref[x] = 1.0 + reaction_ref[x] + weight


def address_kernel(parts_ref, za_ref, zb_ref, send_ref, *, width):
    planes = send_ref.shape[1] - 2
    low, high = received("gz", za_ref[RIM], zb_ref[RIM])
    shape = low.shape
    lane = lane_of(shape)
    low_tag = jnp.broadcast_to(low[:, 2 * width : 2 * width + 1], shape)
    high_tag = jnp.broadcast_to(high[:, 2 * width : 2 * width + 1], shape)
    high = roll_lanes(high, 2 * width)
    lower = lane < 2 * width
    rims = jnp.where(lower, low, high)
    tag = jnp.where(lower, low_tag, high_tag)
    column = lax.rem(lane, width)
    beside = jnp.where(column < 2, -1.0, jnp.where(column >= width - 2, 1.0, -4096.0))
    edge = jnp.where(column == 0, -1.0, jnp.where(column == width - 1, 1.0, -4096.0))
    count = parts_ref.shape[0]
    columns = [
        (roll_lanes(parts_ref[k, planes] + beside, 4 * i), roll_lanes(parts_ref[k, i], 4 * i))
        for k in range(count)
        for i in range(planes)
    ]
    columns.append((roll_lanes(tag + edge, 4 * planes), roll_lanes(rims, 4 * planes)))
    for device in range(send_ref.shape[0]):
        for i in range(planes):
            value = jnp.zeros(shape, F32)
            for k in range(count):
                value = jnp.where(parts_ref[k, planes] == device, parts_ref[k, i], value)
            send_ref[device, i] = value
        send_ref[device, planes] = jnp.where(tag == device, rims, 0.0)
        value = jnp.zeros(shape, F32)
        for spot, source in columns:
            value = jnp.where(spot == device, source, value)
        send_ref[device, planes + 1] = value


def spread(tile, offset, width):
    piece = jnp.where(lane_of(tile.shape) < width, roll_lanes(tile, -offset), 0.0)
    result = piece
    for shift in range(width, LANES, width):
        result = result + roll_lanes(piece, shift)
    return result


def place_kernel(
    home_ref, recv_ref, old_ref, za_ref, zb_ref, ya_ref, yb_ref,
    start_ref, zhalo_ref, yhalo_ref,
):
    slots = home_ref.shape[0]
    width = LANES // slots
    nx, nz, _ = old_ref.shape
    rows = nz // slots
    slot, _ = moved_slot(lambda j: home_ref[j], slots)
    planes = recv_ref.shape[1] - 2
    run = nx // planes
    count = recv_ref.shape[0]
    here = lax.div(lane_of((rows, LANES)), width) == slot

    def total(first, stride, tile):
        value = recv_ref[first, tile]
        for source in range(first + stride, count, stride):
            value = value + recv_ref[source, tile]
        return value

    for k in range(run):
        for i in range(planes):
            x = k * planes + i
            arrived = total(k, run, i)
            for g in range(slots):
                shift = lax.rem(width * (slot - g) + LANES, LANES)
                part = pl.ds(g * rows, rows)
                start_ref[x, part, :] = jnp.where(
                    here, pltpu.roll(arrived, shift, 1), old_ref[x, part, :]
                )

    rims = total(0, 1, planes)
    faces = [received("gz", za_ref[i], zb_ref[i]) for i in range(7)]
    group = lax.div(lane_of((nx, LANES)), width).astype(F32)
    for side in range(2):
        note = faces[RIM][side]
        there = jnp.broadcast_to(note[:, 3 * width : 3 * width + 1], note.shape) == group
        for depth in range(2):
            moved = spread(rims, (2 * side + depth) * width, width)
            zhalo_ref[side, depth] = jnp.where(there, moved, faces[depth][side])

    beside = [total(k, run, planes + 1) for k in range(run)]
    every = beside[0]
    for k in range(1, run):
        every = every + beside[k]
    lane = lane_of((rows, LANES))
    corner_lane = lane_of((nx, LANES))
    halos = received("gy", ya_ref[:nz], yb_ref[:nz])
    corners = received("gy", ya_ref[nz : nz + nx], yb_ref[nz : nz + nx])
    for side in range(2):
        outer = width - 1 if side == 0 else 0
        inward = -1 if side == 0 else 1
        touched = float(slots - 1 if side == 0 else 0)
        note = jnp.broadcast_to(corners[side][0:1, 4:5], (rows, LANES)) == touched
        for g in range(slots):
            value = jnp.zeros((rows, LANES), F32)
            for x in range(nx):
                source = beside[x // planes]
                for depth in range(2):
                    at = g * width + outer + inward * depth + 4 * (x % planes)
                    spot = depth * nx + x
                    value = jnp.where(lane == spot, roll_lanes(source, spot - at), value)
            held = halos[side][g * rows : (g + 1) * rows]
            yhalo_ref[side, g * rows : (g + 1) * rows] = jnp.where(
                note & (lane < 2 * nx), value, held
            )
        corner = corners[side]
        for z_side in range(2):
            note = jnp.broadcast_to(corner[:, 5 + z_side : 6 + z_side], (nx, LANES)) == touched
            at = 2 * width * z_side + outer + 4 * planes
            spot = 2 * z_side
            corner = jnp.where(
                note & (corner_lane == spot), roll_lanes(every, spot - at), corner
            )
        yhalo_ref[side, nz : nz + nx] = corner


def edge_kernel(
    start_ref, conduct_ref, src_ref, rea_ref, zhalo_ref, yhalo_ref, za_ref, zb_ref,
    xa_ref, xb_ref,
):
    nx, nz, _ = start_ref.shape
    _, flags_z, flags_y = edges()
    z_kappa = received("gz", za_ref[KAP1], zb_ref[KAP1])
    z_phi = (zhalo_ref[0, 0], zhalo_ref[1, 0])
    yf = [yhalo_ref[side, :nz] for side in range(2)]
    faces = []
    for me, inner in ((0, 1), (nx - 1, nx - 2)):
        sides = plane_sides(
            me, start_ref[me], conduct_ref[me], [(start_ref[inner], conduct_ref[inner], None)],
            z_phi, z_kappa, yf, yf, flags_z, flags_y,
        )
        sums = gather(start_ref[me] + src_ref[me], rea_ref[me], conduct_ref[me], sides)
        faces.append((start_ref[me], conduct_ref[me], *sums))
    for f in range(4):
        write_pair("gx", xa_ref, xb_ref, slice(f * nz, (f + 1) * nz), faces[0][f], faces[1][f])
    base = 4 * nz
    kappas = received("gz", za_ref[KAP1], zb_ref[KAP1])
    xa_ref[base : base + 8] = jnp.zeros((8, LANES), F32)
    xb_ref[base : base + 8] = jnp.zeros((8, LANES), F32)
    for side in range(2):
        for f, tile in enumerate((zhalo_ref[side, 0], kappas[side])):
            spot = base + 2 * side + f
            write_pair(
                "gx", xa_ref, xb_ref, slice(spot, spot + 1), tile[0:1], tile[nx - 1 : nx]
            )
    lane = lane_of((nz, LANES))
    low = high = jnp.zeros((nz, LANES), F32)
    for side in range(2):
        halo = yhalo_ref[side, :nz]
        for f, offset in enumerate((PHI1 * nx, KAP1 * nx)):
            spot = 2 * side + f
            low = jnp.where(lane == spot, roll_lanes(halo, spot - offset), low)
            high = jnp.where(lane == spot, roll_lanes(halo, spot - offset - nx + 1), high)
    write_pair("gx", xa_ref, xb_ref, slice(base + 8, base + 8 + nz), low, high)


def gather(numerator, denominator, kappa, sides):
    for phi, beside, outside in sides:
        weight = 0.5 * (kappa + beside)
        if outside is not None:
            weight = jnp.where(outside, 0.0, weight)
        numerator = numerator + weight * phi
        denominator = denominator + weight
    return numerator, denominator


def step(numerator, denominator, kappa, sides):
    numerator, denominator = gather(numerator, denominator, kappa, sides)
    return numerator / denominator


def along_rows(phi, kappa, low, high, flags):
    row = row_of(phi.shape)
    last = phi.shape[0] - 1
    low_edge, high_edge = row == 0, row == last
    return [
        (
            jnp.where(low_edge, low[0], roll_rows(phi, 1)),
            jnp.where(low_edge, low[1], roll_rows(kappa, 1)),
            low_edge & flags[0],
        ),
        (
            jnp.where(high_edge, high[0], roll_rows(phi, last)),
            jnp.where(high_edge, high[1], roll_rows(kappa, last)),
            high_edge & flags[1],
        ),
    ]


def along_lanes(phi, kappa, low, high, flags, last=LANES - 1):
    lane = lane_of(phi.shape)
    low_edge, high_edge = lane == 0, lane == last
    return [
        (
            jnp.where(low_edge, low[0], roll_lanes(phi, 1)),
            jnp.where(low_edge, low[1], roll_lanes(kappa, 1)),
            low_edge & flags[0],
        ),
        (
            jnp.where(high_edge, high[0], roll_lanes(phi, -1)),
            jnp.where(high_edge, high[1], roll_lanes(kappa, -1)),
            high_edge & flags[1],
        ),
    ]


def to_row(tile, spot):
    column = jnp.broadcast_to(tile[:, spot : spot + 1], tile.shape)
    return jnp.sum(
        jnp.where(lane_of(tile.shape) == row_of(tile.shape), column, 0.0), axis=0, keepdims=True
    )


def plane_sides(x, phi, kappa, sides, z_phi, z_kappa, y_phi, y_kappa, flags_z, flags_y):
    sides = sides + along_rows(
        phi,
        kappa,
        (z_phi[0][x : x + 1], z_kappa[0][x : x + 1]),
        (z_phi[1][x : x + 1], z_kappa[1][x : x + 1]),
        flags_z,
    )
    spot = KAP1 * z_phi[0].shape[0] + x
    sides += along_lanes(
        phi,
        kappa,
        (roll_lanes(y_phi[0], -x), roll_lanes(y_kappa[0], -spot)),
        (roll_lanes(y_phi[1], LANES - 1 - x), roll_lanes(y_kappa[1], LANES - 1 - spot)),
        flags_y,
    )
    return sides


def inner_kernel(
    start_ref, conduct_ref, src_ref, rea_ref, zhalo_ref, yhalo_ref, za_ref, zb_ref, after_ref,
    first_ref, own_ref,
):
    del after_ref
    nx, nz, _ = start_ref.shape
    _, flags_z, flags_y = edges()
    z_kappa = received("gz", za_ref[KAP1], zb_ref[KAP1])
    z_phi = (zhalo_ref[0, 0], zhalo_ref[1, 0])
    yf = [yhalo_ref[side, :nz] for side in range(2)]
    first_ref[0] = start_ref[0]
    first_ref[nx - 1] = start_ref[nx - 1]
    for x in range(1, nx - 1):
        sides = [(start_ref[i], conduct_ref[i], None) for i in (x - 1, x + 1)]
        sides = plane_sides(
            x, start_ref[x], conduct_ref[x], sides, z_phi, z_kappa, yf, yf, flags_z, flags_y
        )
        first_ref[x] = step(start_ref[x] + src_ref[x], rea_ref[x], conduct_ref[x], sides)

    lane = lane_of((nz, LANES))
    low = high = jnp.zeros((nz, LANES), F32)
    for x in range(nx):
        low = jnp.where(lane == x, roll_lanes(start_ref[x], x), low)
        high = jnp.where(lane == x, roll_lanes(start_ref[x], x + 1), high)
    own_ref[0] = low
    own_ref[1] = high


def sweeps_kernel(
    start_ref, conduct_ref, src_ref, rea_ref, zhalo_ref, yhalo_ref, own_ref,
    za_ref, zb_ref, sya_ref, syb_ref, sxa_ref, sxb_ref, xa_ref, xb_ref, first_ref,
    out_ref,
):
    nx, nz, _ = start_ref.shape
    flags_x, flags_z, flags_y = edges()
    start = [start_ref[x] for x in range(nx)]
    conduct = [conduct_ref[x] for x in range(nx)]
    base = 4 * nz

    def part(axis, a_ref, b_ref, begin, size):
        return received(axis, a_ref[begin : begin + size], b_ref[begin : begin + size])

    xf = [part("gx", xa_ref, xb_ref, f * nz, nz) for f in range(4)]
    num, den = [
        sent("gx", sxa_ref[f * nz : (f + 1) * nz], sxb_ref[f * nz : (f + 1) * nz]) for f in (XNUM, XDEN)
    ]
    xrows = part("gx", xa_ref, xb_ref, base, 8)
    xcols = part("gx", xa_ref, xb_ref, base + 8, nz)
    zf = [received("gz", za_ref[i], zb_ref[i]) for i in range(6)]
    yf = [yhalo_ref[side, :nz] for side in range(2)]
    yt = [yhalo_ref[side, nz : nz + nx] for side in range(2)]
    sf = sent("gy", sya_ref[:nz], syb_ref[:nz])

    def columns(tile, phi_spot, kappa_spot, lane):
        return roll_lanes(tile, lane - phi_spot), roll_lanes(tile, lane - kappa_spot)

    x_first_sweep, ends = [], []
    for side, me in ((0, 0), (1, nx - 1)):
        kappa = xf[XKAP][side]
        sides = [(start[me], conduct[me], None)]
        x_first_sweep.append(step(xf[XNUM][side], xf[XDEN][side], kappa, sides))
        sides = [(xf[XPHI][side], kappa, flags_x[side])]
        ends.append(step(num[side], den[side], conduct[me], sides))

    z_first_sweep = []
    for side in range(2):
        phi, kappa = zhalo_ref[side, 0], zf[KAP1][side]
        me = 0 if side == 0 else nz - 1
        at = 2 * side
        sides = [
            (zhalo_ref[side, 1], zf[KAP2][side], None),
            (start_ref[:, me, :], conduct_ref[:, me, :], None),
        ]
        sides += along_rows(
            phi,
            kappa,
            (xrows[0][at : at + 1], xrows[0][at + 1 : at + 2]),
            (xrows[1][at : at + 1], xrows[1][at + 1 : at + 2]),
            flags_x,
        )
        sides += along_lanes(
            phi,
            kappa,
            columns(yt[0], at, at + 1, 0),
            columns(yt[1], at, at + 1, LANES - 1),
            flags_y,
        )
        z_first_sweep.append(step(phi + zf[SRC][side], zf[REA][side], kappa, sides))

    y_first_sweep = []
    for side in range(2):
        phi, phi2, kappa, kappa2, src, rea = [roll_lanes(yf[side], -f * nx) for f in range(6)]
        at = 2 * side
        sides = [(phi2, kappa2, None), (own_ref[side], roll_lanes(sf[side], -KAP1 * nx), None)]
        sides += along_rows(
            phi,
            kappa,
            (to_row(yt[side], 0), to_row(yt[side], 1)),
            (to_row(yt[side], 2), to_row(yt[side], 3)),
            flags_z,
        )
        sides += along_lanes(
            phi,
            kappa,
            columns(xcols[0], at, at + 1, 0),
            columns(xcols[1], at, at + 1, nx - 1),
            flags_x,
            nx - 1,
        )
        y_first_sweep.append(step(phi + src, rea, kappa, sides))

    first = [ends[0]] + [first_ref[x] for x in range(1, nx - 1)] + [ends[1]]
    for x in range(nx):
        below = (first[x - 1], conduct[x - 1], None)
        if x == 0:
            below = (x_first_sweep[0], xf[XKAP][0], flags_x[0])
        if x == nx - 1:
            above = (x_first_sweep[1], xf[XKAP][1], flags_x[1])
        else:
            above = (first[x + 1], conduct[x + 1], None)
        sides = plane_sides(
            x, first[x], conduct[x], [below, above],
            z_first_sweep, zf[KAP1], y_first_sweep, yf, flags_z, flags_y,
        )
        out_ref[x] = step(start[x] + src_ref[x], rea_ref[x], conduct[x], sides)


def swap(axis, first, second):
    count = lax.axis_size(axis)
    results = []
    for j, value in ((1, second), (0, first)):
        pairs = []
        for low in range(j, count - 1, 2):
            pairs += [(low, low + 1), (low + 1, low)]
        results.append(lax.ppermute(value, axis, pairs))
    return results[::-1]


def call(kernel, operands, outs, smem=0, hbm=(), hbm_outs=(), scratch=()):
    specs = [SMEM] * smem + [VMEM] * (len(operands) - smem)
    operands = list(operands)
    for i in hbm:
        specs[i] = HBM
        operands[i] = pltpu.with_memory_space_constraint(operands[i], pltpu.HBM)
    return pl.pallas_call(
        kernel,
        out_shape=[jax.ShapeDtypeStruct(shape, F32) for shape in outs],
        in_specs=specs,
        out_specs=[HBM if i in hbm_outs else VMEM for i in range(len(outs))],
        scratch_shapes=scratch,
        compiler_params=PARAMS,
    )(*operands)


def on_device(old_field, new_home, conduct, reaction, source, coarse):
    nx, nz, ny = block = old_field.shape
    home = new_home[0, 0]
    slots = home.shape[0]
    rows, width = nz // slots, ny // slots
    line = lax.axis_size("gy")
    part = nx // RUN

    sza, szb, parts = call(
        first_kernel,
        (new_home, old_field, conduct, source, reaction, coarse),
        [(7, nx, ny), (7, nx, ny), (RUN, part + 1, rows, ny)],
        hbm=(0, 1, 2, 3, 4, 5),
        hbm_outs=(2,),
        scratch=[
            pltpu.VMEM((RUN, part + 1, rows, ny), F32),
            pltpu.SMEM(new_home.shape, jnp.int32),
            pltpu.VMEM(block, F32),
            pltpu.VMEM((3, 2, nx, 2, ny), F32),
            pltpu.VMEM(coarse.shape, F32),
            pltpu.SemaphoreType.DMA,
            pltpu.SemaphoreType.DMA((nx,)),
            pltpu.SemaphoreType.DMA((3, 2)),
            pltpu.SemaphoreType.DMA,
            pltpu.SemaphoreType.DMA((RUN,)),
        ],
    )
    za, zb = swap("gz", sza, szb)
    groups = [[i * RUN + k for k in range(RUN)] for i in range(line // RUN)]
    parts = lax.all_to_all(parts, "gy", 0, 0, tiled=True, axis_index_groups=groups)

    def address(*refs):
        address_kernel(*refs, width=width)

    (send,) = call(address, (parts, za, zb), [(line, part + 2, rows, ny)])
    recv = lax.all_to_all(send, "gy", 0, 0, tiled=True)

    def columns(*refs):
        columns_kernel(*refs, width=width)

    sya, syb = call(
        columns, (sza, old_field, conduct, source, reaction, coarse, za, zb), [(nz + nx, ny)] * 2
    )
    ya, yb = swap("gy", sya, syb)
    src, rea = call(fold_kernel, (conduct, source, reaction, coarse, sya), [block, block])
    start, zhalo, yhalo = call(
        place_kernel,
        (home, recv, old_field, za, zb, ya, yb),
        [block, (2, 2, nx, ny), (2, nz + nx, ny)],
        smem=1,
    )
    sxa, sxb = call(
        edge_kernel,
        (start, conduct, src, rea, zhalo, yhalo, za, zb),
        [(5 * nz + 8, ny)] * 2,
    )
    first, own = call(
        inner_kernel,
        (start, conduct, src, rea, zhalo, yhalo, za, zb, sxa),
        [block, (2, nz, ny)],
    )
    xa, xb = swap("gx", sxa, sxb)
    (relaxed,) = call(
        sweeps_kernel,
        (start, conduct, src, rea, zhalo, yhalo, own, za, zb, sya, syb, sxa, sxb, xa, xb, first),
        [block],
    )
    return relaxed


def solution(mesh):
    return jax.shard_map(
        on_device,
        mesh=mesh,
        in_specs=(P("gx", "gz", "gy"),) * 6,
        out_specs=P("gx", "gz", "gy"),
        check_vma=False,
    )
```
